128 devices in a mesh: dp: 8 (over x, core), fsdp: 16 (over z, y).
Axes of the slice: x: 4, y: 4, z: 4, core: 2. Of those that a mesh axis runs over, the one named last changes fastest.
Arguments:
- gradients: bfloat16 [8, 128, 512, 512], P('dp', None, 'fsdp')
- block_owner: int32 [128], replicated, may hold values from 0 to 127, as said below
- left_stat: float32 [256, 512, 512], P(('dp', 'fsdp')), may hold values from -6 to 6
- right_stat: float32 [256, 512, 512], P(('dp', 'fsdp')), may hold values from -6 to 6
- root_left: bfloat16 [256, 512, 512], P(('dp', 'fsdp'))
- root_right: bfloat16 [256, 512, 512], P(('dp', 'fsdp'))
- moment_first: float32 [128, 512, 512], P('dp', 'fsdp'), may hold values from -0.75 to 0.75
- moment_second: float32 [128, 512, 512], P('dp', 'fsdp')
Outputs:
- update: bfloat16 [128, 512, 512], P('dp', 'fsdp')
- moment_first_new: float32 [128, 512, 512], P('dp', 'fsdp')
- moment_second_new: float32 [128, 512, 512], P('dp', 'fsdp')
- left_new: float32 [256, 512, 512], P(('dp', 'fsdp'))
- right_new: float32 [256, 512, 512], P(('dp', 'fsdp'))
The draws below stay inside these ranges and needn't reach their ends.
Inputs may be any that keep to these rules, and one draw needn't show every extreme that they name: Block b's statistics and roots belong to device block_owner[b], devices numbered dp-major over dp and fsdp; block b's owner has dp index b // 16; each device owns at most 2 blocks and in every dp row some device owns exactly 2.
All inputs are finite; a program needn't handle non-finite values.
Results may differ from the reference program's by a relative error of at most 0.029.
Values may be sent and summed in bfloat16 or wider, within the bound.
A program may use at most 128 MiB of HBM per device.

```python
import math
import jax
import jax.numpy as jnp
from jax import lax

BLOCK = 512
BLK_DEV = 1
SLOTS = 2
NBLK = 128
N_DP = 8
N_FSDP = 16


def draw_gradients(key, part):
    key = jax.random.fold_in(key, 1)
    key_row, key_col, key_noise = jax.random.split(key, 3)
    row_scale = 10.0 ** jax.random.uniform(key_row, (1, NBLK, BLOCK, 1), jnp.float32)
    col_scale = 10.0 ** jax.random.uniform(key_col, (1, NBLK, 1, BLOCK), jnp.float32)
    noise = jax.random.normal(key_noise, (N_DP, NBLK, BLOCK, BLOCK), jnp.float32)
    return (0.003 * noise * row_scale * col_scale).astype(jnp.bfloat16)


def owners_of_row(key):
    total = N_FSDP * SLOTS
    group = BLK_DEV * N_FSDP
    first, second = jax.random.split(key)
    order = jax.random.permutation(first, total).astype(jnp.int32)
    ranking = jnp.argsort(order).astype(jnp.int32)
    busiest = order[0] // SLOTS
    candidates = jnp.arange(total, dtype=jnp.int32)
    priority = jnp.where(candidates // SLOTS == busiest, candidates % SLOTS - SLOTS, ranking)
    chosen = jnp.argsort(priority)[:group].astype(jnp.int32)
    owners = (chosen // SLOTS).astype(jnp.int32)
    return owners[jax.random.permutation(second, group)]


def draw_block_owner(key, part):
    key = jax.random.fold_in(key, 7)
    row_keys = jax.random.split(key, N_DP)
    within = jax.vmap(owners_of_row)(row_keys).astype(jnp.int32)
    rows = (jnp.arange(N_DP, dtype=jnp.int32) * N_FSDP)[:, None]
    return (within + rows).reshape(NBLK).astype(jnp.int32)


def root_matrix(key, lowest, highest, spread):
    key_diag, key_off = jax.random.split(key)
    count = N_DP * N_FSDP * SLOTS
    trend = math.sqrt(3.0) ** (jnp.arange(BLOCK, dtype=jnp.float32) / BLOCK)
    diagonal = jnp.exp(jax.random.uniform(key_diag, (count, BLOCK), jnp.float32, math.log(lowest), math.log(highest))) * trend[None, :]
    off_part = jax.random.normal(key_off, (count, BLOCK, BLOCK), jnp.float32) * (spread / math.sqrt(BLOCK))
    return (off_part + diagonal[:, :, None] * jnp.eye(BLOCK, dtype=jnp.float32)[None]).astype(jnp.bfloat16)


def draw_root_left(key, part):
    key = jax.random.fold_in(key, 2)
    return root_matrix(key, 0.5, 2.0, 0.5)


def draw_root_right(key, part):
    key = jax.random.fold_in(key, 3)
    return root_matrix(key, 0.5, 2.0, 0.5)


def second_moment(key, lowest, highest):
    trend = 3.0 ** (-jnp.arange(BLOCK, dtype=jnp.float32) / BLOCK)
    values = jnp.exp(jax.random.uniform(key, (NBLK, BLOCK, BLOCK), jnp.float32, math.log(lowest), math.log(highest)))
    return values * trend[None, :, None]


def draw_moment_second(key, part):
    key = jax.random.fold_in(key, 4)
    return second_moment(key, 0.0001, 0.01)


def steps_of(own_key, shape, pieces, least, top_value):
    loudness, own = 1.0, jax.random.fold_in(own_key, 6)
    for axis_at, blocks in pieces:
        steps = jnp.exp(jax.random.uniform(jax.random.fold_in(own, axis_at), (blocks,), jnp.float32, least / len(pieces), top_value / len(pieces)))
        loudness = loudness * jnp.repeat(steps, shape[axis_at] // blocks).reshape([-1 if axis == axis_at else 1 for axis in range(len(shape))])
    return loudness


def gaussian(rng, shape, scale, bound, cuts=(), kind=jnp.bfloat16):
    gain = steps_of(rng, shape, cuts, -0.22, 0.18) if cuts else 1.0
    array = jax.random.normal(rng, shape, jnp.float32) * scale * gain
    return jnp.minimum(jnp.maximum(array, -bound), bound).astype(kind)


def setup_inputs(seed: int = 0) -> dict:
    splits = jax.random.split(jax.random.key(seed), 9)
    gradients = draw_gradients(jax.random.fold_in(splits[8], 71), 0)
    block_owner = draw_block_owner(jax.random.fold_in(splits[8], 71), 0)
    left_stat = gaussian(splits[2], (N_DP * N_FSDP * SLOTS, BLOCK, BLOCK), 1.0, 6.0, ((0, 128),), jnp.float32)
    right_stat = gaussian(splits[3], (N_DP * N_FSDP * SLOTS, BLOCK, BLOCK), 1.0, 6.0, ((0, 128),), jnp.float32)
    root_left = draw_root_left(jax.random.fold_in(splits[8], 71), 0)
    root_right = draw_root_right(jax.random.fold_in(splits[8], 71), 0)
    moment_first = gaussian(splits[6], (NBLK, BLOCK, BLOCK), 0.05, 0.75, ((0, 8), (1, 16)), jnp.float32)
    moment_second = draw_moment_second(jax.random.fold_in(splits[8], 71), 0)
    return {"gradients": gradients, "block_owner": block_owner, "left_stat": left_stat, "right_stat": right_stat, "root_left": root_left, "root_right": root_right, "moment_first": moment_first, "moment_second": moment_second}


def slot_ranking(block_owner):
    count = block_owner.shape[0]
    matches = block_owner[:, None] == block_owner[None, :]
    earlier = jnp.arange(count)[None, :] < jnp.arange(count)[:, None]
    return lax.optimization_barrier(jnp.sum(jnp.where(matches & earlier, 1, 0), axis=1)).astype(jnp.int32)

def reference(gradients, block_owner, left_stat, right_stat, root_left, root_right, moment_first, moment_second):
    summed = jnp.zeros(gradients.shape[1:], jnp.float32)
    for replica in range(N_DP):
        summed = summed + gradients[replica].astype(jnp.float32)
    grad = summed.astype(jnp.bfloat16)
    position = (block_owner * SLOTS + slot_ranking(block_owner)).astype(jnp.int32)

    def precondition(index):
        block = grad[index]
        where = position[index]
        gram_left = jnp.dot(block, block.T, preferred_element_type=jnp.float32)
        gram_right = jnp.dot(block.T, block, preferred_element_type=jnp.float32)
        half = jnp.dot(root_left[where], block, preferred_element_type=jnp.float32)
        direction = jnp.dot(half, root_right[where].astype(jnp.float32), precision=lax.Precision.HIGHEST)
        return (gram_left, gram_right, direction.astype(jnp.bfloat16))
    gram_left, gram_right, direction = lax.map(precondition, jnp.arange(NBLK, dtype=jnp.int32))
    left_new = (0.95 * left_stat).at[position].add(0.05 * gram_left)
    right_new = (0.95 * right_stat).at[position].add(0.05 * gram_right)
    grad_float = grad.astype(jnp.float32)
    moment_first_new = 0.9 * moment_first + 0.1 * grad_float
    moment_second_new = 0.95 * moment_second + 0.05 * grad_float * grad_float
    adam = moment_first_new / (jnp.sqrt(moment_second_new) + 1e-08)
    adam_sq = lax.optimization_barrier(jnp.sum(adam * adam, axis=(1, 2)))
    direction_float = direction.astype(jnp.float32)
    direction_sq = lax.optimization_barrier(jnp.sum(direction_float * direction_float, axis=(1, 2)))
    graft_scale = jnp.sqrt(adam_sq / (direction_sq + 1e-06))
    update = (-graft_scale[:, None, None] * direction_float).astype(jnp.bfloat16)
    return (update, moment_first_new, moment_second_new, left_new, right_new)
```

```python
import functools

import jax
import jax.numpy as jnp
from jax import lax
from jax.experimental import pallas as pl
from jax.experimental.pallas import tpu as pltpu
from jax.sharding import PartitionSpec as P

F32 = jnp.float32
BF16 = jnp.bfloat16
I32 = jnp.int32
CHUNKS = 4
SIDE = 4
NEAR = ((1, 0), (-1, 0), (0, 1), (0, -1), (1, 1), (-1, -1), (1, -1), (-1, 1))
LEGS = (
    (
        ((1, 1), (1, 1)),
        ((1, 1), (1, 0)),
        ((1, -1), (1, 0)),
        ((1, 1), (0, 1)),
        ((-1, 1), (0, 1)),
        ((1, 0), (1, 0)),
        ((0, 1), (0, 1)),
    ),
    (
        ((-1, -1), (-1, -1)),
        ((-1, 1), (-1, 0)),
        ((-1, -1), (-1, 0)),
        ((1, -1), (0, -1)),
        ((-1, -1), (0, -1)),
        ((-1, 0), (-1, 0)),
        ((0, -1), (0, -1)),
    ),
)


def exchange_kernel(
    owner_ref,
    grad_ref,
    root_left_ref,
    root_right_ref,
    first_ref,
    second_ref,
    left_ref,
    right_ref,
    update_out,
    first_out,
    second_out,
    left_out,
    right_out,
    owner,
    places,
    place,
    own,
    other,
    pair,
    relay_right,
    relay_left,
    from_left,
    from_right,
    reduced,
    outgoing,
    block,
    root_left,
    root_right,
    first,
    second,
    stat_left,
    stat_right,
    direction,
    returned,
    relayed,
    sums,
    all_sums,
    sizes,
    graft,
    update,
    place_sem,
    own_sem,
    load_sem,
    store_sem,
    core_send,
    core_recv,
    ring_send,
    ring_recv,
    owner_send,
    owner_recv,
    back_send,
    back_recv,
    relay_send,
    relay_recv,
    sums_send,
    sums_recv,
):
    lines, _, per_group, strip, columns = grad_ref.shape
    width = columns // CHUNKS
    half = per_group // 2
    slots, rows = block.shape[:2]
    ranks = rows // strip
    count = owner.shape[1]
    dp = lax.axis_index("dp")
    rank = lax.axis_index("fsdp")
    x = dp // 2
    core = dp % 2
    y = rank % SIDE
    z = rank // SIDE
    mate = x * 2 + (1 - core)
    ahead = (x + 1) % lines
    behind = (x + lines - 1) % lines
    across = (x + 2) % lines
    right = ahead * 2 + core
    left = behind * 2 + core
    chunks = range(CHUNKS)

    def cols(k):
        return pl.ds(k * width, width)

    def strip_rows(at):
        return pl.ds(pl.multiple_of(at * strip, strip), strip)

    sign = 1 - 2 * core

    def at_offset(dy, dz):
        target_y = (y + SIDE + sign * dy) % SIDE
        target_z = (z + SIDE + sign * dz) % SIDE
        return target_z * SIDE + target_y

    def each_target(visit):
        @pl.loop(0, SIDE)
        def _(turn):
            for index, (dy, shift) in enumerate(((1, 0), (3, 2), (2, 3), (0, 1))):
                dz = (turn + shift) % SIDE
                target = at_offset(dy, dz)
                if index < 3:
                    visit(target)
                else:
                    pl.when(turn < SIDE - 1)(functools.partial(visit, target))

    owner_load = pltpu.make_async_copy(owner_ref, owner, place_sem.at[0])
    owner_load.start()
    own_loads = []
    for k in chunks:
        load = pltpu.make_async_copy(
            grad_ref.at[:, core, :, :, cols(k)], own.at[k], own_sem.at[k]
        )
        load.start()
        own_loads.append(load)
    loads = [
        pltpu.make_async_copy(src, dst, load_sem.at[index])
        for index, (src, dst) in enumerate(
            (
                (root_left_ref, root_left),
                (root_right_ref, root_right),
                (first_ref, first),
                (second_ref, second),
                (left_ref, stat_left),
                (right_ref, stat_right),
            )
        )
    ]
    barrier = pltpu.get_barrier_semaphore()
    for partner in (mate, right, left):
        pl.semaphore_signal(barrier, inc=1, device_id={"dp": partner})

    @pl.loop(1, ranks)
    def _(step):
        pl.semaphore_signal(barrier, inc=1, device_id={"fsdp": (rank + step) % ranks})

    owner_load.wait()
    along = lax.broadcasted_iota(I32, (count, count), 1)
    down = lax.broadcasted_iota(I32, (count, count), 0)
    owner_row = owner[...]
    owner_all = jnp.broadcast_to(owner_row, (count, count)).astype(F32)
    owner_col = jnp.sum(jnp.where(along == down, owner_all, 0.0), axis=1, keepdims=True)
    same = owner_all == owner_col
    slot_row = jnp.sum(jnp.where(same & (down < along), 1.0, 0.0), axis=0, keepdims=True)
    slot_col = jnp.sum(jnp.where(same & (along < down), 1.0, 0.0), axis=1, keepdims=True)
    offset = (dp * (ranks * slots)).astype(F32)
    place_row = owner_row.astype(F32) * slots + slot_row - offset
    place_col = owner_col * slots + slot_col - offset
    number = (down - dp * per_group + 1).astype(F32)
    held_row = jnp.sum(
        jnp.where(along.astype(F32) == place_col, number, 0.0), axis=0, keepdims=True
    )
    places[0:1] = place_row.astype(I32)
    places[1:2] = held_row.astype(I32)
    place_copy = pltpu.make_async_copy(places, place, place_sem.at[1])
    place_copy.start()

    pl.semaphore_wait(barrier, ranks + 2)

    core_copies = []
    for k in chunks:
        copies = []
        for index, line in enumerate((across, ahead, behind, x)):
            copy = pltpu.make_async_remote_copy(
                src_ref=grad_ref.at[line, 1 - core, :, :, cols(k)],
                dst_ref=other.at[k, line],
                send_sem=core_send.at[k, index],
                recv_sem=core_recv.at[k, line],
                device_id={"dp": mate},
            )
            copy.start()
            copies.append(copy)
        core_copies.append(copies)
    place_copy.wait()

    def held(at):
        return place[1, at]

    def block_of(at):
        return jnp.clip(held(at) - 1, 0, per_group - 1)

    def place_of(index):
        return jnp.clip(place[0, dp * per_group + index], 0, ranks * slots - 1)

    def wait_core(k, line):
        ref = other.at[k, line]
        pltpu.make_async_copy(ref, ref, core_recv.at[k, line]).wait()

    def ring(k, index, src, dst, target):
        return pltpu.make_async_remote_copy(
            src_ref=src,
            dst_ref=dst,
            send_sem=ring_send.at[k, index],
            recv_sem=ring_recv.at[k, index],
            device_id={"dp": target},
        )

    ring_copies = [None] * CHUNKS
    low, high = pl.ds(0, half), pl.ds(half, half)

    def far_sums(k):
        copies = [
            ring(k, 0, pair.at[k, across, low], relay_right.at[k], right),
            ring(k, 1, pair.at[k, across, high], relay_left.at[k], left),
            ring(k, 2, pair.at[k, ahead, high], from_left.at[k, high], right),
            ring(k, 3, pair.at[k, behind, low], from_right.at[k, low], left),
            ring(k, 4, pair.at[k, ahead, low], from_left.at[k, low], right),
            ring(k, 5, pair.at[k, behind, high], from_right.at[k, high], left),
        ]
        ring_copies[k] = copies
        own_loads[k].wait()
        wait_core(k, across)
        pair[k, across] = own[k, across] + other[k, across]
        copies[0].start()
        copies[1].start()

    def near_sums(k):
        copies = ring_copies[k]
        wait_core(k, ahead)
        pair[k, ahead] = own[k, ahead] + other[k, ahead]
        copies[2].start()
        wait_core(k, behind)
        pair[k, behind] = own[k, behind] + other[k, behind]
        copies[3].start()

    def relay(k):
        copies = ring_copies[k]
        copies[0].wait_recv()
        pair[k, ahead, low] = pair[k, ahead, low] + relay_right[k]
        copies[4].start()
        copies[1].wait_recv()
        pair[k, behind, high] = pair[k, behind, high] + relay_left[k]
        copies[5].start()

    def finish(k):
        wait_core(k, x)
        total = own[k, x].astype(F32) + other[k, x].astype(F32)
        for copy in ring_copies[k][2:]:
            copy.wait_recv()
        total = total + from_left[k].astype(F32) + from_right[k].astype(F32)
        reduced[k] = total.astype(BF16)

        def visit(target):
            for slot in range(slots):
                outgoing[k, target, slot] = reduced[k, block_of(target * slots + slot)]
            pltpu.make_async_remote_copy(
                src_ref=outgoing.at[k, target],
                dst_ref=block.at[:, strip_rows(rank), cols(k)],
                send_sem=owner_send.at[k],
                recv_sem=owner_recv.at[k],
                device_id={"fsdp": target},
            ).start()

        each_target(visit)
        for slot in range(slots):
            block[slot, strip_rows(rank), cols(k)] = reduced[k, block_of(rank * slots + slot)]

    far_sums(0)
    near_sums(0)
    far_sums(1)
    relay(0)
    for load in loads:
        load.start()
    for k in chunks:
        if k + 1 < CHUNKS:
            near_sums(k + 1)
        if k + 2 < CHUNKS:
            far_sums(k + 2)
        if k + 1 < CHUNKS:
            relay(k + 1)
        finish(k)

    others = (ranks - 1) * strip

    def arrived(ref, sem):
        pltpu.make_async_copy(ref, ref, sem).wait()

    for k in chunks:
        arrived(block.at[:, pl.ds(0, others), cols(k)], owner_recv.at[k])
    loads[0].wait()
    loads[1].wait()

    for slot in range(slots):
        product = jnp.dot(root_left[slot], block[slot], preferred_element_type=F32)
        direction[slot] = jnp.dot(
            product.astype(BF16), root_right[slot], preferred_element_type=F32
        ).astype(BF16)

        for index, (first_leg, second_leg) in enumerate(LEGS[slot]):
            target = at_offset(first_leg[0] + second_leg[0], first_leg[1] + second_leg[1])
            pltpu.make_async_remote_copy(
                src_ref=direction.at[slot, strip_rows(target)],
                dst_ref=relayed.at[slot, index],
                send_sem=back_send.at[slot],
                recv_sem=relay_recv.at[slot, index],
                device_id={"fsdp": at_offset(*first_leg)},
            ).start()
        for offset in NEAR:
            target = at_offset(*offset)
            pltpu.make_async_remote_copy(
                src_ref=direction.at[slot, strip_rows(target)],
                dst_ref=returned.at[rank, slot],
                send_sem=back_send.at[slot],
                recv_sem=back_recv.at[slot],
                device_id={"fsdp": target},
            ).start()

    for slot in range(slots):
        for index, (first_leg, second_leg) in enumerate(LEGS[slot]):
            origin = at_offset(-first_leg[0], -first_leg[1])
            arrived(relayed.at[slot, index], relay_recv.at[slot, index])
            pltpu.make_async_remote_copy(
                src_ref=relayed.at[slot, index],
                dst_ref=returned.at[origin, slot],
                send_sem=relay_send.at[slot],
                recv_sem=back_recv.at[slot],
                device_id={"fsdp": at_offset(*second_leg)},
            ).start()

    for slot in range(slots):
        returned[rank, slot] = direction[slot, strip_rows(rank)]
        wide = direction[slot].astype(F32)
        wide = jnp.sum((wide * wide).reshape(-1, 8, columns), axis=0)
        sums[2 + slot] = functools.reduce(
            jnp.add, [wide[:, at : at + 128] for at in range(0, columns, 128)]
        )
    loads[2].wait()
    loads[3].wait()

    @pl.loop(0, per_group)
    def _(index):
        total = jnp.zeros((1, 128), F32)
        for k in chunks:
            grad = reduced[k, index].astype(F32)
            first_new = 0.9 * first[index, :, cols(k)] + 0.1 * grad
            second_new = 0.95 * second[index, :, cols(k)] + 0.05 * grad * grad
            first[index, :, cols(k)] = first_new
            second[index, :, cols(k)] = second_new
            adam = first_new / (jnp.sqrt(second_new) + 1e-08)
            part = jnp.sum(adam * adam, axis=0, keepdims=True)
            for at in range(0, width, 128):
                total = total + part[:, at : at + 128]
        sums[index // 8, pl.ds(index % 8, 1)] = total

    def send_sums(target):
        pltpu.make_async_remote_copy(
            src_ref=sums,
            dst_ref=all_sums.at[rank],
            send_sem=sums_send,
            recv_sem=sums_recv,
            device_id={"fsdp": target},
        ).start()

    each_target(send_sums)
    all_sums[rank] = sums[...]
    stores = [
        pltpu.make_async_copy(first, first_out, store_sem.at[0]),
        pltpu.make_async_copy(second, second_out, store_sem.at[1]),
    ]
    for store in stores:
        store.start()

    loads[4].wait()
    loads[5].wait()
    for stat, contract, index, out in ((stat_left, 1, 2, left_out), (stat_right, 0, 3, right_out)):
        for slot in range(slots):
            gram = lax.dot_general(
                block[slot],
                block[slot],
                (((contract,), (contract,)), ((), ())),
                preferred_element_type=F32,
            )
            used = held(rank * slots + slot) > 0
            stat[slot] = 0.95 * stat[slot] + 0.05 * jnp.where(used, gram, 0.0)
        store = pltpu.make_async_copy(stat, out, store_sem.at[index])
        store.start()
        stores.append(store)

    arrived(all_sums.at[pl.ds(0, ranks - 1)], sums_recv)
    for index in range(per_group):
        at = place_of(index)
        sizes[index] = all_sums[at // slots, 2 + at % slots]
    adam_sq = jnp.sum(all_sums[:, 0:2], axis=0).reshape(per_group, 128)
    adam_sq = jnp.sum(adam_sq, axis=1, keepdims=True)
    direction_sq = jnp.sum(jnp.sum(sizes[...], axis=1), axis=1, keepdims=True)
    graft[...] = jnp.broadcast_to(jnp.sqrt(adam_sq / (direction_sq + 1e-06)), graft.shape)

    for slot in range(slots):
        arrived(returned.at[pl.ds(0, ranks - 1), slot], back_recv.at[slot])

    @pl.loop(0, per_group)
    def _(index):
        at = place_of(index)
        scale = -graft[pl.ds(index, 1)]
        value = returned[at // slots, at % slots].astype(F32)
        update[index] = (value * jnp.concatenate([scale] * (columns // 128), axis=1)).astype(BF16)

    store = pltpu.make_async_copy(update, update_out, store_sem.at[4])
    store.start()
    stores.append(store)

    for k in chunks:
        for copy in core_copies[k] + ring_copies[k]:
            copy.wait_send()
        arrived(outgoing.at[k, pl.ds(0, ranks - 1)], owner_send.at[k])
    for slot in range(slots):
        arrived(direction.at[slot, pl.ds(0, others)], back_send.at[slot])
        arrived(relayed.at[slot], relay_send.at[slot])
    arrived(all_sums.at[pl.ds(0, ranks - 1)], sums_send)
    for store in stores:
        store.wait()


def exchange(block_owner, gradients, root_left, root_right, first, second, left, right, ranks):
    lines, _, per_group, strip, columns = gradients.shape
    slots, rows, _ = root_left.shape
    width = columns // CHUNKS
    half = per_group // 2
    anywhere = pl.BlockSpec(memory_space=pl.ANY)
    far = pl.BlockSpec(memory_space=pltpu.HBM)
    dma = pltpu.SemaphoreType.DMA
    vmem = pltpu.VMEM
    return pl.pallas_call(
        exchange_kernel,
        out_shape=(
            jax.ShapeDtypeStruct(first.shape, BF16),
            jax.ShapeDtypeStruct(first.shape, F32),
            jax.ShapeDtypeStruct(first.shape, F32),
            jax.ShapeDtypeStruct(left.shape, F32),
            jax.ShapeDtypeStruct(right.shape, F32),
        ),
        in_specs=[far] * 8,
        out_specs=(anywhere,) * 5,
        scratch_shapes=[
            vmem(block_owner.shape, I32),
            vmem((8, 128), I32),
            pltpu.SMEM((8, 128), I32),
            vmem((CHUNKS, lines, per_group, strip, width), BF16),
            vmem((CHUNKS, lines, per_group, strip, width), BF16),
            vmem((CHUNKS, lines, per_group, strip, width), BF16),
            vmem((CHUNKS, half, strip, width), BF16),
            vmem((CHUNKS, half, strip, width), BF16),
            vmem((CHUNKS, per_group, strip, width), BF16),
            vmem((CHUNKS, per_group, strip, width), BF16),
            vmem((CHUNKS, per_group, strip, width), BF16),
            vmem((CHUNKS, ranks, slots, strip, width), BF16),
            vmem((slots, rows, columns), BF16),
            vmem((slots, rows, columns), BF16),
            vmem((slots, rows, columns), BF16),
            vmem(first.shape, F32),
            vmem(first.shape, F32),
            vmem(left.shape, F32),
            vmem(right.shape, F32),
            vmem((slots, rows, columns), BF16),
            vmem((ranks, slots, strip, columns), BF16),
            vmem((slots, len(LEGS[0]), strip, columns), BF16),
            vmem((4, 8, 128), F32),
            vmem((ranks, 4, 8, 128), F32),
            vmem((per_group, 8, 128), F32),
            vmem((per_group, 128), F32),
            vmem((per_group, strip, columns), BF16),
            dma((2,)),
            dma((CHUNKS,)),
            dma((6,)),
            dma((5,)),
            dma((CHUNKS, 4)),
            dma((CHUNKS, 4)),
            dma((CHUNKS, 6)),
            dma((CHUNKS, 6)),
            dma((CHUNKS,)),
            dma((CHUNKS,)),
            dma((slots,)),
            dma((slots,)),
            dma((slots,)),
            dma((slots, len(LEGS[0]))),
            dma,
            dma,
        ],
        compiler_params=pltpu.CompilerParams(
            collective_id=0, has_side_effects=True, vmem_limit_bytes=40 * 2**20
        ),
        cost_estimate=pl.CostEstimate(
            flops=8 * slots * rows * rows * columns, bytes_accessed=18 * 2**20, transcendentals=0
        ),
        name="exchange",
    )(
        *(
            pltpu.with_memory_space_constraint(value, pltpu.HBM)
            for value in (
                block_owner,
                gradients,
                root_left,
                root_right,
                first,
                second,
                left,
                right,
            )
        )
    )


def publish_kernel(*refs):
    count = (len(refs) - 1) // 2
    sems = refs[-1]
    copies = [
        pltpu.make_async_copy(refs[index], refs[count + index], sems.at[index])
        for index in range(count)
    ]
    for copy in copies:
        copy.start()
    for copy in copies:
        copy.wait()


def publish(results):
    return pl.pallas_call(
        publish_kernel,
        out_shape=[jax.ShapeDtypeStruct(value.shape, value.dtype) for value in results],
        in_specs=[pl.BlockSpec(memory_space=pl.ANY)] * len(results),
        out_specs=[pl.BlockSpec(memory_space=pltpu.HBM)] * len(results),
        scratch_shapes=[pltpu.SemaphoreType.DMA((len(results),))],
        compiler_params=pltpu.CompilerParams(vmem_limit_bytes=2**20),
        name="publish",
    )(*(pltpu.with_memory_space_constraint(value, pltpu.VMEM) for value in results))


def shards(
    gradients,
    block_owner,
    left_stat,
    right_stat,
    root_left,
    root_right,
    moment_first,
    moment_second,
):
    dp_count = lax.axis_size("dp")
    ranks = lax.axis_size("fsdp")
    count = block_owner.shape[0]
    strip, columns = gradients.shape[2:]
    results = exchange(
        block_owner.reshape(1, count),
        gradients.reshape(dp_count // 2, 2, count // dp_count, strip, columns),
        root_left,
        root_right,
        moment_first,
        moment_second,
        left_stat,
        right_stat,
        ranks,
    )
    return tuple(publish(results))


def solution(mesh):
    placed = (
        P("dp", None, "fsdp", None),
        P(),
        P(("dp", "fsdp"), None, None),
        P(("dp", "fsdp"), None, None),
        P(("dp", "fsdp"), None, None),
        P(("dp", "fsdp"), None, None),
        P("dp", "fsdp", None),
        P("dp", "fsdp", None),
    )
    return jax.shard_map(
        shards,
        mesh=mesh,
        in_specs=placed,
        out_specs=(
            P("dp", "fsdp", None),
            P("dp", "fsdp", None),
            P("dp", "fsdp", None),
            P(("dp", "fsdp"), None, None),
            P(("dp", "fsdp"), None, None),
        ),
        check_vma=False,
    )
```

```python
import functools

import jax
import jax.numpy as jnp
from jax import lax
from jax.experimental import pallas as pl
from jax.experimental.pallas import tpu as pltpu
from jax.sharding import PartitionSpec as P

F32 = jnp.float32
BF16 = jnp.bfloat16
I32 = jnp.int32
CHUNKS = 4
SIDE = 4
NEAR = ((1, 0), (-1, 0), (0, 1), (0, -1), (1, 1), (-1, -1), (1, -1), (-1, 1))
LEGS = (
    ((1, 1), (1, 1)),
    ((-1, 1), (-1, 0)),
    ((-1, -1), (-1, 0)),
    ((1, -1), (0, -1)),
    ((-1, -1), (0, -1)),
    ((1, 0), (1, 0)),
    ((0, 1), (0, 1)),
)


def legs_of(slot):
    sign = 1 - 2 * slot
    return [tuple((sign * dy, sign * dz) for dy, dz in legs) for legs in LEGS]


def exchange_kernel(
    owner_ref,
    grad_ref,
    root_left_ref,
    root_right_ref,
    first_ref,
    second_ref,
    left_ref,
    right_ref,
    update_out,
    first_out,
    second_out,
    left_out,
    right_out,
    owner,
    places,
    place,
    own,
    other,
    pair,
    relay_right,
    relay_left,
    from_left,
    from_right,
    reduced,
    outgoing,
    block,
    root_left,
    root_right,
    first,
    second,
    stat_left,
    stat_right,
    direction,
    returned,
    relayed,
    sums,
    all_sums,
    sizes,
    graft,
    update,
    place_sem,
    own_sem,
    load_sem,
    store_sem,
    core_send,
    core_recv,
    ring_send,
    ring_recv,
    owner_send,
    owner_recv,
    back_send,
    back_recv,
    relay_send,
    relay_recv,
    sums_send,
    sums_recv,
):
    lines, _, per_group, strip, columns = grad_ref.shape
    width = columns // CHUNKS
    half = per_group // 2
    slots, rows = block.shape[:2]
    ranks = rows // strip
    count = owner.shape[1]
    dp = lax.axis_index("dp")
    rank = lax.axis_index("fsdp")
    x = dp // 2
    core = dp % 2
    y = rank % SIDE
    z = rank // SIDE
    mate = x * 2 + (1 - core)
    sign = 1 - 2 * core
    ahead = (x + lines + sign) % lines
    behind = (x + lines - sign) % lines
    across = (x + 2) % lines
    right = ahead * 2 + core
    left = behind * 2 + core
    chunks = range(CHUNKS)

    def cols(k):
        return pl.ds(k * width, width)

    def strip_rows(at):
        return pl.ds(pl.multiple_of(at * strip, strip), strip)

    def at_offset(dy, dz):
        target_y = (y + SIDE + sign * dy) % SIDE
        target_z = (z + SIDE + sign * dz) % SIDE
        return target_z * SIDE + target_y

    def each_target(visit):
        @pl.loop(0, SIDE)
        def _(turn):
            for index, (dy, shift) in enumerate(((1, 0), (3, 2), (2, 3), (0, 1))):
                dz = (turn + shift) % SIDE
                target = at_offset(dy, dz)
                if index < 3:
                    visit(target)
                else:
                    pl.when(turn < SIDE - 1)(functools.partial(visit, target))

    owner_load = pltpu.make_async_copy(owner_ref, owner, place_sem.at[0])
    owner_load.start()
    own_loads = []
    for k in chunks:
        load = pltpu.make_async_copy(
            grad_ref.at[:, core, :, :, cols(k)], own.at[k], own_sem.at[k]
        )
        load.start()
        own_loads.append(load)
    loads = [
        pltpu.make_async_copy(src, dst, load_sem.at[index])
        for index, (src, dst) in enumerate(
            (
                (root_left_ref, root_left),
                (root_right_ref, root_right),
                (first_ref, first),
                (second_ref, second),
                (left_ref, stat_left),
                (right_ref, stat_right),
            )
        )
    ]
    barrier = pltpu.get_barrier_semaphore()
    for partner in (mate, right, left):
        pl.semaphore_signal(barrier, inc=1, device_id={"dp": partner})

    @pl.loop(1, ranks)
    def _(step):
        pl.semaphore_signal(barrier, inc=1, device_id={"fsdp": (rank + step) % ranks})

    owner_load.wait()
    along = lax.broadcasted_iota(I32, (count, count), 1)
    down = lax.broadcasted_iota(I32, (count, count), 0)
    owner_row = owner[...]
    owner_all = jnp.broadcast_to(owner_row, (count, count)).astype(F32)
    owner_col = jnp.sum(jnp.where(along == down, owner_all, 0.0), axis=1, keepdims=True)
    same = owner_all == owner_col
    slot_row = jnp.sum(jnp.where(same & (down < along), 1.0, 0.0), axis=0, keepdims=True)
    slot_col = jnp.sum(jnp.where(same & (along < down), 1.0, 0.0), axis=1, keepdims=True)
    offset = (dp * (ranks * slots)).astype(F32)
    place_row = owner_row.astype(F32) * slots + slot_row - offset
    place_col = owner_col * slots + slot_col - offset
    number = (down - dp * per_group + 1).astype(F32)
    held_row = jnp.sum(
        jnp.where(along.astype(F32) == place_col, number, 0.0), axis=0, keepdims=True
    )
    places[0:1] = place_row.astype(I32)
    places[1:2] = held_row.astype(I32)
    place_copy = pltpu.make_async_copy(places, place, place_sem.at[1])
    place_copy.start()

    pl.semaphore_wait(barrier, ranks + 2)

    core_copies = []
    for k in chunks:
        copies = []
        for index, line in enumerate((across, ahead, behind, x)):
            copy = pltpu.make_async_remote_copy(
                src_ref=grad_ref.at[line, 1 - core, :, :, cols(k)],
                dst_ref=other.at[k, line],
                send_sem=core_send.at[k, index],
                recv_sem=core_recv.at[k, line],
                device_id={"dp": mate},
            )
            copy.start()
            copies.append(copy)
        core_copies.append(copies)
    place_copy.wait()

    def held(at):
        return place[1, at]

    def block_of(at):
        return jnp.clip(held(at) - 1, 0, per_group - 1)

    def place_of(index):
        return jnp.clip(place[0, dp * per_group + index], 0, ranks * slots - 1)

    def wait_core(k, line):
        ref = other.at[k, line]
        pltpu.make_async_copy(ref, ref, core_recv.at[k, line]).wait()

    def ring(k, index, src, dst, target):
        return pltpu.make_async_remote_copy(
            src_ref=src,
            dst_ref=dst,
            send_sem=ring_send.at[k, index],
            recv_sem=ring_recv.at[k, index],
            device_id={"dp": target},
        )

    ring_copies = [None] * CHUNKS
    low, high = pl.ds(0, half), pl.ds(half, half)

    def far_sums(k):
        copies = [
            ring(k, 0, pair.at[k, across, low], relay_right.at[k], right),
            ring(k, 1, pair.at[k, across, high], relay_left.at[k], left),
            ring(k, 2, pair.at[k, ahead, high], from_left.at[k, high], right),
            ring(k, 3, pair.at[k, behind, low], from_right.at[k, low], left),
            ring(k, 4, pair.at[k, ahead, low], from_left.at[k, low], right),
            ring(k, 5, pair.at[k, behind, high], from_right.at[k, high], left),
        ]
        ring_copies[k] = copies
        own_loads[k].wait()
        wait_core(k, across)
        pair[k, across] = own[k, across] + other[k, across]
        copies[0].start()
        copies[1].start()

    def near_sums(k):
        copies = ring_copies[k]
        wait_core(k, ahead)
        pair[k, ahead] = own[k, ahead] + other[k, ahead]
        copies[2].start()
        wait_core(k, behind)
        pair[k, behind] = own[k, behind] + other[k, behind]
        copies[3].start()

    def relay(k):
        copies = ring_copies[k]
        copies[0].wait_recv()
        pair[k, ahead, low] = pair[k, ahead, low] + relay_right[k]
        copies[4].start()
        copies[1].wait_recv()
        pair[k, behind, high] = pair[k, behind, high] + relay_left[k]
        copies[5].start()
    def finish(k):
        wait_core(k, x)
        total = own[k, x].astype(F32) + other[k, x].astype(F32)
        for copy in ring_copies[k][2:]:
            copy.wait_recv()
        total = total + from_left[k].astype(F32) + from_right[k].astype(F32)
        reduced[k] = total.astype(BF16)

        def visit(target):
            for slot in range(slots):
                outgoing[k, target, slot] = reduced[k, block_of(target * slots + slot)]
            pltpu.make_async_remote_copy(
                src_ref=outgoing.at[k, target],
                dst_ref=block.at[:, strip_rows(rank), cols(k)],
                send_sem=owner_send.at[k],
                recv_sem=owner_recv.at[k],
                device_id={"fsdp": target},
            ).start()

        each_target(visit)
        for slot in range(slots):
            block[slot, strip_rows(rank), cols(k)] = reduced[k, block_of(rank * slots + slot)]

    far_sums(0)
    near_sums(0)
    far_sums(1)
    relay(0)
    for load in loads:
        load.start()
    for k in chunks:
        if k + 1 < CHUNKS:
            near_sums(k + 1)
        if k + 2 < CHUNKS:
            far_sums(k + 2)
        if k + 1 < CHUNKS:
            relay(k + 1)
        finish(k)

    others = (ranks - 1) * strip

    def arrived(ref, sem):
        pltpu.make_async_copy(ref, ref, sem).wait()

    for k in chunks:
        arrived(block.at[:, pl.ds(0, others), cols(k)], owner_recv.at[k])
    loads[0].wait()
    loads[1].wait()

    for slot in range(slots):
        product = jnp.dot(root_left[slot], block[slot], preferred_element_type=F32)
        direction[slot] = jnp.dot(
            product.astype(BF16), root_right[slot], preferred_element_type=F32
        ).astype(BF16)

        for index, (first_leg, second_leg) in enumerate(legs_of(slot)):
            target = at_offset(first_leg[0] + second_leg[0], first_leg[1] + second_leg[1])
            pltpu.make_async_remote_copy(
                src_ref=direction.at[slot, strip_rows(target)],
                dst_ref=relayed.at[slot, index],
                send_sem=back_send.at[slot],
                recv_sem=relay_recv.at[slot, index],
                device_id={"fsdp": at_offset(*first_leg)},
            ).start()
        for offset in NEAR:
            target = at_offset(*offset)
            pltpu.make_async_remote_copy(
                src_ref=direction.at[slot, strip_rows(target)],
                dst_ref=returned.at[rank, slot],
                send_sem=back_send.at[slot],
                recv_sem=back_recv.at[slot],
                device_id={"fsdp": target},
            ).start()

    for slot in range(slots):
        for index, (first_leg, second_leg) in enumerate(legs_of(slot)):
            origin = at_offset(-first_leg[0], -first_leg[1])
            arrived(relayed.at[slot, index], relay_recv.at[slot, index])
            pltpu.make_async_remote_copy(
                src_ref=relayed.at[slot, index],
                dst_ref=returned.at[origin, slot],
                send_sem=relay_send.at[slot],
                recv_sem=back_recv.at[slot],
                device_id={"fsdp": at_offset(*second_leg)},
            ).start()

    for slot in range(slots):
        returned[rank, slot] = direction[slot, strip_rows(rank)]
        wide = direction[slot].astype(F32)
        wide = jnp.sum((wide * wide).reshape(-1, 8, columns), axis=0)
        sums[2 + slot] = functools.reduce(
            jnp.add, [wide[:, at : at + 128] for at in range(0, columns, 128)]
        )
    loads[2].wait()
    loads[3].wait()

    @pl.loop(0, per_group)
    def _(index):
        total = jnp.zeros((1, 128), F32)
        for k in chunks:
            grad = reduced[k, index].astype(F32)
            first_new = 0.9 * first[index, :, cols(k)] + 0.1 * grad
            second_new = 0.95 * second[index, :, cols(k)] + 0.05 * grad * grad
            first[index, :, cols(k)] = first_new
            second[index, :, cols(k)] = second_new
            adam = first_new / (jnp.sqrt(second_new) + 1e-08)
            part = jnp.sum(adam * adam, axis=0, keepdims=True)
            for at in range(0, width, 128):
                total = total + part[:, at : at + 128]
        sums[index // 8, pl.ds(index % 8, 1)] = total

    def send_sums(target):
        pltpu.make_async_remote_copy(
            src_ref=sums,
            dst_ref=all_sums.at[rank],
            send_sem=sums_send,
            recv_sem=sums_recv,
            device_id={"fsdp": target},
        ).start()

    each_target(send_sums)
    all_sums[rank] = sums[...]
    stores = [
        pltpu.make_async_copy(first, first_out, store_sem.at[0]),
        pltpu.make_async_copy(second, second_out, store_sem.at[1]),
    ]
    for store in stores:
        store.start()

    loads[4].wait()
    loads[5].wait()
    for stat, contract, index, out in ((stat_left, 1, 2, left_out), (stat_right, 0, 3, right_out)):
        for slot in range(slots):
            gram = lax.dot_general(
                block[slot],
                block[slot],
                (((contract,), (contract,)), ((), ())),
                preferred_element_type=F32,
            )
            used = held(rank * slots + slot) > 0
            stat[slot] = 0.95 * stat[slot] + 0.05 * jnp.where(used, gram, 0.0)
        store = pltpu.make_async_copy(stat, out, store_sem.at[index])
        store.start()
        stores.append(store)

    arrived(all_sums.at[pl.ds(0, ranks - 1)], sums_recv)
    for index in range(per_group):
        at = place_of(index)
        sizes[index] = all_sums[at // slots, 2 + at % slots]
    adam_sq = jnp.sum(all_sums[:, 0:2], axis=0).reshape(per_group, 128)
    adam_sq = jnp.sum(adam_sq, axis=1, keepdims=True)
    direction_sq = jnp.sum(jnp.sum(sizes[...], axis=1), axis=1, keepdims=True)
    graft[...] = jnp.broadcast_to(jnp.sqrt(adam_sq / (direction_sq + 1e-06)), graft.shape)

    for slot in range(slots):
        arrived(returned.at[pl.ds(0, ranks - 1), slot], back_recv.at[slot])

    @pl.loop(0, per_group)
    def _(index):
        at = place_of(index)
        scale = -graft[pl.ds(index, 1)]
        value = returned[at // slots, at % slots].astype(F32)
        update[index] = (value * jnp.concatenate([scale] * (columns // 128), axis=1)).astype(BF16)

    store = pltpu.make_async_copy(update, update_out, store_sem.at[4])
    store.start()
    stores.append(store)

    for k in chunks:
        for copy in core_copies[k] + ring_copies[k]:
            copy.wait_send()
        arrived(outgoing.at[k, pl.ds(0, ranks - 1)], owner_send.at[k])
    for slot in range(slots):
        arrived(direction.at[slot, pl.ds(0, others)], back_send.at[slot])
        arrived(relayed.at[slot], relay_send.at[slot])
    arrived(all_sums.at[pl.ds(0, ranks - 1)], sums_send)
    for store in stores:
        store.wait()


def exchange(block_owner, gradients, root_left, root_right, first, second, left, right, ranks):
    lines, _, per_group, strip, columns = gradients.shape
    slots, rows, _ = root_left.shape
    width = columns // CHUNKS
    half = per_group // 2
    anywhere = pl.BlockSpec(memory_space=pl.ANY)
    far = pl.BlockSpec(memory_space=pltpu.HBM)
    dma = pltpu.SemaphoreType.DMA
    vmem = pltpu.VMEM
    return pl.pallas_call(
        exchange_kernel,
        out_shape=(
            jax.ShapeDtypeStruct(first.shape, BF16),
            jax.ShapeDtypeStruct(first.shape, F32),
            jax.ShapeDtypeStruct(first.shape, F32),
            jax.ShapeDtypeStruct(left.shape, F32),
            jax.ShapeDtypeStruct(right.shape, F32),
        ),
        in_specs=[far] * 8,
        out_specs=(anywhere,) * 5,
        scratch_shapes=[
            vmem(block_owner.shape, I32),
            vmem((8, 128), I32),
            pltpu.SMEM((8, 128), I32),
            vmem((CHUNKS, lines, per_group, strip, width), BF16),
            vmem((CHUNKS, lines, per_group, strip, width), BF16),
            vmem((CHUNKS, lines, per_group, strip, width), BF16),
            vmem((CHUNKS, half, strip, width), BF16),
            vmem((CHUNKS, half, strip, width), BF16),
            vmem((CHUNKS, per_group, strip, width), BF16),
            vmem((CHUNKS, per_group, strip, width), BF16),
            vmem((CHUNKS, per_group, strip, width), BF16),
            vmem((CHUNKS, ranks, slots, strip, width), BF16),
            vmem((slots, rows, columns), BF16),
            vmem((slots, rows, columns), BF16),
            vmem((slots, rows, columns), BF16),
            vmem(first.shape, F32),
            vmem(first.shape, F32),
            vmem(left.shape, F32),
            vmem(right.shape, F32),
            vmem((slots, rows, columns), BF16),
            vmem((ranks, slots, strip, columns), BF16),
            vmem((slots, len(LEGS), strip, columns), BF16),
            vmem((4, 8, 128), F32),
            vmem((ranks, 4, 8, 128), F32),
            vmem((per_group, 8, 128), F32),
            vmem((per_group, 128), F32),
            vmem((per_group, strip, columns), BF16),
            dma((2,)),
            dma((CHUNKS,)),
            dma((6,)),
            dma((5,)),
            dma((CHUNKS, 4)),
            dma((CHUNKS, 4)),
            dma((CHUNKS, 6)),
            dma((CHUNKS, 6)),
            dma((CHUNKS,)),
            dma((CHUNKS,)),
            dma((slots,)),
            dma((slots,)),
            dma((slots,)),
            dma((slots, len(LEGS))),
            dma,
            dma,
        ],
        compiler_params=pltpu.CompilerParams(
            collective_id=0, has_side_effects=True, vmem_limit_bytes=40 * 2**20
        ),
        cost_estimate=pl.CostEstimate(
            flops=8 * slots * rows * rows * columns, bytes_accessed=18 * 2**20, transcendentals=0
        ),
        name="exchange",
    )(
        *(
            pltpu.with_memory_space_constraint(value, pltpu.HBM)
            for value in (
                block_owner,
                gradients,
                root_left,
                root_right,
                first,
                second,
                left,
                right,
            )
        )
    )


def publish_kernel(*refs):
    count = (len(refs) - 1) // 2
    sems = refs[-1]
    copies = [
        pltpu.make_async_copy(refs[index], refs[count + index], sems.at[index])
        for index in range(count)
    ]
    for copy in copies:
        copy.start()
    for copy in copies:
        copy.wait()


def publish(results):
    return pl.pallas_call(
        publish_kernel,
        out_shape=[jax.ShapeDtypeStruct(value.shape, value.dtype) for value in results],
        in_specs=[pl.BlockSpec(memory_space=pl.ANY)] * len(results),
        out_specs=[pl.BlockSpec(memory_space=pltpu.HBM)] * len(results),
        scratch_shapes=[pltpu.SemaphoreType.DMA((len(results),))],
        compiler_params=pltpu.CompilerParams(vmem_limit_bytes=2**20),
        name="publish",
    )(*(pltpu.with_memory_space_constraint(value, pltpu.VMEM) for value in results))


def shards(
    gradients,
    block_owner,
    left_stat,
    right_stat,
    root_left,
    root_right,
    moment_first,
    moment_second,
):
    dp_count = lax.axis_size("dp")
    ranks = lax.axis_size("fsdp")
    count = block_owner.shape[0]
    strip, columns = gradients.shape[2:]
    results = exchange(
        block_owner.reshape(1, count),
        gradients.reshape(dp_count // 2, 2, count // dp_count, strip, columns),
        root_left,
        root_right,
        moment_first,
        moment_second,
        left_stat,
        right_stat,
        ranks,
    )
    return tuple(publish(results))


def solution(mesh):
    placed = (
        P("dp", None, "fsdp", None),
        P(),
        P(("dp", "fsdp"), None, None),
        P(("dp", "fsdp"), None, None),
        P(("dp", "fsdp"), None, None),
        P(("dp", "fsdp"), None, None),
        P("dp", "fsdp", None),
        P("dp", "fsdp", None),
    )
    return jax.shard_map(
        shards,
        mesh=mesh,
        in_specs=placed,
        out_specs=(
            P("dp", "fsdp", None),
            P("dp", "fsdp", None),
            P("dp", "fsdp", None),
            P(("dp", "fsdp"), None, None),
            P(("dp", "fsdp"), None, None),
        ),
        check_vma=False,
    )
```

```python
import functools

import jax
import jax.numpy as jnp
from jax import lax
from jax.experimental import pallas as pl
from jax.experimental.pallas import tpu as pltpu
from jax.sharding import PartitionSpec as P

F32 = jnp.float32
BF16 = jnp.bfloat16
I32 = jnp.int32
CHUNKS = 4
GROUPS = ((0, 1), (2,), (3,))
SIDE = 4
NEAR = ((1, 0), (-1, 0), (0, 1), (0, -1), (1, 1), (-1, -1), (1, -1), (-1, 1))
LEGS = (
    ((1, 1), (1, 1)),
    ((-1, 1), (-1, 0)),
    ((-1, -1), (-1, 0)),
    ((1, -1), (0, -1)),
    ((-1, -1), (0, -1)),
    ((1, 0), (1, 0)),
    ((0, 1), (0, 1)),
)


def legs_of(slot):
    sign = 1 - 2 * slot
    return [tuple((sign * dy, sign * dz) for dy, dz in legs) for legs in LEGS]


def exchange_kernel(
    owner_ref,
    grad_ref,
    root_left_ref,
    root_right_ref,
    first_ref,
    second_ref,
    left_ref,
    right_ref,
    update_out,
    first_out,
    second_out,
    left_out,
    right_out,
    owner,
    places,
    place,
    own,
    other,
    pair,
    relay_right,
    relay_left,
    from_left,
    from_right,
    reduced,
    outgoing_a,
    outgoing_b,
    outgoing_c,
    block,
    root_left,
    root_right,
    first,
    second,
    stat_left,
    stat_right,
    direction,
    returned,
    relayed,
    sums,
    all_sums,
    sizes,
    graft,
    update,
    adam_sums,
    place_sem,
    own_sem,
    load_sem,
    store_sem,
    core_send,
    core_recv,
    ring_send,
    ring_recv,
    owner_send,
    owner_recv,
    back_send,
    back_recv,
    relay_send,
    relay_recv,
    sums_send,
    sums_recv,
):
    outgoing = (outgoing_a, outgoing_b, outgoing_c)
    lines, _, per_group, strip, columns = grad_ref.shape
    height, width = strip // 2, columns // 2
    half = per_group // 2
    slots, rows = block.shape[:2]
    ranks = rows // strip
    count = owner.shape[1]
    dp = lax.axis_index("dp")
    rank = lax.axis_index("fsdp")
    x = dp // 2
    core = dp % 2
    y = rank % SIDE
    z = rank // SIDE
    mate = x * 2 + (1 - core)
    sign = 1 - 2 * core
    ahead = (x + lines + sign) % lines
    behind = (x + lines - sign) % lines
    across = (x + 2) % lines
    right = ahead * 2 + core
    left = behind * 2 + core
    chunks = range(CHUNKS)

    def upper(k):
        return pl.ds(k // 2 * height, height)

    def cols(k):
        return pl.ds(k % 2 * width, width)

    def strip_rows(at):
        return pl.ds(pl.multiple_of(at * strip, strip), strip)

    def at_offset(dy, dz):
        target_y = (y + SIDE + sign * dy) % SIDE
        target_z = (z + SIDE + sign * dz) % SIDE
        return target_z * SIDE + target_y

    def each_target(visit):
        @pl.loop(0, SIDE)
        def _(turn):
            for index, (dy, shift) in enumerate(((1, 0), (3, 2), (2, 3), (0, 1))):
                dz = (turn + shift) % SIDE
                target = at_offset(dy, dz)
                if index < 3:
                    visit(target)
                else:
                    pl.when(turn < SIDE - 1)(functools.partial(visit, target))

    owner_load = pltpu.make_async_copy(owner_ref, owner, place_sem.at[0])
    owner_load.start()
    order = (across, ahead, behind, x)
    own_loads = {}
    for part in range(2):
        for index, line in enumerate(order):
            there = pl.ds(part * height, height)
            load = pltpu.make_async_copy(
                grad_ref.at[line, core, :, there],
                own.at[line, :, there],
                own_sem.at[part, index],
            )
            load.start()
            own_loads[part, index] = load
    loads = [
        pltpu.make_async_copy(src, dst, load_sem.at[index])
        for index, (src, dst) in enumerate(
            (
                (root_left_ref, root_left),
                (root_right_ref, root_right),
                (first_ref, first),
                (second_ref, second),
                (left_ref, stat_left),
                (right_ref, stat_right),
            )
        )
    ]
    barrier = pltpu.get_barrier_semaphore()
    for partner in (mate, right, left):
        pl.semaphore_signal(barrier, inc=1, device_id={"dp": partner})

    @pl.loop(1, ranks)
    def _(step):
        pl.semaphore_signal(barrier, inc=1, device_id={"fsdp": (rank + step) % ranks})

    owner_load.wait()
    along = lax.broadcasted_iota(I32, (count, count), 1)
    down = lax.broadcasted_iota(I32, (count, count), 0)
    owner_row = owner[...]
    owner_all = jnp.broadcast_to(owner_row, (count, count)).astype(F32)
    owner_col = jnp.sum(jnp.where(along == down, owner_all, 0.0), axis=1, keepdims=True)
    same = owner_all == owner_col
    slot_row = jnp.sum(jnp.where(same & (down < along), 1.0, 0.0), axis=0, keepdims=True)
    slot_col = jnp.sum(jnp.where(same & (along < down), 1.0, 0.0), axis=1, keepdims=True)
    offset = (dp * (ranks * slots)).astype(F32)
    place_row = owner_row.astype(F32) * slots + slot_row - offset
    place_col = owner_col * slots + slot_col - offset
    number = (down - dp * per_group + 1).astype(F32)
    held_row = jnp.sum(
        jnp.where(along.astype(F32) == place_col, number, 0.0), axis=0, keepdims=True
    )
    places[0:1] = place_row.astype(I32)
    places[1:2] = held_row.astype(I32)
    place_copy = pltpu.make_async_copy(places, place, place_sem.at[1])
    place_copy.start()

    pl.semaphore_wait(barrier, ranks + 2)

    core_copies = {}
    for part in range(2):
        for index, line in enumerate(order):
            there = pl.ds(part * height, height)
            copy = pltpu.make_async_remote_copy(
                src_ref=grad_ref.at[line, 1 - core, :, there],
                dst_ref=other.at[line, :, there],
                send_sem=core_send.at[part, index],
                recv_sem=core_recv.at[part, line],
                device_id={"dp": mate},
            )
            copy.start()
            core_copies[part, index] = copy
    place_copy.wait()

    def held(at):
        return place[1, at]

    def block_of(at):
        return jnp.clip(held(at) - 1, 0, per_group - 1)

    def place_of(index):
        return jnp.clip(place[0, dp * per_group + index], 0, ranks * slots - 1)

    def ready(k, index):
        if k % 2 == 0:
            part, line = k // 2, order[index]
            own_loads[part, index].wait()
            ref = other.at[line, :, upper(k)]
            pltpu.make_async_copy(ref, ref, core_recv.at[part, line]).wait()

    def both(k, index):
        line = order[index]
        return own[line, :, upper(k), cols(k)], other[line, :, upper(k), cols(k)]

    def pair_sum(k, index):
        ready(k, index)
        mine, its = both(k, index)
        pair[k, order[index]] = mine + its

    def ring(k, index, src, dst, target):
        return pltpu.make_async_remote_copy(
            src_ref=src,
            dst_ref=dst,
            send_sem=ring_send.at[k, index],
            recv_sem=ring_recv.at[k, index],
            device_id={"dp": target},
        )

    ring_copies = [None] * CHUNKS
    low, high = pl.ds(0, half), pl.ds(half, half)

    def far_sums(k):
        copies = [
            ring(k, 0, pair.at[k, across, low], relay_right.at[k], right),
            ring(k, 1, pair.at[k, across, high], relay_left.at[k], left),
            ring(k, 2, pair.at[k, ahead, high], from_left.at[k, high], right),
            ring(k, 3, pair.at[k, behind, low], from_right.at[k, low], left),
            ring(k, 4, pair.at[k, ahead, low], from_left.at[k, low], right),
            ring(k, 5, pair.at[k, behind, high], from_right.at[k, high], left),
        ]
        ring_copies[k] = copies
        pair_sum(k, 0)
        copies[0].start()
        copies[1].start()

    def near_sums(k):
        copies = ring_copies[k]
        pair_sum(k, 1)
        copies[2].start()
        pair_sum(k, 2)
        copies[3].start()

    def relay(k):
        copies = ring_copies[k]
        copies[0].wait_recv()
        pair[k, ahead, low] = pair[k, ahead, low] + relay_right[k]
        copies[4].start()
        copies[1].wait_recv()
        pair[k, behind, high] = pair[k, behind, high] + relay_left[k]
        copies[5].start()
    def finish(k):
        ready(k, 3)
        mine, its = both(k, 3)
        total = mine.astype(F32) + its.astype(F32)
        for copy in ring_copies[k][2:]:
            copy.wait_recv()
        total = total + from_left[k].astype(F32) + from_right[k].astype(F32)
        reduced[k] = total.astype(BF16)

    def group_rows(group):
        return pl.ds(
            pl.multiple_of(rank * strip + GROUPS[group][0] // 2 * height, height), height
        )

    def group_cols(group):
        return pl.ds(GROUPS[group][0] % 2 * width, len(GROUPS[group]) * width)

    def to_owners(group):
        def visit(target):
            for slot in range(slots):
                at = block_of(target * slots + slot)
                for index, k in enumerate(GROUPS[group]):
                    outgoing[group][target, slot, :, cols(index)] = reduced[k, at]
            pltpu.make_async_remote_copy(
                src_ref=outgoing[group].at[target],
                dst_ref=block.at[:, group_rows(group), group_cols(group)],
                send_sem=owner_send.at[group],
                recv_sem=owner_recv.at[group],
                device_id={"fsdp": target},
            ).start()

        each_target(visit)
        for slot in range(slots):
            at = block_of(rank * slots + slot)
            for k in GROUPS[group]:
                block[slot, group_rows(group), cols(k)] = reduced[k, at]

    def moments(k):
        step = 4

        @pl.loop(0, per_group // step)
        def _(turn):
            here = pl.ds(turn * step, step)
            grad = reduced[k, here].astype(F32)
            first_new = 0.9 * first[here, upper(k), cols(k)] + 0.1 * grad
            second_new = 0.95 * second[here, upper(k), cols(k)] + 0.05 * grad * grad
            first[here, upper(k), cols(k)] = first_new
            second[here, upper(k), cols(k)] = second_new
            adam = first_new / (jnp.sqrt(second_new) + 1e-08)
            adam = jnp.sum((adam * adam).reshape(step, height // 8, 8, width), axis=1)
            adam_sums[k, here] = adam[:, :, :128] + adam[:, :, 128:]

    far_sums(0)
    near_sums(0)
    far_sums(1)
    relay(0)
    for load in loads:
        load.start()
    near_sums(1)
    far_sums(2)
    relay(1)
    finish(0)
    loads[2].wait()
    loads[3].wait()
    near_sums(2)
    far_sums(3)
    moments(0)
    relay(2)
    finish(1)
    to_owners(0)
    near_sums(3)
    relay(3)
    moments(1)
    finish(2)
    to_owners(1)
    finish(3)
    to_owners(2)
    moments(2)
    moments(3)

    stores = [
        pltpu.make_async_copy(first, first_out, store_sem.at[0]),
        pltpu.make_async_copy(second, second_out, store_sem.at[1]),
    ]
    for store in stores:
        store.start()

    others = (ranks - 1) * strip

    def arrived(ref, sem):
        pltpu.make_async_copy(ref, ref, sem).wait()

    for group in range(len(GROUPS)):
        arrived(outgoing[group].at[pl.ds(0, ranks - 1)], owner_recv.at[group])
    loads[0].wait()
    loads[1].wait()

    for slot in range(slots):
        product = jnp.dot(root_left[slot], block[slot], preferred_element_type=F32)
        direction[slot] = jnp.dot(
            product.astype(BF16), root_right[slot], preferred_element_type=F32
        ).astype(BF16)

        for index, (first_leg, second_leg) in enumerate(legs_of(slot)):
            target = at_offset(first_leg[0] + second_leg[0], first_leg[1] + second_leg[1])
            pltpu.make_async_remote_copy(
                src_ref=direction.at[slot, strip_rows(target)],
                dst_ref=relayed.at[slot, index],
                send_sem=back_send.at[slot],
                recv_sem=relay_recv.at[slot, index],
                device_id={"fsdp": at_offset(*first_leg)},
            ).start()
        for offset in NEAR:
            target = at_offset(*offset)
            pltpu.make_async_remote_copy(
                src_ref=direction.at[slot, strip_rows(target)],
                dst_ref=returned.at[rank, slot],
                send_sem=back_send.at[slot],
                recv_sem=back_recv.at[slot],
                device_id={"fsdp": target},
            ).start()

    for slot in range(slots):
        for index, (first_leg, second_leg) in enumerate(legs_of(slot)):
            origin = at_offset(-first_leg[0], -first_leg[1])
            arrived(relayed.at[slot, index], relay_recv.at[slot, index])
            pltpu.make_async_remote_copy(
                src_ref=relayed.at[slot, index],
                dst_ref=returned.at[origin, slot],
                send_sem=relay_send.at[slot],
                recv_sem=back_recv.at[slot],
                device_id={"fsdp": at_offset(*second_leg)},
            ).start()

    for slot in range(slots):
        returned[rank, slot] = direction[slot, strip_rows(rank)]
        wide = direction[slot].astype(F32)
        wide = jnp.sum((wide * wide).reshape(-1, 8, columns), axis=0)
        sums[2 + slot] = functools.reduce(
            jnp.add, [wide[:, at : at + 128] for at in range(0, columns, 128)]
        )
    adam = jnp.sum(jnp.sum(adam_sums[...], axis=0), axis=1)
    for index in range(2):
        sums[index] = adam[index * 8 : index * 8 + 8]

    def send_sums(target):
        pltpu.make_async_remote_copy(
            src_ref=sums,
            dst_ref=all_sums.at[rank],
            send_sem=sums_send,
            recv_sem=sums_recv,
            device_id={"fsdp": target},
        ).start()

    each_target(send_sums)
    all_sums[rank] = sums[...]
    loads[4].wait()
    loads[5].wait()
    for stat, contract, index, out in ((stat_left, 1, 2, left_out), (stat_right, 0, 3, right_out)):
        for slot in range(slots):
            gram = lax.dot_general(
                block[slot],
                block[slot],
                (((contract,), (contract,)), ((), ())),
                preferred_element_type=F32,
            )
            used = held(rank * slots + slot) > 0
            stat[slot] = 0.95 * stat[slot] + 0.05 * jnp.where(used, gram, 0.0)
        store = pltpu.make_async_copy(stat, out, store_sem.at[index])
        store.start()
        stores.append(store)

    arrived(all_sums.at[pl.ds(0, ranks - 1)], sums_recv)
    for index in range(per_group):
        at = place_of(index)
        sizes[index] = all_sums[at // slots, 2 + at % slots]
    adam_sq = jnp.sum(all_sums[:, 0:2], axis=0).reshape(per_group, 128)
    adam_sq = jnp.sum(adam_sq, axis=1, keepdims=True)
    direction_sq = jnp.sum(jnp.sum(sizes[...], axis=1), axis=1, keepdims=True)
    graft[...] = jnp.broadcast_to(jnp.sqrt(adam_sq / (direction_sq + 1e-06)), graft.shape)

    for slot in range(slots):
        arrived(returned.at[pl.ds(0, ranks - 1), slot], back_recv.at[slot])

    @pl.loop(0, per_group)
    def _(index):
        at = place_of(index)
        scale = -graft[pl.ds(index, 1)]
        value = returned[at // slots, at % slots].astype(F32)
        update[index] = (value * jnp.concatenate([scale] * (columns // 128), axis=1)).astype(BF16)

    store = pltpu.make_async_copy(update, update_out, store_sem.at[4])
    store.start()
    stores.append(store)

    for k in chunks:
        for copy in ring_copies[k]:
            copy.wait_send()
    for copy in core_copies.values():
        copy.wait_send()
    for group in range(len(GROUPS)):
        arrived(outgoing[group].at[pl.ds(0, ranks - 1)], owner_send.at[group])
    for slot in range(slots):
        arrived(direction.at[slot, pl.ds(0, others)], back_send.at[slot])
        arrived(relayed.at[slot], relay_send.at[slot])
    arrived(all_sums.at[pl.ds(0, ranks - 1)], sums_send)
    for store in stores:
        store.wait()


def exchange(block_owner, gradients, root_left, root_right, first, second, left, right, ranks):
    lines, _, per_group, strip, columns = gradients.shape
    slots, rows, _ = root_left.shape
    height, width = strip // 2, columns // 2
    half = per_group // 2
    anywhere = pl.BlockSpec(memory_space=pl.ANY)
    far = pl.BlockSpec(memory_space=pltpu.HBM)
    dma = pltpu.SemaphoreType.DMA
    vmem = pltpu.VMEM
    return pl.pallas_call(
        exchange_kernel,
        out_shape=(
            jax.ShapeDtypeStruct(first.shape, BF16),
            jax.ShapeDtypeStruct(first.shape, F32),
            jax.ShapeDtypeStruct(first.shape, F32),
            jax.ShapeDtypeStruct(left.shape, F32),
            jax.ShapeDtypeStruct(right.shape, F32),
        ),
        in_specs=[far] * 8,
        out_specs=(anywhere,) * 5,
        scratch_shapes=[
            vmem(block_owner.shape, I32),
            vmem((8, 128), I32),
            pltpu.SMEM((8, 128), I32),
            vmem((lines, per_group, strip, columns), BF16),
            vmem((lines, per_group, strip, columns), BF16),
            vmem((CHUNKS, lines, per_group, height, width), BF16),
            vmem((CHUNKS, half, height, width), BF16),
            vmem((CHUNKS, half, height, width), BF16),
            vmem((CHUNKS, per_group, height, width), BF16),
            vmem((CHUNKS, per_group, height, width), BF16),
            vmem((CHUNKS, per_group, height, width), BF16),
            *(
                vmem((ranks, slots, height, len(group) * width), BF16)
                for group in GROUPS
            ),
            vmem((slots, rows, columns), BF16),
            vmem((slots, rows, columns), BF16),
            vmem((slots, rows, columns), BF16),
            vmem(first.shape, F32),
            vmem(first.shape, F32),
            vmem(left.shape, F32),
            vmem(right.shape, F32),
            vmem((slots, rows, columns), BF16),
            vmem((ranks, slots, strip, columns), BF16),
            vmem((slots, len(LEGS), strip, columns), BF16),
            vmem((4, 8, 128), F32),
            vmem((ranks, 4, 8, 128), F32),
            vmem((per_group, 8, 128), F32),
            vmem((per_group, 128), F32),
            vmem((per_group, strip, columns), BF16),
            vmem((CHUNKS, per_group, 8, 128), F32),
            dma((2,)),
            dma((2, 4)),
            dma((6,)),
            dma((5,)),
            dma((2, 4)),
            dma((2, 4)),
            dma((CHUNKS, 6)),
            dma((CHUNKS, 6)),
            dma((len(GROUPS),)),
            dma((len(GROUPS),)),
            dma((slots,)),
            dma((slots,)),
            dma((slots,)),
            dma((slots, len(LEGS))),
            dma,
            dma,
        ],
        compiler_params=pltpu.CompilerParams(
            collective_id=0, has_side_effects=True, vmem_limit_bytes=40 * 2**20
        ),
        cost_estimate=pl.CostEstimate(
            flops=8 * slots * rows * rows * columns, bytes_accessed=18 * 2**20, transcendentals=0
        ),
        name="exchange",
    )(
        *(
            pltpu.with_memory_space_constraint(value, pltpu.HBM)
            for value in (
                block_owner,
                gradients,
                root_left,
                root_right,
                first,
                second,
                left,
                right,
            )
        )
    )


def publish_kernel(*refs):
    count = (len(refs) - 1) // 2
    sems = refs[-1]
    copies = [
        pltpu.make_async_copy(refs[index], refs[count + index], sems.at[index])
        for index in range(count)
    ]
    for copy in copies:
        copy.start()
    for copy in copies:
        copy.wait()


def publish(results):
    return pl.pallas_call(
        publish_kernel,
        out_shape=[jax.ShapeDtypeStruct(value.shape, value.dtype) for value in results],
        in_specs=[pl.BlockSpec(memory_space=pl.ANY)] * len(results),
        out_specs=[pl.BlockSpec(memory_space=pltpu.HBM)] * len(results),
        scratch_shapes=[pltpu.SemaphoreType.DMA((len(results),))],
        compiler_params=pltpu.CompilerParams(vmem_limit_bytes=2**20),
        name="publish",
    )(*(pltpu.with_memory_space_constraint(value, pltpu.VMEM) for value in results))


def shards(
    gradients,
    block_owner,
    left_stat,
    right_stat,
    root_left,
    root_right,
    moment_first,
    moment_second,
):
    dp_count = lax.axis_size("dp")
    ranks = lax.axis_size("fsdp")
    count = block_owner.shape[0]
    strip, columns = gradients.shape[2:]
    results = exchange(
        block_owner.reshape(1, count),
        gradients.reshape(dp_count // 2, 2, count // dp_count, strip, columns),
        root_left,
        root_right,
        moment_first,
        moment_second,
        left_stat,
        right_stat,
        ranks,
    )
    return tuple(publish(results))


def solution(mesh):
    placed = (
        P("dp", None, "fsdp", None),
        P(),
        P(("dp", "fsdp"), None, None),
        P(("dp", "fsdp"), None, None),
        P(("dp", "fsdp"), None, None),
        P(("dp", "fsdp"), None, None),
        P("dp", "fsdp", None),
        P("dp", "fsdp", None),
    )
    return jax.shard_map(
        shards,
        mesh=mesh,
        in_specs=placed,
        out_specs=(
            P("dp", "fsdp", None),
            P("dp", "fsdp", None),
            P("dp", "fsdp", None),
            P(("dp", "fsdp"), None, None),
            P(("dp", "fsdp"), None, None),
        ),
        check_vma=False,
    )
```

```python
import functools

import jax
import jax.numpy as jnp
from jax import lax
from jax.experimental import pallas as pl
from jax.experimental.pallas import tpu as pltpu
from jax.sharding import PartitionSpec as P

F32 = jnp.float32
BF16 = jnp.bfloat16
I32 = jnp.int32
PARTS = ((0, 0, 1), (0, 1, 1), (0, 2, 2), (1, 0, 2), (1, 2, 1), (1, 3, 1))
CHUNKS = len(PARTS)
SIDE = 4
NEAR = ((1, 0), (-1, 0), (0, 1), (0, -1), (1, 1), (-1, -1), (1, -1), (-1, 1))
LEGS = (
    ((1, 1), (1, 1)),
    ((-1, 1), (-1, 0)),
    ((-1, -1), (-1, 0)),
    ((1, -1), (0, -1)),
    ((-1, -1), (0, -1)),
    ((1, 0), (1, 0)),
    ((0, 1), (0, 1)),
)


def legs_of(slot):
    sign = 1 - 2 * slot
    return [tuple((sign * dy, sign * dz) for dy, dz in legs) for legs in LEGS]


def exchange_kernel(
    owner_ref,
    grad_ref,
    root_left_ref,
    root_right_ref,
    first_ref,
    second_ref,
    left_ref,
    right_ref,
    returned,
    graft_out,
    places_out,
    first_out,
    second_out,
    left_out,
    right_out,
    owner,
    places,
    place,
    own,
    other,
    pair,
    relay_right,
    relay_left,
    from_left,
    from_right,
    reduced,
    outgoing,
    block,
    root_left,
    root_right,
    first,
    second,
    stat_left,
    stat_right,
    direction,
    relayed,
    sums,
    all_sums,
    sizes,
    graft,
    adam_sums,
    place_sem,
    own_sem,
    load_sem,
    store_sem,
    core_send,
    core_recv,
    ring_send,
    ring_recv,
    owner_send,
    owner_recv,
    back_send,
    back_recv,
    relay_send,
    relay_recv,
    sums_send,
    sums_recv,
):
    lines, _, per_group, strip, columns = grad_ref.shape
    height = strip // 2
    half = per_group // 2
    slots, rows = block.shape[:2]
    ranks = rows // strip
    count = owner.shape[1]
    dp = lax.axis_index("dp")
    rank = lax.axis_index("fsdp")
    x = dp // 2
    core = dp % 2
    y = rank % SIDE
    z = rank // SIDE
    mate = x * 2 + (1 - core)
    sign = 1 - 2 * core
    ahead = (x + lines + sign) % lines
    behind = (x + lines - sign) % lines
    across = (x + 2) % lines
    right = ahead * 2 + core
    left = behind * 2 + core
    chunks = range(CHUNKS)

    def upper(k):
        return pl.ds(PARTS[k][0] * height, height)

    def cols(k):
        return pl.ds(PARTS[k][1] * 128, PARTS[k][2] * 128)

    def strip_rows(at):
        return pl.ds(pl.multiple_of(at * strip, strip), strip)

    def at_offset(dy, dz):
        target_y = (y + SIDE + sign * dy) % SIDE
        target_z = (z + SIDE + sign * dz) % SIDE
        return target_z * SIDE + target_y

    def each_target(visit):
        @pl.loop(0, SIDE)
        def _(turn):
            for index, (dy, shift) in enumerate(((1, 0), (3, 2), (2, 3), (0, 1))):
                dz = (turn + shift) % SIDE
                target = at_offset(dy, dz)
                if index < 3:
                    visit(target)
                else:
                    pl.when(turn < SIDE - 1)(functools.partial(visit, target))

    owner_load = pltpu.make_async_copy(owner_ref, owner, place_sem.at[0])
    owner_load.start()
    order = (across, ahead, behind, x)
    own_loads = {}
    for part in range(2):
        for index, line in enumerate(order):
            there = pl.ds(part * height, height)
            load = pltpu.make_async_copy(
                grad_ref.at[line, core, :, there],
                own.at[line, :, there],
                own_sem.at[part, index],
            )
            load.start()
            own_loads[part, index] = load
    loads = [
        pltpu.make_async_copy(src, dst, load_sem.at[index])
        for index, (src, dst) in enumerate(
            (
                (root_left_ref, root_left),
                (root_right_ref, root_right),
                (first_ref, first),
                (second_ref, second),
                (left_ref, stat_left),
                (right_ref, stat_right),
            )
        )
    ]
    barrier = pltpu.get_barrier_semaphore()
    for partner in (mate, right, left):
        pl.semaphore_signal(barrier, inc=1, device_id={"dp": partner})

    @pl.loop(1, ranks)
    def _(step):
        pl.semaphore_signal(barrier, inc=1, device_id={"fsdp": (rank + step) % ranks})

    owner_load.wait()
    along = lax.broadcasted_iota(I32, (count, count), 1)
    down = lax.broadcasted_iota(I32, (count, count), 0)
    owner_row = owner[...]
    owner_all = jnp.broadcast_to(owner_row, (count, count)).astype(F32)
    owner_col = jnp.sum(jnp.where(along == down, owner_all, 0.0), axis=1, keepdims=True)
    same = owner_all == owner_col
    slot_row = jnp.sum(jnp.where(same & (down < along), 1.0, 0.0), axis=0, keepdims=True)
    slot_col = jnp.sum(jnp.where(same & (along < down), 1.0, 0.0), axis=1, keepdims=True)
    offset = (dp * (ranks * slots)).astype(F32)
    place_row = owner_row.astype(F32) * slots + slot_row - offset
    place_col = owner_col * slots + slot_col - offset
    number = (down - dp * per_group + 1).astype(F32)
    held_row = jnp.sum(
        jnp.where(along.astype(F32) == place_col, number, 0.0), axis=0, keepdims=True
    )
    places[0:1] = place_row.astype(I32)
    places[1:2] = held_row.astype(I32)
    place_copy = pltpu.make_async_copy(places, place, place_sem.at[1])
    place_copy.start()

    pl.semaphore_wait(barrier, ranks + 2)

    core_copies = {}
    for part in range(2):
        for index, line in enumerate(order):
            there = pl.ds(part * height, height)
            copy = pltpu.make_async_remote_copy(
                src_ref=grad_ref.at[line, 1 - core, :, there],
                dst_ref=other.at[line, :, there],
                send_sem=core_send.at[part, index],
                recv_sem=core_recv.at[part, line],
                device_id={"dp": mate},
            )
            copy.start()
            core_copies[part, index] = copy
    place_copy.wait()

    def held(at):
        return place[1, at]

    def block_of(at):
        return jnp.clip(held(at) - 1, 0, per_group - 1)

    def place_of(index):
        return jnp.clip(place[0, dp * per_group + index], 0, ranks * slots - 1)

    def ready(k, index):
        if PARTS[k][1] == 0:
            part, line = PARTS[k][0], order[index]
            own_loads[part, index].wait()
            ref = other.at[line, :, upper(k)]
            pltpu.make_async_copy(ref, ref, core_recv.at[part, line]).wait()

    def both(k, index):
        line = order[index]
        return own[line, :, upper(k), cols(k)], other[line, :, upper(k), cols(k)]

    def pair_sum(k, index):
        ready(k, index)
        mine, its = both(k, index)
        pair[k][order[index]] = mine + its

    def ring(k, index, src, dst, target):
        return pltpu.make_async_remote_copy(
            src_ref=src,
            dst_ref=dst,
            send_sem=ring_send.at[k, index],
            recv_sem=ring_recv.at[k, index],
            device_id={"dp": target},
        )

    ring_copies = [None] * CHUNKS
    low, high = pl.ds(0, half), pl.ds(half, half)

    def far_sums(k):
        copies = [
            ring(k, 0, pair[k].at[across, low], relay_right[k], right),
            ring(k, 1, pair[k].at[across, high], relay_left[k], left),
            ring(k, 2, pair[k].at[ahead, high], from_left[k].at[high], right),
            ring(k, 3, pair[k].at[behind, low], from_right[k].at[low], left),
            ring(k, 4, pair[k].at[ahead, low], from_left[k].at[low], right),
            ring(k, 5, pair[k].at[behind, high], from_right[k].at[high], left),
        ]
        ring_copies[k] = copies
        pair_sum(k, 0)
        copies[0].start()
        copies[1].start()

    def near_sums(k):
        copies = ring_copies[k]
        pair_sum(k, 1)
        copies[2].start()
        pair_sum(k, 2)
        copies[3].start()

    def relay(k):
        copies = ring_copies[k]
        copies[0].wait_recv()
        pair[k][ahead, low] = pair[k][ahead, low] + relay_right[k][...]
        copies[4].start()
        copies[1].wait_recv()
        pair[k][behind, high] = pair[k][behind, high] + relay_left[k][...]
        copies[5].start()
    def finish(k):
        ready(k, 3)
        mine, its = both(k, 3)
        total = mine.astype(F32) + its.astype(F32)
        for copy in ring_copies[k][2:]:
            copy.wait_recv()
        total = total + from_left[k][...].astype(F32) + from_right[k][...].astype(F32)
        reduced[k][...] = total.astype(BF16)

    def strip_part(k):
        return pl.ds(pl.multiple_of(rank * strip + PARTS[k][0] * height, height), height)

    def to_owners(k):
        def visit(target):
            for slot in range(slots):
                outgoing[k][target, slot] = reduced[k][block_of(target * slots + slot)]
            pltpu.make_async_remote_copy(
                src_ref=outgoing[k].at[target],
                dst_ref=block.at[:, strip_part(k), cols(k)],
                send_sem=owner_send.at[k],
                recv_sem=owner_recv.at[k],
                device_id={"fsdp": target},
            ).start()

        each_target(visit)
        for slot in range(slots):
            block[slot, strip_part(k), cols(k)] = reduced[k][block_of(rank * slots + slot)]

    def moments(k):
        step = 4

        @pl.loop(0, per_group // step)
        def _(turn):
            here = pl.ds(turn * step, step)
            grad = reduced[k][here].astype(F32)
            first_new = 0.9 * first[here, upper(k), cols(k)] + 0.1 * grad
            second_new = 0.95 * second[here, upper(k), cols(k)] + 0.05 * grad * grad
            first[here, upper(k), cols(k)] = first_new
            second[here, upper(k), cols(k)] = second_new
            adam = first_new / (jnp.sqrt(second_new) + 1e-08)
            adam = jnp.sum((adam * adam).reshape(step, height // 8, 8, -1), axis=1)
            adam_sums[k, here] = functools.reduce(
                jnp.add, [adam[:, :, at * 128 : at * 128 + 128] for at in range(PARTS[k][2])]
            )

    far_sums(0)
    near_sums(0)
    far_sums(1)
    relay(0)
    for load in loads:
        load.start()
    for k in chunks:
        if k + 1 < CHUNKS:
            near_sums(k + 1)
        if k + 2 < CHUNKS:
            far_sums(k + 2)
        if k + 1 < CHUNKS:
            relay(k + 1)
        if k == 1:
            loads[2].wait()
            loads[3].wait()
        if 1 <= k < CHUNKS - 2:
            moments(k - 1)
        finish(k)
        to_owners(k)
    for k in range(CHUNKS - 3, CHUNKS):
        moments(k)

    stores = [
        pltpu.make_async_copy(first, first_out, store_sem.at[0]),
        pltpu.make_async_copy(second, second_out, store_sem.at[1]),
    ]
    for store in stores:
        store.start()

    others = (ranks - 1) * strip

    def arrived(ref, sem):
        pltpu.make_async_copy(ref, ref, sem).wait()

    for k in chunks:
        arrived(outgoing[k].at[pl.ds(0, ranks - 1)], owner_recv.at[k])
    loads[0].wait()
    loads[1].wait()

    for slot in range(slots):
        product = jnp.dot(root_left[slot], block[slot], preferred_element_type=F32)
        direction[slot] = jnp.dot(
            product.astype(BF16), root_right[slot], preferred_element_type=F32
        ).astype(BF16)

        for index, (first_leg, second_leg) in enumerate(legs_of(slot)):
            target = at_offset(first_leg[0] + second_leg[0], first_leg[1] + second_leg[1])
            pltpu.make_async_remote_copy(
                src_ref=direction.at[slot, strip_rows(target)],
                dst_ref=relayed.at[slot, index],
                send_sem=back_send.at[slot],
                recv_sem=relay_recv.at[slot, index],
                device_id={"fsdp": at_offset(*first_leg)},
            ).start()
        for offset in NEAR:
            target = at_offset(*offset)
            pltpu.make_async_remote_copy(
                src_ref=direction.at[slot, strip_rows(target)],
                dst_ref=returned.at[rank, slot],
                send_sem=back_send.at[slot],
                recv_sem=back_recv.at[slot],
                device_id={"fsdp": target},
            ).start()

    for slot in range(slots):
        for index, (first_leg, second_leg) in enumerate(legs_of(slot)):
            origin = at_offset(-first_leg[0], -first_leg[1])
            arrived(relayed.at[slot, index], relay_recv.at[slot, index])
            pltpu.make_async_remote_copy(
                src_ref=relayed.at[slot, index],
                dst_ref=returned.at[origin, slot],
                send_sem=relay_send.at[slot],
                recv_sem=back_recv.at[slot],
                device_id={"fsdp": at_offset(*second_leg)},
            ).start()

    for slot in range(slots):
        keep = pltpu.make_async_copy(
            direction.at[slot, strip_rows(rank)], returned.at[rank, slot], store_sem.at[4 + slot]
        )
        keep.start()
        stores.append(keep)
        wide = direction[slot].astype(F32)
        wide = jnp.sum((wide * wide).reshape(-1, 8, columns), axis=0)
        sums[2 + slot] = functools.reduce(
            jnp.add, [wide[:, at : at + 128] for at in range(0, columns, 128)]
        )
    adam = jnp.sum(jnp.sum(adam_sums[...], axis=0), axis=1)
    for index in range(2):
        sums[index] = adam[index * 8 : index * 8 + 8]

    def send_sums(target):
        pltpu.make_async_remote_copy(
            src_ref=sums,
            dst_ref=all_sums.at[rank],
            send_sem=sums_send,
            recv_sem=sums_recv,
            device_id={"fsdp": target},
        ).start()

    each_target(send_sums)
    all_sums[rank] = sums[...]
    loads[4].wait()
    loads[5].wait()
    for stat, contract, index, out in ((stat_left, 1, 2, left_out), (stat_right, 0, 3, right_out)):
        for slot in range(slots):
            gram = lax.dot_general(
                block[slot],
                block[slot],
                (((contract,), (contract,)), ((), ())),
                preferred_element_type=F32,
            )
            used = held(rank * slots + slot) > 0
            stat[slot] = 0.95 * stat[slot] + 0.05 * jnp.where(used, gram, 0.0)
        store = pltpu.make_async_copy(stat, out, store_sem.at[index])
        store.start()
        stores.append(store)

    arrived(all_sums.at[pl.ds(0, ranks - 1)], sums_recv)
    for index in range(per_group):
        at = place_of(index)
        sizes[index] = all_sums[at // slots, 2 + at % slots]
    adam_sq = jnp.sum(all_sums[:, 0:2], axis=0).reshape(per_group, 128)
    adam_sq = jnp.sum(adam_sq, axis=1, keepdims=True)
    direction_sq = jnp.sum(jnp.sum(sizes[...], axis=1), axis=1, keepdims=True)
    graft[...] = jnp.broadcast_to(jnp.sqrt(adam_sq / (direction_sq + 1e-06)), graft.shape)

    for index, (src, out) in enumerate(((graft, graft_out), (places, places_out))):
        store = pltpu.make_async_copy(src, out, store_sem.at[6 + index])
        store.start()
        stores.append(store)
    for slot in range(slots):
        arrived(returned.at[pl.ds(0, ranks - 1), slot], back_recv.at[slot])

    for k in chunks:
        for copy in ring_copies[k]:
            copy.wait_send()
    for copy in core_copies.values():
        copy.wait_send()
    for k in chunks:
        arrived(outgoing[k].at[pl.ds(0, ranks - 1)], owner_send.at[k])
    for slot in range(slots):
        arrived(direction.at[slot, pl.ds(0, others)], back_send.at[slot])
        arrived(relayed.at[slot], relay_send.at[slot])
    arrived(all_sums.at[pl.ds(0, ranks - 1)], sums_send)
    for store in stores:
        store.wait()


def exchange(block_owner, gradients, root_left, root_right, first, second, left, right, ranks):
    lines, _, per_group, strip, columns = gradients.shape
    slots, rows, _ = root_left.shape
    height = strip // 2
    widths = [tiles * 128 for _, _, tiles in PARTS]
    half = per_group // 2
    anywhere = pl.BlockSpec(memory_space=pl.ANY)
    far = pl.BlockSpec(memory_space=pltpu.HBM)
    dma = pltpu.SemaphoreType.DMA
    vmem = pltpu.VMEM
    return pl.pallas_call(
        exchange_kernel,
        out_shape=(
            jax.ShapeDtypeStruct((ranks, slots, strip, columns), BF16),
            jax.ShapeDtypeStruct((per_group, 128), F32),
            jax.ShapeDtypeStruct((8, 128), I32),
            jax.ShapeDtypeStruct(first.shape, F32),
            jax.ShapeDtypeStruct(first.shape, F32),
            jax.ShapeDtypeStruct(left.shape, F32),
            jax.ShapeDtypeStruct(right.shape, F32),
        ),
        in_specs=[far] * 8,
        out_specs=(anywhere,) * 7,
        scratch_shapes=[
            vmem(block_owner.shape, I32),
            vmem((8, 128), I32),
            pltpu.SMEM((8, 128), I32),
            vmem((lines, per_group, strip, columns), BF16),
            vmem((lines, per_group, strip, columns), BF16),
            [vmem((lines, per_group, height, wide), BF16) for wide in widths],
            [vmem((half, height, wide), BF16) for wide in widths],
            [vmem((half, height, wide), BF16) for wide in widths],
            [vmem((per_group, height, wide), BF16) for wide in widths],
            [vmem((per_group, height, wide), BF16) for wide in widths],
            [vmem((per_group, height, wide), BF16) for wide in widths],
            [vmem((ranks, slots, height, wide), BF16) for wide in widths],
            vmem((slots, rows, columns), BF16),
            vmem((slots, rows, columns), BF16),
            vmem((slots, rows, columns), BF16),
            vmem(first.shape, F32),
            vmem(first.shape, F32),
            vmem(left.shape, F32),
            vmem(right.shape, F32),
            vmem((slots, rows, columns), BF16),
            vmem((slots, len(LEGS), strip, columns), BF16),
            vmem((4, 8, 128), F32),
            vmem((ranks, 4, 8, 128), F32),
            vmem((per_group, 8, 128), F32),
            vmem((per_group, 128), F32),
            vmem((CHUNKS, per_group, 8, 128), F32),
            dma((2,)),
            dma((2, 4)),
            dma((6,)),
            dma((8,)),
            dma((2, 4)),
            dma((2, 4)),
            dma((CHUNKS, 6)),
            dma((CHUNKS, 6)),
            dma((CHUNKS,)),
            dma((CHUNKS,)),
            dma((slots,)),
            dma((slots,)),
            dma((slots,)),
            dma((slots, len(LEGS))),
            dma,
            dma,
        ],
        compiler_params=pltpu.CompilerParams(
            collective_id=0, has_side_effects=True, vmem_limit_bytes=40 * 2**20
        ),
        cost_estimate=pl.CostEstimate(
            flops=8 * slots * rows * rows * columns, bytes_accessed=18 * 2**20, transcendentals=0
        ),
        name="exchange",
    )(
        *(
            pltpu.with_memory_space_constraint(value, pltpu.HBM)
            for value in (
                block_owner,
                gradients,
                root_left,
                root_right,
                first,
                second,
                left,
                right,
            )
        )
    )


def publish_kernel(
    returned,
    graft,
    places,
    first,
    second,
    left,
    right,
    update_out,
    first_out,
    second_out,
    left_out,
    right_out,
    place,
    update,
    sems,
):
    per_group, strip, columns = update.shape
    ranks, slots = returned.shape[:2]
    place_copy = pltpu.make_async_copy(places, place, sems.at[5])
    place_copy.start()
    pairs = ((left, left_out), (right, right_out), (first, first_out), (second, second_out))
    copies = [
        pltpu.make_async_copy(src, out, sems.at[index]) for index, (src, out) in enumerate(pairs)
    ]
    for copy in copies:
        copy.start()
    place_copy.wait()
    dp = lax.axis_index("dp")

    @pl.loop(0, per_group)
    def _(index):
        at = jnp.clip(place[0, dp * per_group + index], 0, ranks * slots - 1)
        scale = -graft[pl.ds(index, 1)]
        value = returned[at // slots, at % slots].astype(F32)
        update[index] = (value * jnp.concatenate([scale] * (columns // 128), axis=1)).astype(BF16)

    copies.append(pltpu.make_async_copy(update, update_out, sems.at[4]))
    copies[-1].start()
    for copy in copies:
        copy.wait()


def publish(results):
    returned, graft, places, first, second, left, right = results
    anywhere = pl.BlockSpec(memory_space=pl.ANY)
    near = pl.BlockSpec(memory_space=pltpu.VMEM)
    shapes = [(first.shape, BF16)] + [(value.shape, F32) for value in results[3:]]
    return pl.pallas_call(
        publish_kernel,
        out_shape=[jax.ShapeDtypeStruct(*shape) for shape in shapes],
        in_specs=[near, near] + [anywhere] * 5,
        out_specs=[pl.BlockSpec(memory_space=pltpu.HBM)] * 5,
        scratch_shapes=[
            pltpu.SMEM((8, 128), I32),
            pltpu.VMEM(first.shape, BF16),
            pltpu.SemaphoreType.DMA((6,)),
        ],
        compiler_params=pltpu.CompilerParams(vmem_limit_bytes=4 * 2**20),
        name="publish",
    )(*(pltpu.with_memory_space_constraint(value, pltpu.VMEM) for value in results))


def shards(
    gradients,
    block_owner,
    left_stat,
    right_stat,
    root_left,
    root_right,
    moment_first,
    moment_second,
):
    dp_count = lax.axis_size("dp")
    ranks = lax.axis_size("fsdp")
    count = block_owner.shape[0]
    strip, columns = gradients.shape[2:]
    results = exchange(
        block_owner.reshape(1, count),
        gradients.reshape(dp_count // 2, 2, count // dp_count, strip, columns),
        root_left,
        root_right,
        moment_first,
        moment_second,
        left_stat,
        right_stat,
        ranks,
    )
    return tuple(publish(results))


def solution(mesh):
    placed = (
        P("dp", None, "fsdp", None),
        P(),
        P(("dp", "fsdp"), None, None),
        P(("dp", "fsdp"), None, None),
        P(("dp", "fsdp"), None, None),
        P(("dp", "fsdp"), None, None),
        P("dp", "fsdp", None),
        P("dp", "fsdp", None),
    )
    return jax.shard_map(
        shards,
        mesh=mesh,
        in_specs=placed,
        out_specs=(
            P("dp", "fsdp", None),
            P("dp", "fsdp", None),
            P("dp", "fsdp", None),
            P(("dp", "fsdp"), None, None),
            P(("dp", "fsdp"), None, None),
        ),
        check_vma=False,
    )
```

```python
import functools

import jax
import jax.numpy as jnp
from jax import lax
from jax.experimental import pallas as pl
from jax.experimental.pallas import tpu as pltpu
from jax.sharding import PartitionSpec as P

F32 = jnp.float32
BF16 = jnp.bfloat16
I32 = jnp.int32
PARTS = ((0, 0, 1), (0, 1, 1), (0, 2, 2), (1, 0, 2), (1, 2, 1), (1, 3, 1))
CHUNKS = len(PARTS)
SIDE = 4
NEAR = ((1, 1), (-1, -1), (1, -1), (-1, 1), (1, 0), (-1, 0), (0, 1), (0, -1))
LEGS = (
    ((1, 1), (1, 1)),
    ((-1, 1), (-1, 0)),
    ((-1, -1), (-1, 0)),
    ((1, -1), (0, -1)),
    ((-1, -1), (0, -1)),
    ((1, 0), (1, 0)),
    ((0, 1), (0, 1)),
)


def legs_of(slot):
    sign = 1 - 2 * slot
    return [tuple((sign * dy, sign * dz) for dy, dz in legs) for legs in LEGS]


def exchange_kernel(
    owner_ref,
    grad_ref,
    root_left_ref,
    root_right_ref,
    first_ref,
    second_ref,
    left_ref,
    right_ref,
    returned,
    graft_out,
    places_out,
    first_out,
    second_out,
    left_out,
    right_out,
    owner,
    places,
    place,
    own,
    other,
    pair,
    relay_right,
    relay_left,
    from_left,
    from_right,
    reduced,
    outgoing,
    block,
    root_left,
    root_right,
    first,
    second,
    stat_left,
    stat_right,
    direction,
    relayed,
    sums,
    all_sums,
    sizes,
    graft,
    adam_sums,
    place_sem,
    own_sem,
    load_sem,
    store_sem,
    core_send,
    core_recv,
    ring_send,
    ring_recv,
    owner_send,
    owner_recv,
    back_send,
    back_recv,
    leg_send,
    relay_send,
    relay_recv,
    last_recv,
    sums_send,
    sums_recv,
):
    lines, _, per_group, strip, columns = grad_ref.shape
    height = strip // 2
    half = per_group // 2
    slots, rows = block.shape[:2]
    ranks = rows // strip
    count = owner.shape[1]
    dp = lax.axis_index("dp")
    rank = lax.axis_index("fsdp")
    x = dp // 2
    core = dp % 2
    y = rank % SIDE
    z = rank // SIDE
    mate = x * 2 + (1 - core)
    sign = 1 - 2 * core
    ahead = (x + lines + sign) % lines
    behind = (x + lines - sign) % lines
    across = (x + 2) % lines
    right = ahead * 2 + core
    left = behind * 2 + core
    chunks = range(CHUNKS)

    def upper(k):
        return pl.ds(PARTS[k][0] * height, height)

    def cols(k):
        return pl.ds(PARTS[k][1] * 128, PARTS[k][2] * 128)

    def strip_rows(at):
        return pl.ds(pl.multiple_of(at * strip, strip), strip)

    def at_offset(dy, dz):
        target_y = (y + SIDE + sign * dy) % SIDE
        target_z = (z + SIDE + sign * dz) % SIDE
        return target_z * SIDE + target_y

    def each_target(visit, turns=(0, SIDE)):
        @pl.loop(*turns)
        def _(turn):
            for index, (dy, shift) in enumerate(((1, 0), (3, 2), (2, 3), (0, 1))):
                dz = (turn + shift) % SIDE
                target = at_offset(dy, dz)
                if index < 3:
                    visit(target)
                else:
                    pl.when(turn < SIDE - 1)(functools.partial(visit, target))

    owner_load = pltpu.make_async_copy(owner_ref, owner, place_sem.at[0])
    owner_load.start()
    order = (across, ahead, behind, x)
    own_loads = {}
    for part in range(2):
        for index, line in enumerate(order):
            there = pl.ds(part * height, height)
            load = pltpu.make_async_copy(
                grad_ref.at[line, core, :, there],
                own.at[line, :, there],
                own_sem.at[part, index],
            )
            load.start()
            own_loads[part, index] = load
    loads = [
        pltpu.make_async_copy(src, dst, load_sem.at[index])
        for index, (src, dst) in enumerate(
            (
                (root_left_ref, root_left),
                (root_right_ref, root_right),
                (first_ref, first),
                (second_ref, second),
                (left_ref, stat_left),
                (right_ref, stat_right),
            )
        )
    ]
    barrier = pltpu.get_barrier_semaphore()
    for partner in (mate, right, left):
        pl.semaphore_signal(barrier, inc=1, device_id={"dp": partner})

    @pl.loop(1, ranks)
    def _(step):
        pl.semaphore_signal(barrier, inc=1, device_id={"fsdp": (rank + step) % ranks})

    owner_load.wait()
    along = lax.broadcasted_iota(I32, (count, count), 1)
    down = lax.broadcasted_iota(I32, (count, count), 0)
    owner_row = owner[...]
    owner_all = jnp.broadcast_to(owner_row, (count, count)).astype(F32)
    owner_col = jnp.sum(jnp.where(along == down, owner_all, 0.0), axis=1, keepdims=True)
    same = owner_all == owner_col
    slot_row = jnp.sum(jnp.where(same & (down < along), 1.0, 0.0), axis=0, keepdims=True)
    slot_col = jnp.sum(jnp.where(same & (along < down), 1.0, 0.0), axis=1, keepdims=True)
    offset = (dp * (ranks * slots)).astype(F32)
    place_row = owner_row.astype(F32) * slots + slot_row - offset
    place_col = owner_col * slots + slot_col - offset
    number = (down - dp * per_group + 1).astype(F32)
    held_row = jnp.sum(
        jnp.where(along.astype(F32) == place_col, number, 0.0), axis=0, keepdims=True
    )
    places[0:1] = place_row.astype(I32)
    places[1:2] = held_row.astype(I32)
    place_copy = pltpu.make_async_copy(places, place, place_sem.at[1])
    place_copy.start()

    pl.semaphore_wait(barrier, ranks + 2)

    core_copies = {}
    for part in range(2):
        for index, line in enumerate(order):
            there = pl.ds(part * height, height)
            copy = pltpu.make_async_remote_copy(
                src_ref=grad_ref.at[line, 1 - core, :, there],
                dst_ref=other.at[line, :, there],
                send_sem=core_send.at[part, index],
                recv_sem=core_recv.at[part, line],
                device_id={"dp": mate},
            )
            copy.start()
            core_copies[part, index] = copy
    place_copy.wait()

    def held(at):
        return place[1, at]

    def block_of(at):
        return jnp.clip(held(at) - 1, 0, per_group - 1)

    def place_of(index):
        return jnp.clip(place[0, dp * per_group + index], 0, ranks * slots - 1)

    def ready(k, index):
        if PARTS[k][1] == 0:
            part, line = PARTS[k][0], order[index]
            own_loads[part, index].wait()
            ref = other.at[line, :, upper(k)]
            pltpu.make_async_copy(ref, ref, core_recv.at[part, line]).wait()

    def both(k, index):
        line = order[index]
        return own[line, :, upper(k), cols(k)], other[line, :, upper(k), cols(k)]

    def pair_sum(k, index):
        ready(k, index)
        mine, its = both(k, index)
        pair[k][order[index]] = mine + its

    def ring(k, index, src, dst, target):
        return pltpu.make_async_remote_copy(
            src_ref=src,
            dst_ref=dst,
            send_sem=ring_send.at[k, index],
            recv_sem=ring_recv.at[k, index],
            device_id={"dp": target},
        )

    ring_copies = [None] * CHUNKS
    low, high = pl.ds(0, half), pl.ds(half, half)

    def far_sums(k):
        copies = [
            ring(k, 0, pair[k].at[across, low], relay_right[k], right),
            ring(k, 1, pair[k].at[across, high], relay_left[k], left),
            ring(k, 2, pair[k].at[ahead, high], from_left[k].at[high], right),
            ring(k, 3, pair[k].at[behind, low], from_right[k].at[low], left),
            ring(k, 4, pair[k].at[ahead, low], from_left[k].at[low], right),
            ring(k, 5, pair[k].at[behind, high], from_right[k].at[high], left),
        ]
        ring_copies[k] = copies
        pair_sum(k, 0)
        copies[0].start()
        copies[1].start()

    def near_sums(k):
        copies = ring_copies[k]
        pair_sum(k, 1)
        copies[2].start()
        pair_sum(k, 2)
        copies[3].start()

    def relay(k):
        copies = ring_copies[k]
        copies[0].wait_recv()
        pair[k][ahead, low] = pair[k][ahead, low] + relay_right[k][...]
        copies[4].start()
        copies[1].wait_recv()
        pair[k][behind, high] = pair[k][behind, high] + relay_left[k][...]
        copies[5].start()
    def finish(k):
        ready(k, 3)
        mine, its = both(k, 3)
        total = mine.astype(F32) + its.astype(F32)
        for copy in ring_copies[k][2:]:
            copy.wait_recv()
        total = total + from_left[k][...].astype(F32) + from_right[k][...].astype(F32)
        reduced[k][...] = total.astype(BF16)

    def strip_part(k):
        return pl.ds(pl.multiple_of(rank * strip + PARTS[k][0] * height, height), height)

    def to_owners(k, turns):
        def visit(target):
            for slot in range(slots):
                outgoing[k][target, slot] = reduced[k][block_of(target * slots + slot)]
            pltpu.make_async_remote_copy(
                src_ref=outgoing[k].at[target],
                dst_ref=block.at[:, strip_part(k), cols(k)],
                send_sem=owner_send.at[k],
                recv_sem=owner_recv.at[k],
                device_id={"fsdp": target},
            ).start()

        each_target(visit, turns)
        if turns[0] > 0:
            return
        for slot in range(slots):
            block[slot, strip_part(k), cols(k)] = reduced[k][block_of(rank * slots + slot)]

    def moments(k):
        step = 4

        @pl.loop(0, per_group // step)
        def _(turn):
            here = pl.ds(turn * step, step)
            grad = reduced[k][here].astype(F32)
            first_new = 0.9 * first[here, upper(k), cols(k)] + 0.1 * grad
            second_new = 0.95 * second[here, upper(k), cols(k)] + 0.05 * grad * grad
            first[here, upper(k), cols(k)] = first_new
            second[here, upper(k), cols(k)] = second_new
            adam = first_new / (jnp.sqrt(second_new) + 1e-08)
            adam = jnp.sum((adam * adam).reshape(step, height // 8, 8, -1), axis=1)
            adam_sums[k, here] = functools.reduce(
                jnp.add, [adam[:, :, at * 128 : at * 128 + 128] for at in range(PARTS[k][2])]
            )

    far_sums(0)
    near_sums(0)
    far_sums(1)
    relay(0)
    for load in loads:
        load.start()
    for k in chunks:
        if k + 1 < CHUNKS:
            near_sums(k + 1)
        if k + 2 < CHUNKS:
            far_sums(k + 2)
        if k > 0:
            to_owners(k - 1, (2, SIDE))
        if k + 1 < CHUNKS:
            relay(k + 1)
        if k == 1:
            loads[2].wait()
            loads[3].wait()
        if 1 <= k < CHUNKS - 2:
            moments(k - 1)
        finish(k)
        to_owners(k, (0, 2))
    to_owners(CHUNKS - 1, (2, SIDE))
    for k in range(CHUNKS - 3, CHUNKS):
        moments(k)

    stores = [
        pltpu.make_async_copy(first, first_out, store_sem.at[0]),
        pltpu.make_async_copy(second, second_out, store_sem.at[1]),
    ]
    for store in stores:
        store.start()

    def arrived(ref, sem):
        pltpu.make_async_copy(ref, ref, sem).wait()

    for k in chunks:
        arrived(outgoing[k].at[pl.ds(0, ranks - 1)], owner_recv.at[k])
    loads[0].wait()
    loads[1].wait()

    def first_legs(slot):
        for index, (first_leg, second_leg) in enumerate(legs_of(slot)):
            target = at_offset(first_leg[0] + second_leg[0], first_leg[1] + second_leg[1])
            pltpu.make_async_remote_copy(
                src_ref=direction.at[slot, strip_rows(target)],
                dst_ref=relayed.at[slot, index],
                send_sem=leg_send.at[slot],
                recv_sem=relay_recv.at[slot, index],
                device_id={"fsdp": at_offset(*first_leg)},
            ).start()

    def relays_arrived(slot):
        for index in range(len(LEGS)):
            arrived(relayed.at[slot, index], relay_recv.at[slot, index])

    def second_legs(slot):
        for index, (first_leg, second_leg) in enumerate(legs_of(slot)):
            origin = at_offset(-first_leg[0], -first_leg[1])
            pltpu.make_async_remote_copy(
                src_ref=relayed.at[slot, index],
                dst_ref=returned.at[origin, slot],
                send_sem=relay_send.at[slot],
                recv_sem=last_recv.at[slot],
                device_id={"fsdp": at_offset(*second_leg)},
            ).start()

    def near_round(lo, hi):
        for index in range(lo, hi):
            target = at_offset(*NEAR[index])
            pltpu.make_async_remote_copy(
                src_ref=direction.at[:, strip_rows(target)],
                dst_ref=returned.at[rank],
                send_sem=back_send,
                recv_sem=back_recv.at[index],
                device_id={"fsdp": target},
            ).start()

    def near_arrived(lo, hi):
        for index in range(lo, hi):
            arrived(returned.at[rank], back_recv.at[index])

    def precondition(slot):
        product = jnp.dot(root_left[slot], block[slot], preferred_element_type=F32)
        direction[slot] = jnp.dot(
            product.astype(BF16), root_right[slot], preferred_element_type=F32
        ).astype(BF16)

    def sum_squares(slot):
        wide = direction[slot].astype(F32)
        wide = jnp.sum((wide * wide).reshape(-1, 8, columns), axis=0)
        sums[2 + slot] = functools.reduce(
            jnp.add, [wide[:, at : at + 128] for at in range(0, columns, 128)]
        )

    def statistics(stat, contract, slot):
        gram = lax.dot_general(
            block[slot],
            block[slot],
            (((contract,), (contract,)), ((), ())),
            preferred_element_type=F32,
        )
        used = held(rank * slots + slot) > 0
        stat[slot] = 0.95 * stat[slot] + 0.05 * jnp.where(used, gram, 0.0)

    precondition(0)
    first_legs(0)
    precondition(1)
    first_legs(1)
    sum_squares(0)
    sum_squares(1)
    adam = jnp.sum(jnp.sum(adam_sums[...], axis=0), axis=1)
    for index in range(2):
        sums[index] = adam[index * 8 : index * 8 + 8]
    relays_arrived(0)
    near_round(0, 2)
    near_round(2, 4)
    loads[4].wait()
    loads[5].wait()
    relays_arrived(1)
    near_round(4, 8)
    statistics(stat_left, 1, 0)
    near_arrived(0, 4)
    second_legs(0)
    statistics(stat_right, 0, 0)
    near_arrived(4, 8)
    second_legs(1)

    def send_sums(target):
        pltpu.make_async_remote_copy(
            src_ref=sums,
            dst_ref=all_sums.at[rank],
            send_sem=sums_send,
            recv_sem=sums_recv,
            device_id={"fsdp": target},
        ).start()

    each_target(send_sums)
    all_sums[rank] = sums[...]
    for slot in range(slots):
        keep = pltpu.make_async_copy(
            direction.at[slot, strip_rows(rank)], returned.at[rank, slot], store_sem.at[4 + slot]
        )
        keep.start()
        stores.append(keep)
    statistics(stat_left, 1, 1)
    statistics(stat_right, 0, 1)
    for stat, index, out in ((stat_left, 2, left_out), (stat_right, 3, right_out)):
        store = pltpu.make_async_copy(stat, out, store_sem.at[index])
        store.start()
        stores.append(store)

    arrived(all_sums.at[pl.ds(0, ranks - 1)], sums_recv)
    for index in range(per_group):
        at = place_of(index)
        sizes[index] = all_sums[at // slots, 2 + at % slots]
    adam_sq = jnp.sum(all_sums[:, 0:2], axis=0).reshape(per_group, 128)
    adam_sq = jnp.sum(adam_sq, axis=1, keepdims=True)
    direction_sq = jnp.sum(jnp.sum(sizes[...], axis=1), axis=1, keepdims=True)
    graft[...] = jnp.broadcast_to(jnp.sqrt(adam_sq / (direction_sq + 1e-06)), graft.shape)
    for index, (src, out) in enumerate(((graft, graft_out), (places, places_out))):
        store = pltpu.make_async_copy(src, out, store_sem.at[6 + index])
        store.start()
        stores.append(store)
    for slot in range(slots):
        arrived(relayed.at[slot], last_recv.at[slot])

    for k in chunks:
        for copy in ring_copies[k]:
            copy.wait_send()
    for copy in core_copies.values():
        copy.wait_send()
    for k in chunks:
        arrived(outgoing[k].at[pl.ds(0, ranks - 1)], owner_send.at[k])
    arrived(returned.at[pl.ds(0, len(NEAR))], back_send)
    for slot in range(slots):
        arrived(relayed.at[slot], leg_send.at[slot])
        arrived(relayed.at[slot], relay_send.at[slot])
    arrived(all_sums.at[pl.ds(0, ranks - 1)], sums_send)
    for store in stores:
        store.wait()


def exchange(block_owner, gradients, root_left, root_right, first, second, left, right, ranks):
    lines, _, per_group, strip, columns = gradients.shape
    slots, rows, _ = root_left.shape
    height = strip // 2
    widths = [tiles * 128 for _, _, tiles in PARTS]
    half = per_group // 2
    anywhere = pl.BlockSpec(memory_space=pl.ANY)
    far = pl.BlockSpec(memory_space=pltpu.HBM)
    dma = pltpu.SemaphoreType.DMA
    vmem = pltpu.VMEM
    return pl.pallas_call(
        exchange_kernel,
        out_shape=(
            jax.ShapeDtypeStruct((ranks, slots, strip, columns), BF16),
            jax.ShapeDtypeStruct((per_group, 128), F32),
            jax.ShapeDtypeStruct((8, 128), I32),
            jax.ShapeDtypeStruct(first.shape, F32),
            jax.ShapeDtypeStruct(first.shape, F32),
            jax.ShapeDtypeStruct(left.shape, F32),
            jax.ShapeDtypeStruct(right.shape, F32),
        ),
        in_specs=[far] * 8,
        out_specs=(anywhere,) * 7,
        scratch_shapes=[
            vmem(block_owner.shape, I32),
            vmem((8, 128), I32),
            pltpu.SMEM((8, 128), I32),
            vmem((lines, per_group, strip, columns), BF16),
            vmem((lines, per_group, strip, columns), BF16),
            [vmem((lines, per_group, height, wide), BF16) for wide in widths],
            [vmem((half, height, wide), BF16) for wide in widths],
            [vmem((half, height, wide), BF16) for wide in widths],
            [vmem((per_group, height, wide), BF16) for wide in widths],
            [vmem((per_group, height, wide), BF16) for wide in widths],
            [vmem((per_group, height, wide), BF16) for wide in widths],
            [vmem((ranks, slots, height, wide), BF16) for wide in widths],
            vmem((slots, rows, columns), BF16),
            vmem((slots, rows, columns), BF16),
            vmem((slots, rows, columns), BF16),
            vmem(first.shape, F32),
            vmem(first.shape, F32),
            vmem(left.shape, F32),
            vmem(right.shape, F32),
            vmem((slots, rows, columns), BF16),
            vmem((slots, len(LEGS), strip, columns), BF16),
            vmem((4, 8, 128), F32),
            vmem((ranks, 4, 8, 128), F32),
            vmem((per_group, 8, 128), F32),
            vmem((per_group, 128), F32),
            vmem((CHUNKS, per_group, 8, 128), F32),
            dma((2,)),
            dma((2, 4)),
            dma((6,)),
            dma((8,)),
            dma((2, 4)),
            dma((2, 4)),
            dma((CHUNKS, 6)),
            dma((CHUNKS, 6)),
            dma((CHUNKS,)),
            dma((CHUNKS,)),
            dma,
            dma((len(NEAR),)),
            dma((slots,)),
            dma((slots,)),
            dma((slots, len(LEGS))),
            dma((slots,)),
            dma,
            dma,
        ],
        compiler_params=pltpu.CompilerParams(
            collective_id=0, has_side_effects=True, vmem_limit_bytes=40 * 2**20
        ),
        cost_estimate=pl.CostEstimate(
            flops=8 * slots * rows * rows * columns, bytes_accessed=18 * 2**20, transcendentals=0
        ),
        name="exchange",
    )(
        *(
            pltpu.with_memory_space_constraint(value, pltpu.HBM)
            for value in (
                block_owner,
                gradients,
                root_left,
                root_right,
                first,
                second,
                left,
                right,
            )
        )
    )


def publish_kernel(
    returned,
    graft,
    places,
    first,
    second,
    left,
    right,
    update_out,
    first_out,
    second_out,
    left_out,
    right_out,
    place,
    update,
    sems,
):
    per_group, strip, columns = update.shape
    ranks, slots = returned.shape[:2]
    place_copy = pltpu.make_async_copy(places, place, sems.at[5])
    place_copy.start()
    pairs = ((left, left_out), (right, right_out), (first, first_out), (second, second_out))
    copies = [
        pltpu.make_async_copy(src, out, sems.at[index]) for index, (src, out) in enumerate(pairs)
    ]
    for copy in copies:
        copy.start()
    place_copy.wait()
    dp = lax.axis_index("dp")

    @pl.loop(0, per_group)
    def _(index):
        at = jnp.clip(place[0, dp * per_group + index], 0, ranks * slots - 1)
        scale = -graft[pl.ds(index, 1)]
        value = returned[at // slots, at % slots].astype(F32)
        update[index] = (value * jnp.concatenate([scale] * (columns // 128), axis=1)).astype(BF16)

    copies.append(pltpu.make_async_copy(update, update_out, sems.at[4]))
    copies[-1].start()
    for copy in copies:
        copy.wait()


def publish(results):
    returned, graft, places, first, second, left, right = results
    anywhere = pl.BlockSpec(memory_space=pl.ANY)
    near = pl.BlockSpec(memory_space=pltpu.VMEM)
    shapes = [(first.shape, BF16)] + [(value.shape, F32) for value in results[3:]]
    return pl.pallas_call(
        publish_kernel,
        out_shape=[jax.ShapeDtypeStruct(*shape) for shape in shapes],
        in_specs=[near, near] + [anywhere] * 5,
        out_specs=[pl.BlockSpec(memory_space=pltpu.HBM)] * 5,
        scratch_shapes=[
            pltpu.SMEM((8, 128), I32),
            pltpu.VMEM(first.shape, BF16),
            pltpu.SemaphoreType.DMA((6,)),
        ],
        compiler_params=pltpu.CompilerParams(vmem_limit_bytes=4 * 2**20),
        name="publish",
    )(*(pltpu.with_memory_space_constraint(value, pltpu.VMEM) for value in results))


def shards(
    gradients,
    block_owner,
    left_stat,
    right_stat,
    root_left,
    root_right,
    moment_first,
    moment_second,
):
    dp_count = lax.axis_size("dp")
    ranks = lax.axis_size("fsdp")
    count = block_owner.shape[0]
    strip, columns = gradients.shape[2:]
    results = exchange(
        block_owner.reshape(1, count),
        gradients.reshape(dp_count // 2, 2, count // dp_count, strip, columns),
        root_left,
        root_right,
        moment_first,
        moment_second,
        left_stat,
        right_stat,
        ranks,
    )
    return tuple(publish(results))


def solution(mesh):
    placed = (
        P("dp", None, "fsdp", None),
        P(),
        P(("dp", "fsdp"), None, None),
        P(("dp", "fsdp"), None, None),
        P(("dp", "fsdp"), None, None),
        P(("dp", "fsdp"), None, None),
        P("dp", "fsdp", None),
        P("dp", "fsdp", None),
    )
    return jax.shard_map(
        shards,
        mesh=mesh,
        in_specs=placed,
        out_specs=(
            P("dp", "fsdp", None),
            P("dp", "fsdp", None),
            P("dp", "fsdp", None),
            P(("dp", "fsdp"), None, None),
            P(("dp", "fsdp"), None, None),
        ),
        check_vma=False,
    )
```

```python
import functools

import jax
import jax.numpy as jnp
from jax import lax
from jax.experimental import pallas as pl
from jax.experimental.pallas import tpu as pltpu
from jax.sharding import PartitionSpec as P

F32 = jnp.float32
BF16 = jnp.bfloat16
I32 = jnp.int32
PARTS = ((0, 0, 1), (0, 1, 1), (0, 2, 2), (1, 0, 2), (1, 2, 1), (1, 3, 1))
CHUNKS = len(PARTS)
SIDE = 4
NEAR = ((1, 0), (-1, 0), (0, 1), (0, -1), (1, 1), (-1, -1), (1, -1), (-1, 1))
LEGS = (
    ((1, 1), (1, 1)),
    ((-1, 1), (-1, 0)),
    ((-1, -1), (-1, 0)),
    ((1, -1), (0, -1)),
    ((-1, -1), (0, -1)),
    ((1, 0), (1, 0)),
    ((0, 1), (0, 1)),
)


def legs_of(slot):
    sign = 1 - 2 * slot
    return [tuple((sign * dy, sign * dz) for dy, dz in legs) for legs in LEGS]


def exchange_kernel(
    owner_ref,
    grad_ref,
    root_left_ref,
    root_right_ref,
    first_ref,
    second_ref,
    left_ref,
    right_ref,
    returned,
    graft_out,
    places_out,
    first_out,
    second_out,
    left_out,
    right_out,
    owner,
    places,
    place,
    own,
    lend,
    other,
    pair,
    relay_right,
    relay_left,
    from_left,
    from_right,
    reduced,
    outgoing,
    block,
    root_left,
    root_right,
    first,
    second,
    stat_left,
    stat_right,
    direction,
    relayed,
    sums,
    all_sums,
    sizes,
    graft,
    adam_sums,
    place_sem,
    own_sem,
    load_sem,
    store_sem,
    core_send,
    core_recv,
    ring_send,
    ring_recv,
    owner_send,
    owner_recv,
    back_send,
    back_recv,
    relay_send,
    relay_recv,
    sums_send,
    sums_recv,
):
    lines, _, per_group, strip, columns = grad_ref.shape
    height = strip // 2
    half = per_group // 2
    slots, rows = block.shape[:2]
    ranks = rows // strip
    count = owner.shape[1]
    dp = lax.axis_index("dp")
    rank = lax.axis_index("fsdp")
    x = dp // 2
    core = dp % 2
    y = rank % SIDE
    z = rank // SIDE
    mate = x * 2 + (1 - core)
    sign = 1 - 2 * core
    ahead = (x + lines + sign) % lines
    behind = (x + lines - sign) % lines
    across = (x + 2) % lines
    right = ahead * 2 + core
    left = behind * 2 + core
    chunks = range(CHUNKS)

    def upper(k):
        return pl.ds(PARTS[k][0] * height, height)

    def cols(k):
        return pl.ds(PARTS[k][1] * 128, PARTS[k][2] * 128)

    def strip_rows(at):
        return pl.ds(pl.multiple_of(at * strip, strip), strip)

    def at_offset(dy, dz):
        target_y = (y + SIDE + sign * dy) % SIDE
        target_z = (z + SIDE + sign * dz) % SIDE
        return target_z * SIDE + target_y

    def each_target(visit):
        @pl.loop(0, SIDE)
        def _(turn):
            for index, (dy, shift) in enumerate(((1, 0), (3, 2), (2, 3), (0, 1))):
                dz = (turn + shift) % SIDE
                target = at_offset(dy, dz)
                if index < 3:
                    visit(target)
                else:
                    pl.when(turn < SIDE - 1)(functools.partial(visit, target))

    owner_load = pltpu.make_async_copy(owner_ref, owner, place_sem.at[0])
    owner_load.start()
    order = (across, ahead, behind, x)
    lend_loads, own_loads = [], []
    for index, line in enumerate(order):
        lend_loads.append(
            pltpu.make_async_copy(grad_ref.at[line, 1 - core], lend.at[line], own_sem.at[0, index])
        )
        own_loads.append(
            pltpu.make_async_copy(grad_ref.at[line, core], own.at[line], own_sem.at[1, index])
        )
    for load in lend_loads + own_loads:
        load.start()
    loads = [
        pltpu.make_async_copy(src, dst, load_sem.at[index])
        for index, (src, dst) in enumerate(
            (
                (root_left_ref, root_left),
                (root_right_ref, root_right),
                (first_ref, first),
                (second_ref, second),
                (left_ref, stat_left),
                (right_ref, stat_right),
            )
        )
    ]
    barrier = pltpu.get_barrier_semaphore()
    for partner in (mate, right, left):
        pl.semaphore_signal(barrier, inc=1, device_id={"dp": partner})

    @pl.loop(1, ranks)
    def _(step):
        pl.semaphore_signal(barrier, inc=1, device_id={"fsdp": (rank + step) % ranks})

    owner_load.wait()
    along = lax.broadcasted_iota(I32, (count, count), 1)
    down = lax.broadcasted_iota(I32, (count, count), 0)
    owner_row = owner[...]
    owner_all = jnp.broadcast_to(owner_row, (count, count)).astype(F32)
    owner_col = jnp.sum(jnp.where(along == down, owner_all, 0.0), axis=1, keepdims=True)
    same = owner_all == owner_col
    slot_row = jnp.sum(jnp.where(same & (down < along), 1.0, 0.0), axis=0, keepdims=True)
    slot_col = jnp.sum(jnp.where(same & (along < down), 1.0, 0.0), axis=1, keepdims=True)
    offset = (dp * (ranks * slots)).astype(F32)
    place_row = owner_row.astype(F32) * slots + slot_row - offset
    place_col = owner_col * slots + slot_col - offset
    number = (down - dp * per_group + 1).astype(F32)
    held_row = jnp.sum(
        jnp.where(along.astype(F32) == place_col, number, 0.0), axis=0, keepdims=True
    )
    places[0:1] = place_row.astype(I32)
    places[1:2] = held_row.astype(I32)
    place_copy = pltpu.make_async_copy(places, place, place_sem.at[1])
    place_copy.start()

    pl.semaphore_wait(barrier, ranks + 2)

    core_copies = []
    for index, line in enumerate(order):
        lend_loads[index].wait()
        copy = pltpu.make_async_remote_copy(
            src_ref=lend.at[line],
            dst_ref=other.at[line],
            send_sem=core_send.at[index],
            recv_sem=core_recv.at[line],
            device_id={"dp": mate},
        )
        copy.start()
        core_copies.append(copy)
    place_copy.wait()

    def held(at):
        return place[1, at]

    def block_of(at):
        return jnp.clip(held(at) - 1, 0, per_group - 1)

    def place_of(index):
        return jnp.clip(place[0, dp * per_group + index], 0, ranks * slots - 1)

    def ready(k, index):
        if k == 0:
            line = order[index]
            own_loads[index].wait()
            pltpu.make_async_copy(other.at[line], other.at[line], core_recv.at[line]).wait()

    def both(k, index):
        line = order[index]
        return own[line, :, upper(k), cols(k)], other[line, :, upper(k), cols(k)]

    def pair_sum(k, index):
        ready(k, index)
        mine, its = both(k, index)
        pair[k][order[index]] = mine + its

    def ring(k, index, src, dst, target):
        return pltpu.make_async_remote_copy(
            src_ref=src,
            dst_ref=dst,
            send_sem=ring_send.at[k, index],
            recv_sem=ring_recv.at[k, index],
            device_id={"dp": target},
        )

    ring_copies = [None] * CHUNKS
    low, high = pl.ds(0, half), pl.ds(half, half)

    def far_sums(k):
        copies = [
            ring(k, 0, pair[k].at[across, low], relay_right[k], right),
            ring(k, 1, pair[k].at[across, high], relay_left[k], left),
            ring(k, 2, pair[k].at[ahead, high], from_left[k].at[high], right),
            ring(k, 3, pair[k].at[behind, low], from_right[k].at[low], left),
            ring(k, 4, pair[k].at[ahead, low], from_left[k].at[low], right),
            ring(k, 5, pair[k].at[behind, high], from_right[k].at[high], left),
        ]
        ring_copies[k] = copies
        pair_sum(k, 0)
        copies[0].start()
        copies[1].start()

    def near_sums(k):
        copies = ring_copies[k]
        pair_sum(k, 1)
        copies[2].start()
        pair_sum(k, 2)
        copies[3].start()

    def relay(k):
        copies = ring_copies[k]
        copies[0].wait_recv()
        pair[k][ahead, low] = pair[k][ahead, low] + relay_right[k][...]
        copies[4].start()
        copies[1].wait_recv()
        pair[k][behind, high] = pair[k][behind, high] + relay_left[k][...]
        copies[5].start()
    def finish(k):
        ready(k, 3)
        mine, its = both(k, 3)
        total = mine.astype(F32) + its.astype(F32)
        for copy in ring_copies[k][2:]:
            copy.wait_recv()
        total = total + from_left[k][...].astype(F32) + from_right[k][...].astype(F32)
        reduced[k][...] = total.astype(BF16)

    def strip_part(k):
        return pl.ds(pl.multiple_of(rank * strip + PARTS[k][0] * height, height), height)

    def to_owners(k):
        def visit(target):
            for slot in range(slots):
                outgoing[k][target, slot] = reduced[k][block_of(target * slots + slot)]
            pltpu.make_async_remote_copy(
                src_ref=outgoing[k].at[target],
                dst_ref=block.at[:, strip_part(k), cols(k)],
                send_sem=owner_send.at[k],
                recv_sem=owner_recv.at[k],
                device_id={"fsdp": target},
            ).start()

        each_target(visit)
        for slot in range(slots):
            block[slot, strip_part(k), cols(k)] = reduced[k][block_of(rank * slots + slot)]

    def moments(k):
        step = 4

        @pl.loop(0, per_group // step)
        def _(turn):
            here = pl.ds(turn * step, step)
            grad = reduced[k][here].astype(F32)
            first_new = 0.9 * first[here, upper(k), cols(k)] + 0.1 * grad
            second_new = 0.95 * second[here, upper(k), cols(k)] + 0.05 * grad * grad
            first[here, upper(k), cols(k)] = first_new
            second[here, upper(k), cols(k)] = second_new
            adam = first_new / (jnp.sqrt(second_new) + 1e-08)
            adam = jnp.sum((adam * adam).reshape(step, height // 8, 8, -1), axis=1)
            adam_sums[k, here] = functools.reduce(
                jnp.add, [adam[:, :, at * 128 : at * 128 + 128] for at in range(PARTS[k][2])]
            )

    far_sums(0)
    near_sums(0)
    far_sums(1)
    relay(0)
    for load in loads:
        load.start()
    for k in chunks:
        if k + 1 < CHUNKS:
            near_sums(k + 1)
        if k + 2 < CHUNKS:
            far_sums(k + 2)
        if k + 1 < CHUNKS:
            relay(k + 1)
        if k == 1:
            loads[2].wait()
            loads[3].wait()
        if 1 <= k < CHUNKS - 2:
            moments(k - 1)
        finish(k)
        to_owners(k)
    for k in range(CHUNKS - 3, CHUNKS):
        moments(k)

    stores = [
        pltpu.make_async_copy(first, first_out, store_sem.at[0]),
        pltpu.make_async_copy(second, second_out, store_sem.at[1]),
    ]
    for store in stores:
        store.start()

    others = (ranks - 1) * strip

    def arrived(ref, sem):
        pltpu.make_async_copy(ref, ref, sem).wait()

    for k in chunks:
        arrived(outgoing[k].at[pl.ds(0, ranks - 1)], owner_recv.at[k])
    loads[0].wait()
    loads[1].wait()

    for slot in range(slots):
        product = jnp.dot(root_left[slot], block[slot], preferred_element_type=F32)
        direction[slot] = jnp.dot(
            product.astype(BF16), root_right[slot], preferred_element_type=F32
        ).astype(BF16)

        for index, (first_leg, second_leg) in enumerate(legs_of(slot)):
            target = at_offset(first_leg[0] + second_leg[0], first_leg[1] + second_leg[1])
            pltpu.make_async_remote_copy(
                src_ref=direction.at[slot, strip_rows(target)],
                dst_ref=relayed.at[slot, index],
                send_sem=back_send.at[slot],
                recv_sem=relay_recv.at[slot, index],
                device_id={"fsdp": at_offset(*first_leg)},
            ).start()
        for offset in NEAR:
            target = at_offset(*offset)
            pltpu.make_async_remote_copy(
                src_ref=direction.at[slot, strip_rows(target)],
                dst_ref=returned.at[rank, slot],
                send_sem=back_send.at[slot],
                recv_sem=back_recv.at[slot],
                device_id={"fsdp": target},
            ).start()

    for slot in range(slots):
        for index, (first_leg, second_leg) in enumerate(legs_of(slot)):
            origin = at_offset(-first_leg[0], -first_leg[1])
            arrived(relayed.at[slot, index], relay_recv.at[slot, index])
            pltpu.make_async_remote_copy(
                src_ref=relayed.at[slot, index],
                dst_ref=returned.at[origin, slot],
                send_sem=relay_send.at[slot],
                recv_sem=back_recv.at[slot],
                device_id={"fsdp": at_offset(*second_leg)},
            ).start()

    for slot in range(slots):
        keep = pltpu.make_async_copy(
            direction.at[slot, strip_rows(rank)], returned.at[rank, slot], store_sem.at[4 + slot]
        )
        keep.start()
        stores.append(keep)
        wide = direction[slot].astype(F32)
        wide = jnp.sum((wide * wide).reshape(-1, 8, columns), axis=0)
        sums[2 + slot] = functools.reduce(
            jnp.add, [wide[:, at : at + 128] for at in range(0, columns, 128)]
        )
    adam = jnp.sum(jnp.sum(adam_sums[...], axis=0), axis=1)
    for index in range(2):
        sums[index] = adam[index * 8 : index * 8 + 8]

    def send_sums(target):
        pltpu.make_async_remote_copy(
            src_ref=sums,
            dst_ref=all_sums.at[rank],
            send_sem=sums_send,
            recv_sem=sums_recv,
            device_id={"fsdp": target},
        ).start()

    each_target(send_sums)
    all_sums[rank] = sums[...]
    loads[4].wait()
    loads[5].wait()
    for stat, contract, index, out in ((stat_left, 1, 2, left_out), (stat_right, 0, 3, right_out)):
        for slot in range(slots):
            gram = lax.dot_general(
                block[slot],
                block[slot],
                (((contract,), (contract,)), ((), ())),
                preferred_element_type=F32,
            )
            used = held(rank * slots + slot) > 0
            stat[slot] = 0.95 * stat[slot] + 0.05 * jnp.where(used, gram, 0.0)
        store = pltpu.make_async_copy(stat, out, store_sem.at[index])
        store.start()
        stores.append(store)

    arrived(all_sums.at[pl.ds(0, ranks - 1)], sums_recv)
    for index in range(per_group):
        at = place_of(index)
        sizes[index] = all_sums[at // slots, 2 + at % slots]
    adam_sq = jnp.sum(all_sums[:, 0:2], axis=0).reshape(per_group, 128)
    adam_sq = jnp.sum(adam_sq, axis=1, keepdims=True)
    direction_sq = jnp.sum(jnp.sum(sizes[...], axis=1), axis=1, keepdims=True)
    graft[...] = jnp.broadcast_to(jnp.sqrt(adam_sq / (direction_sq + 1e-06)), graft.shape)

    for index, (src, out) in enumerate(((graft, graft_out), (places, places_out))):
        store = pltpu.make_async_copy(src, out, store_sem.at[6 + index])
        store.start()
        stores.append(store)
    for slot in range(slots):
        arrived(returned.at[pl.ds(0, ranks - 1), slot], back_recv.at[slot])

    for k in chunks:
        for copy in ring_copies[k]:
            copy.wait_send()
    for copy in core_copies:
        copy.wait_send()
    for k in chunks:
        arrived(outgoing[k].at[pl.ds(0, ranks - 1)], owner_send.at[k])
    for slot in range(slots):
        arrived(direction.at[slot, pl.ds(0, others)], back_send.at[slot])
        arrived(relayed.at[slot], relay_send.at[slot])
    arrived(all_sums.at[pl.ds(0, ranks - 1)], sums_send)
    for store in stores:
        store.wait()


def exchange(block_owner, gradients, root_left, root_right, first, second, left, right, ranks):
    lines, _, per_group, strip, columns = gradients.shape
    slots, rows, _ = root_left.shape
    height = strip // 2
    widths = [tiles * 128 for _, _, tiles in PARTS]
    half = per_group // 2
    anywhere = pl.BlockSpec(memory_space=pl.ANY)
    far = pl.BlockSpec(memory_space=pltpu.HBM)
    dma = pltpu.SemaphoreType.DMA
    vmem = pltpu.VMEM
    return pl.pallas_call(
        exchange_kernel,
        out_shape=(
            jax.ShapeDtypeStruct((ranks, slots, strip, columns), BF16),
            jax.ShapeDtypeStruct((per_group, 128), F32),
            jax.ShapeDtypeStruct((8, 128), I32),
            jax.ShapeDtypeStruct(first.shape, F32),
            jax.ShapeDtypeStruct(first.shape, F32),
            jax.ShapeDtypeStruct(left.shape, F32),
            jax.ShapeDtypeStruct(right.shape, F32),
        ),
        in_specs=[far] * 8,
        out_specs=(anywhere,) * 7,
        scratch_shapes=[
            vmem(block_owner.shape, I32),
            vmem((8, 128), I32),
            pltpu.SMEM((8, 128), I32),
            vmem((lines, per_group, strip, columns), BF16),
            vmem((lines, per_group, strip, columns), BF16),
            vmem((lines, per_group, strip, columns), BF16),
            [vmem((lines, per_group, height, wide), BF16) for wide in widths],
            [vmem((half, height, wide), BF16) for wide in widths],
            [vmem((half, height, wide), BF16) for wide in widths],
            [vmem((per_group, height, wide), BF16) for wide in widths],
            [vmem((per_group, height, wide), BF16) for wide in widths],
            [vmem((per_group, height, wide), BF16) for wide in widths],
            [vmem((ranks, slots, height, wide), BF16) for wide in widths],
            vmem((slots, rows, columns), BF16),
            vmem((slots, rows, columns), BF16),
            vmem((slots, rows, columns), BF16),
            vmem(first.shape, F32),
            vmem(first.shape, F32),
            vmem(left.shape, F32),
            vmem(right.shape, F32),
            vmem((slots, rows, columns), BF16),
            vmem((slots, len(LEGS), strip, columns), BF16),
            vmem((4, 8, 128), F32),
            vmem((ranks, 4, 8, 128), F32),
            vmem((per_group, 8, 128), F32),
            vmem((per_group, 128), F32),
            vmem((CHUNKS, per_group, 8, 128), F32),
            dma((2,)),
            dma((2, 4)),
            dma((6,)),
            dma((8,)),
            dma((4,)),
            dma((4,)),
            dma((CHUNKS, 6)),
            dma((CHUNKS, 6)),
            dma((CHUNKS,)),
            dma((CHUNKS,)),
            dma((slots,)),
            dma((slots,)),
            dma((slots,)),
            dma((slots, len(LEGS))),
            dma,
            dma,
        ],
        compiler_params=pltpu.CompilerParams(
            collective_id=0, has_side_effects=True, vmem_limit_bytes=40 * 2**20
        ),
        cost_estimate=pl.CostEstimate(
            flops=8 * slots * rows * rows * columns, bytes_accessed=18 * 2**20, transcendentals=0
        ),
        name="exchange",
    )(
        *(
            pltpu.with_memory_space_constraint(value, pltpu.HBM)
            for value in (
                block_owner,
                gradients,
                root_left,
                root_right,
                first,
                second,
                left,
                right,
            )
        )
    )


def publish_kernel(
    returned,
    graft,
    places,
    first,
    second,
    left,
    right,
    update_out,
    first_out,
    second_out,
    left_out,
    right_out,
    place,
    update,
    sems,
):
    per_group, strip, columns = update.shape
    ranks, slots = returned.shape[:2]
    place_copy = pltpu.make_async_copy(places, place, sems.at[5])
    place_copy.start()
    pairs = ((left, left_out), (right, right_out), (first, first_out), (second, second_out))
    copies = [
        pltpu.make_async_copy(src, out, sems.at[index]) for index, (src, out) in enumerate(pairs)
    ]
    for copy in copies:
        copy.start()
    place_copy.wait()
    dp = lax.axis_index("dp")

    @pl.loop(0, per_group)
    def _(index):
        at = jnp.clip(place[0, dp * per_group + index], 0, ranks * slots - 1)
        scale = -graft[pl.ds(index, 1)]
        value = returned[at // slots, at % slots].astype(F32)
        update[index] = (value * jnp.concatenate([scale] * (columns // 128), axis=1)).astype(BF16)

    copies.append(pltpu.make_async_copy(update, update_out, sems.at[4]))
    copies[-1].start()
    for copy in copies:
        copy.wait()


def publish(results):
    returned, graft, places, first, second, left, right = results
    anywhere = pl.BlockSpec(memory_space=pl.ANY)
    near = pl.BlockSpec(memory_space=pltpu.VMEM)
    shapes = [(first.shape, BF16)] + [(value.shape, F32) for value in results[3:]]
    return pl.pallas_call(
        publish_kernel,
        out_shape=[jax.ShapeDtypeStruct(*shape) for shape in shapes],
        in_specs=[near, near] + [anywhere] * 5,
        out_specs=[pl.BlockSpec(memory_space=pltpu.HBM)] * 5,
        scratch_shapes=[
            pltpu.SMEM((8, 128), I32),
            pltpu.VMEM(first.shape, BF16),
            pltpu.SemaphoreType.DMA((6,)),
        ],
        compiler_params=pltpu.CompilerParams(vmem_limit_bytes=4 * 2**20),
        name="publish",
    )(*(pltpu.with_memory_space_constraint(value, pltpu.VMEM) for value in results))


def shards(
    gradients,
    block_owner,
    left_stat,
    right_stat,
    root_left,
    root_right,
    moment_first,
    moment_second,
):
    dp_count = lax.axis_size("dp")
    ranks = lax.axis_size("fsdp")
    count = block_owner.shape[0]
    strip, columns = gradients.shape[2:]
    results = exchange(
        block_owner.reshape(1, count),
        gradients.reshape(dp_count // 2, 2, count // dp_count, strip, columns),
        root_left,
        root_right,
        moment_first,
        moment_second,
        left_stat,
        right_stat,
        ranks,
    )
    return tuple(publish(results))


def solution(mesh):
    placed = (
        P("dp", None, "fsdp", None),
        P(),
        P(("dp", "fsdp"), None, None),
        P(("dp", "fsdp"), None, None),
        P(("dp", "fsdp"), None, None),
        P(("dp", "fsdp"), None, None),
        P("dp", "fsdp", None),
        P("dp", "fsdp", None),
    )
    return jax.shard_map(
        shards,
        mesh=mesh,
        in_specs=placed,
        out_specs=(
            P("dp", "fsdp", None),
            P("dp", "fsdp", None),
            P("dp", "fsdp", None),
            P(("dp", "fsdp"), None, None),
            P(("dp", "fsdp"), None, None),
        ),
        check_vma=False,
    )
```

```python
import functools

import jax
import jax.numpy as jnp
from jax import lax
from jax.experimental import pallas as pl
from jax.experimental.pallas import tpu as pltpu
from jax.sharding import PartitionSpec as P

F32 = jnp.float32
BF16 = jnp.bfloat16
I32 = jnp.int32
PARTS = ((0, 0, 1), (0, 1, 1), (0, 2, 2), (1, 0, 2), (1, 2, 1), (1, 3, 1))
CHUNKS = len(PARTS)
SIDE = 4
NEAR = ((1, 0), (-1, 0), (0, 1), (0, -1), (1, 1), (-1, -1), (1, -1), (-1, 1))
LEGS = (
    ((1, 1), (1, 1)),
    ((-1, 1), (-1, 0)),
    ((-1, -1), (-1, 0)),
    ((1, -1), (0, -1)),
    ((-1, -1), (0, -1)),
    ((1, 0), (1, 0)),
    ((0, 1), (0, 1)),
)


def legs_of(slot):
    sign = 1 - 2 * slot
    return [tuple((sign * dy, sign * dz) for dy, dz in legs) for legs in LEGS]


def exchange_kernel(
    owner_ref,
    grad_ref,
    root_left_ref,
    root_right_ref,
    first_ref,
    second_ref,
    left_ref,
    right_ref,
    returned,
    graft,
    places,
    first_out,
    second_out,
    left_out,
    right_out,
    owner,
    place,
    own,
    lend,
    other,
    pair,
    relay_right,
    relay_left,
    from_left,
    from_right,
    reduced,
    outgoing,
    block,
    root_left,
    root_right,
    first,
    second,
    stat_left,
    stat_right,
    direction,
    relayed,
    sums,
    all_sums,
    sizes,
    adam_sums,
    place_sem,
    own_sem,
    load_sem,
    core_send,
    core_recv,
    ring_send,
    ring_recv,
    owner_send,
    owner_recv,
    back_send,
    back_recv,
    relay_send,
    relay_recv,
    sums_send,
    sums_recv,
):
    lines, _, per_group, strip, columns = grad_ref.shape
    height = strip // 2
    half = per_group // 2
    slots, rows = block.shape[:2]
    ranks = rows // strip
    count = owner.shape[1]
    dp = lax.axis_index("dp")
    rank = lax.axis_index("fsdp")
    x = dp // 2
    core = dp % 2
    y = rank % SIDE
    z = rank // SIDE
    mate = x * 2 + (1 - core)
    sign = 1 - 2 * core
    ahead = (x + lines + sign) % lines
    behind = (x + lines - sign) % lines
    across = (x + 2) % lines
    right = ahead * 2 + core
    left = behind * 2 + core
    chunks = range(CHUNKS)

    def upper(k):
        return pl.ds(PARTS[k][0] * height, height)

    def cols(k):
        return pl.ds(PARTS[k][1] * 128, PARTS[k][2] * 128)

    def strip_rows(at):
        return pl.ds(pl.multiple_of(at * strip, strip), strip)

    def at_offset(dy, dz):
        target_y = (y + SIDE + sign * dy) % SIDE
        target_z = (z + SIDE + sign * dz) % SIDE
        return target_z * SIDE + target_y

    def each_target(visit):
        @pl.loop(0, SIDE)
        def _(turn):
            for index, (dy, shift) in enumerate(((1, 0), (3, 2), (2, 3), (0, 1))):
                dz = (turn + shift) % SIDE
                target = at_offset(dy, dz)
                if index < 3:
                    visit(target)
                else:
                    pl.when(turn < SIDE - 1)(functools.partial(visit, target))

    owner_load = pltpu.make_async_copy(owner_ref, owner, place_sem.at[0])
    owner_load.start()
    order = (across, ahead, behind, x)
    lend_loads, own_loads = [], []
    for index, line in enumerate(order):
        lend_loads.append(
            pltpu.make_async_copy(grad_ref.at[line, 1 - core], lend.at[line], own_sem.at[0, index])
        )
        own_loads.append(
            pltpu.make_async_copy(grad_ref.at[line, core], own.at[line], own_sem.at[1, index])
        )
    for load in lend_loads + own_loads:
        load.start()
    loads = [
        pltpu.make_async_copy(src, dst, load_sem.at[index])
        for index, (src, dst) in enumerate(
            (
                (root_left_ref, root_left),
                (root_right_ref, root_right),
                (first_ref, first),
                (second_ref, second),
                (left_ref, stat_left),
                (right_ref, stat_right),
            )
        )
    ]
    barrier = pltpu.get_barrier_semaphore()
    for partner in (mate, right, left):
        pl.semaphore_signal(barrier, inc=1, device_id={"dp": partner})

    @pl.loop(1, ranks)
    def _(step):
        pl.semaphore_signal(barrier, inc=1, device_id={"fsdp": (rank + step) % ranks})

    owner_load.wait()
    along = lax.broadcasted_iota(I32, (count, count), 1)
    down = lax.broadcasted_iota(I32, (count, count), 0)
    owner_row = owner[...]
    owner_all = jnp.broadcast_to(owner_row, (count, count)).astype(F32)
    owner_col = jnp.sum(jnp.where(along == down, owner_all, 0.0), axis=1, keepdims=True)
    same = owner_all == owner_col
    slot_row = jnp.sum(jnp.where(same & (down < along), 1.0, 0.0), axis=0, keepdims=True)
    slot_col = jnp.sum(jnp.where(same & (along < down), 1.0, 0.0), axis=1, keepdims=True)
    offset = (dp * (ranks * slots)).astype(F32)
    place_row = owner_row.astype(F32) * slots + slot_row - offset
    place_col = owner_col * slots + slot_col - offset
    number = (down - dp * per_group + 1).astype(F32)
    held_row = jnp.sum(
        jnp.where(along.astype(F32) == place_col, number, 0.0), axis=0, keepdims=True
    )
    places[...] = jnp.concatenate(
        [place_row, held_row, jnp.zeros((6, count), F32)], axis=0
    ).astype(I32)
    place_copy = pltpu.make_async_copy(places, place, place_sem.at[1])
    place_copy.start()

    pl.semaphore_wait(barrier, ranks + 2)

    core_copies = []
    for index, line in enumerate(order):
        lend_loads[index].wait()
        copy = pltpu.make_async_remote_copy(
            src_ref=lend.at[line],
            dst_ref=other.at[line],
            send_sem=core_send.at[index],
            recv_sem=core_recv.at[line],
            device_id={"dp": mate},
        )
        copy.start()
        core_copies.append(copy)
    place_copy.wait()

    def held(at):
        return place[1, at]

    def block_of(at):
        return jnp.clip(held(at) - 1, 0, per_group - 1)

    def place_of(index):
        return jnp.clip(place[0, dp * per_group + index], 0, ranks * slots - 1)

    def ready(k, index):
        if k == 0:
            line = order[index]
            own_loads[index].wait()
            pltpu.make_async_copy(other.at[line], other.at[line], core_recv.at[line]).wait()

    def both(k, index):
        line = order[index]
        return own[line, :, upper(k), cols(k)], other[line, :, upper(k), cols(k)]

    def pair_sum(k, index):
        ready(k, index)
        mine, its = both(k, index)
        pair[k][order[index]] = mine + its

    def ring(k, index, src, dst, target):
        return pltpu.make_async_remote_copy(
            src_ref=src,
            dst_ref=dst,
            send_sem=ring_send.at[k, index],
            recv_sem=ring_recv.at[k, index],
            device_id={"dp": target},
        )

    ring_copies = [None] * CHUNKS
    low, high = pl.ds(0, half), pl.ds(half, half)

    def far_sums(k):
        copies = [
            ring(k, 0, pair[k].at[across, low], relay_right[k], right),
            ring(k, 1, pair[k].at[across, high], relay_left[k], left),
            ring(k, 2, pair[k].at[ahead, high], from_left[k].at[high], right),
            ring(k, 3, pair[k].at[behind, low], from_right[k].at[low], left),
            ring(k, 4, pair[k].at[ahead, low], from_left[k].at[low], right),
            ring(k, 5, pair[k].at[behind, high], from_right[k].at[high], left),
        ]
        ring_copies[k] = copies
        pair_sum(k, 0)
        copies[0].start()
        copies[1].start()

    def near_sums(k):
        copies = ring_copies[k]
        pair_sum(k, 1)
        copies[2].start()
        pair_sum(k, 2)
        copies[3].start()

    def relay(k):
        copies = ring_copies[k]
        copies[0].wait_recv()
        pair[k][ahead, low] = pair[k][ahead, low] + relay_right[k][...]
        copies[4].start()
        copies[1].wait_recv()
        pair[k][behind, high] = pair[k][behind, high] + relay_left[k][...]
        copies[5].start()
    def finish(k):
        ready(k, 3)
        mine, its = both(k, 3)
        total = mine.astype(F32) + its.astype(F32)
        for copy in ring_copies[k][2:]:
            copy.wait_recv()
        total = total + from_left[k][...].astype(F32) + from_right[k][...].astype(F32)
        reduced[k][...] = total.astype(BF16)

    def strip_part(k):
        return pl.ds(pl.multiple_of(rank * strip + PARTS[k][0] * height, height), height)

    def to_owners(k):
        def visit(target):
            for slot in range(slots):
                outgoing[k][target, slot] = reduced[k][block_of(target * slots + slot)]
            pltpu.make_async_remote_copy(
                src_ref=outgoing[k].at[target],
                dst_ref=block.at[:, strip_part(k), cols(k)],
                send_sem=owner_send.at[k],
                recv_sem=owner_recv.at[k],
                device_id={"fsdp": target},
            ).start()

        each_target(visit)
        for slot in range(slots):
            block[slot, strip_part(k), cols(k)] = reduced[k][block_of(rank * slots + slot)]

    def moments(k):
        step = 4

        @pl.loop(0, per_group // step)
        def _(turn):
            here = pl.ds(turn * step, step)
            grad = reduced[k][here].astype(F32)
            first_new = 0.9 * first[here, upper(k), cols(k)] + 0.1 * grad
            second_new = 0.95 * second[here, upper(k), cols(k)] + 0.05 * grad * grad
            first_out[here, upper(k), cols(k)] = first_new
            second_out[here, upper(k), cols(k)] = second_new
            adam = first_new / (jnp.sqrt(second_new) + 1e-08)
            adam = jnp.sum((adam * adam).reshape(step, height // 8, 8, -1), axis=1)
            adam_sums[k, here] = functools.reduce(
                jnp.add, [adam[:, :, at * 128 : at * 128 + 128] for at in range(PARTS[k][2])]
            )

    far_sums(0)
    near_sums(0)
    far_sums(1)
    relay(0)
    for load in loads:
        load.start()
    for k in chunks:
        if k + 1 < CHUNKS:
            near_sums(k + 1)
        if k + 2 < CHUNKS:
            far_sums(k + 2)
        if k + 1 < CHUNKS:
            relay(k + 1)
        if k == 1:
            loads[2].wait()
            loads[3].wait()
        if 1 <= k < CHUNKS - 2:
            moments(k - 1)
        finish(k)
        to_owners(k)
    for k in range(CHUNKS - 3, CHUNKS):
        moments(k)

    def arrived(ref, sem):
        pltpu.make_async_copy(ref, ref, sem).wait()

    for k in chunks:
        arrived(outgoing[k].at[pl.ds(0, ranks - 1)], owner_recv.at[k])
    loads[0].wait()
    loads[1].wait()

    for slot in range(slots):
        product = jnp.dot(root_left[slot], block[slot], preferred_element_type=F32)
        direction[slot] = jnp.dot(
            product.astype(BF16), root_right[slot], preferred_element_type=F32
        ).astype(BF16)

        for index, (first_leg, second_leg) in enumerate(legs_of(slot)):
            target = at_offset(first_leg[0] + second_leg[0], first_leg[1] + second_leg[1])
            pltpu.make_async_remote_copy(
                src_ref=direction.at[slot, strip_rows(target)],
                dst_ref=relayed.at[slot, index],
                send_sem=back_send.at[slot],
                recv_sem=relay_recv.at[slot, index],
                device_id={"fsdp": at_offset(*first_leg)},
            ).start()
        for offset in NEAR:
            target = at_offset(*offset)
            pltpu.make_async_remote_copy(
                src_ref=direction.at[slot, strip_rows(target)],
                dst_ref=returned.at[rank, slot],
                send_sem=back_send.at[slot],
                recv_sem=back_recv.at[slot],
                device_id={"fsdp": target},
            ).start()

    for slot in range(slots):
        for index, (first_leg, second_leg) in enumerate(legs_of(slot)):
            origin = at_offset(-first_leg[0], -first_leg[1])
            arrived(relayed.at[slot, index], relay_recv.at[slot, index])
            pltpu.make_async_remote_copy(
                src_ref=relayed.at[slot, index],
                dst_ref=returned.at[origin, slot],
                send_sem=relay_send.at[slot],
                recv_sem=back_recv.at[slot],
                device_id={"fsdp": at_offset(*second_leg)},
            ).start()

    for slot in range(slots):
        returned[rank, slot] = direction[slot, strip_rows(rank)]
        wide = direction[slot].astype(F32)
        wide = jnp.sum((wide * wide).reshape(-1, 8, columns), axis=0)
        sums[2 + slot] = functools.reduce(
            jnp.add, [wide[:, at : at + 128] for at in range(0, columns, 128)]
        )
    adam = jnp.sum(jnp.sum(adam_sums[...], axis=0), axis=1)
    for index in range(2):
        sums[index] = adam[index * 8 : index * 8 + 8]

    def send_sums(target):
        pltpu.make_async_remote_copy(
            src_ref=sums,
            dst_ref=all_sums.at[rank],
            send_sem=sums_send,
            recv_sem=sums_recv,
            device_id={"fsdp": target},
        ).start()

    each_target(send_sums)
    all_sums[rank] = sums[...]
    loads[4].wait()
    loads[5].wait()
    for stat, contract, out in ((stat_left, 1, left_out), (stat_right, 0, right_out)):
        for slot in range(slots):
            gram = lax.dot_general(
                block[slot],
                block[slot],
                (((contract,), (contract,)), ((), ())),
                preferred_element_type=F32,
            )
            used = held(rank * slots + slot) > 0
            out[slot] = 0.95 * stat[slot] + 0.05 * jnp.where(used, gram, 0.0)

    arrived(all_sums.at[pl.ds(0, ranks - 1)], sums_recv)
    for index in range(per_group):
        at = place_of(index)
        sizes[index] = all_sums[at // slots, 2 + at % slots]
    adam_sq = jnp.sum(all_sums[:, 0:2], axis=0).reshape(per_group, 128)
    adam_sq = jnp.sum(adam_sq, axis=1, keepdims=True)
    direction_sq = jnp.sum(jnp.sum(sizes[...], axis=1), axis=1, keepdims=True)
    graft[...] = jnp.broadcast_to(jnp.sqrt(adam_sq / (direction_sq + 1e-06)), graft.shape)

    for slot in range(slots):
        arrived(returned.at[pl.ds(0, ranks - 1), slot], back_recv.at[slot])

    for k in chunks:
        for copy in ring_copies[k]:
            copy.wait_send()
    for copy in core_copies:
        copy.wait_send()
    for k in chunks:
        arrived(outgoing[k].at[pl.ds(0, ranks - 1)], owner_send.at[k])
    for slot in range(slots):
        arrived(direction.at[slot, pl.ds(0, (ranks - 1) * strip)], back_send.at[slot])
        arrived(relayed.at[slot], relay_send.at[slot])
    arrived(all_sums.at[pl.ds(0, ranks - 1)], sums_send)


def exchange(block_owner, gradients, root_left, root_right, first, second, left, right, ranks):
    lines, _, per_group, strip, columns = gradients.shape
    slots, rows, _ = root_left.shape
    height = strip // 2
    widths = [tiles * 128 for _, _, tiles in PARTS]
    half = per_group // 2
    far = pl.BlockSpec(memory_space=pltpu.HBM)
    dma = pltpu.SemaphoreType.DMA
    vmem = pltpu.VMEM
    return pl.pallas_call(
        exchange_kernel,
        out_shape=(
            pltpu.VMEM((ranks, slots, strip, columns), BF16),
            pltpu.VMEM((per_group, 128), F32),
            pltpu.VMEM((8, 128), I32),
            pltpu.VMEM(first.shape, F32),
            pltpu.VMEM(first.shape, F32),
            pltpu.VMEM(left.shape, F32),
            pltpu.VMEM(right.shape, F32),
        ),
        in_specs=[far] * 8,
        out_specs=(pl.BlockSpec(memory_space=pltpu.VMEM),) * 7,
        scratch_shapes=[
            vmem(block_owner.shape, I32),
            pltpu.SMEM((8, 128), I32),
            vmem((lines, per_group, strip, columns), BF16),
            vmem((lines, per_group, strip, columns), BF16),
            vmem((lines, per_group, strip, columns), BF16),
            [vmem((lines, per_group, height, wide), BF16) for wide in widths],
            [vmem((half, height, wide), BF16) for wide in widths],
            [vmem((half, height, wide), BF16) for wide in widths],
            [vmem((per_group, height, wide), BF16) for wide in widths],
            [vmem((per_group, height, wide), BF16) for wide in widths],
            [vmem((per_group, height, wide), BF16) for wide in widths],
            [vmem((ranks, slots, height, wide), BF16) for wide in widths],
            vmem((slots, rows, columns), BF16),
            vmem((slots, rows, columns), BF16),
            vmem((slots, rows, columns), BF16),
            vmem(first.shape, F32),
            vmem(first.shape, F32),
            vmem(left.shape, F32),
            vmem(right.shape, F32),
            vmem((slots, rows, columns), BF16),
            vmem((slots, len(LEGS), strip, columns), BF16),
            vmem((4, 8, 128), F32),
            vmem((ranks, 4, 8, 128), F32),
            vmem((per_group, 8, 128), F32),
            vmem((CHUNKS, per_group, 8, 128), F32),
            dma((2,)),
            dma((2, 4)),
            dma((6,)),
            dma((4,)),
            dma((4,)),
            dma((CHUNKS, 6)),
            dma((CHUNKS, 6)),
            dma((CHUNKS,)),
            dma((CHUNKS,)),
            dma((slots,)),
            dma((slots,)),
            dma((slots,)),
            dma((slots, len(LEGS))),
            dma,
            dma,
        ],
        compiler_params=pltpu.CompilerParams(
            collective_id=0, has_side_effects=True, vmem_limit_bytes=40 * 2**20
        ),
        cost_estimate=pl.CostEstimate(
            flops=8 * slots * rows * rows * columns, bytes_accessed=18 * 2**20, transcendentals=0
        ),
        name="exchange",
    )(
        *(
            pltpu.with_memory_space_constraint(value, pltpu.HBM)
            for value in (
                block_owner,
                gradients,
                root_left,
                root_right,
                first,
                second,
                left,
                right,
            )
        )
    )


def publish_kernel(
    returned,
    graft,
    places,
    first,
    second,
    left,
    right,
    update_out,
    first_out,
    second_out,
    left_out,
    right_out,
    place,
    update,
    sems,
):
    per_group, strip, columns = update.shape
    ranks, slots = returned.shape[:2]
    place_copy = pltpu.make_async_copy(places, place, sems.at[5])
    place_copy.start()
    pairs = ((left, left_out), (right, right_out), (first, first_out), (second, second_out))
    copies = [
        pltpu.make_async_copy(src, out, sems.at[index]) for index, (src, out) in enumerate(pairs)
    ]
    for copy in copies:
        copy.start()
    place_copy.wait()
    dp = lax.axis_index("dp")

    @pl.loop(0, per_group)
    def _(index):
        at = jnp.clip(place[0, dp * per_group + index], 0, ranks * slots - 1)
        scale = -graft[pl.ds(index, 1)]
        value = returned[at // slots, at % slots].astype(F32)
        update[index] = (value * jnp.concatenate([scale] * (columns // 128), axis=1)).astype(BF16)

    copies.append(pltpu.make_async_copy(update, update_out, sems.at[4]))
    copies[-1].start()
    for copy in copies:
        copy.wait()


def publish(results):
    returned, graft, places, first, second, left, right = results
    anywhere = pl.BlockSpec(memory_space=pl.ANY)
    near = pl.BlockSpec(memory_space=pltpu.VMEM)
    shapes = [(first.shape, BF16)] + [(value.shape, F32) for value in results[3:]]
    return pl.pallas_call(
        publish_kernel,
        out_shape=[jax.ShapeDtypeStruct(*shape) for shape in shapes],
        in_specs=[near, near] + [anywhere] * 5,
        out_specs=[pl.BlockSpec(memory_space=pltpu.HBM)] * 5,
        scratch_shapes=[
            pltpu.SMEM((8, 128), I32),
            pltpu.VMEM(first.shape, BF16),
            pltpu.SemaphoreType.DMA((6,)),
        ],
        compiler_params=pltpu.CompilerParams(vmem_limit_bytes=4 * 2**20),
        name="publish",
    )(*(pltpu.with_memory_space_constraint(value, pltpu.VMEM) for value in results))


def shards(
    gradients,
    block_owner,
    left_stat,
    right_stat,
    root_left,
    root_right,
    moment_first,
    moment_second,
):
    dp_count = lax.axis_size("dp")
    ranks = lax.axis_size("fsdp")
    count = block_owner.shape[0]
    strip, columns = gradients.shape[2:]
    results = exchange(
        block_owner.reshape(1, count),
        gradients.reshape(dp_count // 2, 2, count // dp_count, strip, columns),
        root_left,
        root_right,
        moment_first,
        moment_second,
        left_stat,
        right_stat,
        ranks,
    )
    return tuple(publish(results))


def solution(mesh):
    placed = (
        P("dp", None, "fsdp", None),
        P(),
        P(("dp", "fsdp"), None, None),
        P(("dp", "fsdp"), None, None),
        P(("dp", "fsdp"), None, None),
        P(("dp", "fsdp"), None, None),
        P("dp", "fsdp", None),
        P("dp", "fsdp", None),
    )
    return jax.shard_map(
        shards,
        mesh=mesh,
        in_specs=placed,
        out_specs=(
            P("dp", "fsdp", None),
            P("dp", "fsdp", None),
            P("dp", "fsdp", None),
            P(("dp", "fsdp"), None, None),
            P(("dp", "fsdp"), None, None),
        ),
        check_vma=False,
    )
```

```python
import functools

import jax
import jax.numpy as jnp
from jax import lax
from jax.experimental import pallas as pl
from jax.experimental.pallas import tpu as pltpu
from jax.sharding import PartitionSpec as P

F32 = jnp.float32
BF16 = jnp.bfloat16
I32 = jnp.int32
PARTS = ((0, 0, 1), (0, 1, 1), (0, 2, 2), (1, 0, 2), (1, 2, 1), (1, 3, 1))
CHUNKS = len(PARTS)
SIDE = 4
NEAR = ((1, 0), (-1, 0), (0, 1), (0, -1), (1, 1), (-1, -1), (1, -1), (-1, 1))
LEGS = (
    ((1, 1), (1, 1)),
    ((-1, 1), (-1, 0)),
    ((-1, -1), (-1, 0)),
    ((1, -1), (0, -1)),
    ((-1, -1), (0, -1)),
    ((1, 0), (1, 0)),
    ((0, 1), (0, 1)),
)


def legs_of(slot):
    sign = 1 - 2 * slot
    return [tuple((sign * dy, sign * dz) for dy, dz in legs) for legs in LEGS]


def exchange_kernel(
    owner_ref,
    grad_ref,
    root_left_ref,
    root_right_ref,
    first_ref,
    second_ref,
    left_ref,
    right_ref,
    returned,
    graft,
    places,
    first_out,
    second_out,
    left_out,
    right_out,
    owner,
    place,
    own,
    lend,
    other,
    pair,
    relay_right,
    relay_left,
    from_left,
    from_right,
    reduced,
    outgoing,
    block,
    root_left,
    root_right,
    first,
    second,
    stat_left,
    stat_right,
    direction,
    relayed,
    sums,
    all_sums,
    sizes,
    adam_sums,
    place_sem,
    own_sem,
    load_sem,
    core_send,
    core_recv,
    ring_send,
    ring_recv,
    owner_send,
    owner_recv,
    back_send,
    back_recv,
    relay_send,
    relay_recv,
    sums_send,
    sums_recv,
):
    lines, _, per_group, strip, columns = grad_ref.shape
    height = strip // 2
    half = per_group // 2
    slots, rows = block.shape[:2]
    ranks = rows // strip
    count = owner.shape[1]
    dp = lax.axis_index("dp")
    rank = lax.axis_index("fsdp")
    x = dp // 2
    core = dp % 2
    y = rank % SIDE
    z = rank // SIDE
    mate = x * 2 + (1 - core)
    sign = 1 - 2 * core
    ahead = (x + lines + sign) % lines
    behind = (x + lines - sign) % lines
    across = (x + 2) % lines
    right = ahead * 2 + core
    left = behind * 2 + core
    chunks = range(CHUNKS)

    def upper(k):
        return pl.ds(PARTS[k][0] * height, height)

    def cols(k):
        return pl.ds(PARTS[k][1] * 128, PARTS[k][2] * 128)

    def strip_rows(at):
        return pl.ds(pl.multiple_of(at * strip, strip), strip)

    def at_offset(dy, dz):
        target_y = (y + SIDE + sign * dy) % SIDE
        target_z = (z + SIDE + sign * dz) % SIDE
        return target_z * SIDE + target_y

    def each_target(visit):
        @pl.loop(0, SIDE)
        def _(turn):
            for index, (dy, shift) in enumerate(((1, 0), (3, 2), (2, 3), (0, 1))):
                dz = (turn + shift) % SIDE
                target = at_offset(dy, dz)
                if index < 3:
                    visit(target)
                else:
                    pl.when(turn < SIDE - 1)(functools.partial(visit, target))

    owner_load = pltpu.make_async_copy(owner_ref, owner, place_sem.at[0])
    owner_load.start()
    order = (across, ahead, behind, x)
    lend_loads, own_loads = [], []
    for index, line in enumerate(order):
        lend_loads.append(
            pltpu.make_async_copy(grad_ref.at[line, 1 - core], lend.at[line], own_sem.at[0, index])
        )
        own_loads.append(
            pltpu.make_async_copy(grad_ref.at[line, core], own.at[line], own_sem.at[1, index])
        )
    for load in lend_loads + own_loads:
        load.start()
    loads = [
        pltpu.make_async_copy(src, dst, load_sem.at[index])
        for index, (src, dst) in enumerate(
            (
                (root_left_ref, root_left),
                (root_right_ref, root_right),
                (first_ref, first),
                (second_ref, second),
                (left_ref, stat_left),
                (right_ref, stat_right),
            )
        )
    ]
    barrier = pltpu.get_barrier_semaphore()
    for partner in (mate, right, left):
        pl.semaphore_signal(barrier, inc=1, device_id={"dp": partner})

    @pl.loop(1, ranks)
    def _(step):
        pl.semaphore_signal(barrier, inc=1, device_id={"fsdp": (rank + step) % ranks})

    owner_load.wait()
    along = lax.broadcasted_iota(I32, (count, count), 1)
    down = lax.broadcasted_iota(I32, (count, count), 0)
    owner_row = owner[...]
    owner_all = jnp.broadcast_to(owner_row, (count, count)).astype(F32)
    owner_col = jnp.sum(jnp.where(along == down, owner_all, 0.0), axis=1, keepdims=True)
    same = owner_all == owner_col
    slot_row = jnp.sum(jnp.where(same & (down < along), 1.0, 0.0), axis=0, keepdims=True)
    slot_col = jnp.sum(jnp.where(same & (along < down), 1.0, 0.0), axis=1, keepdims=True)
    offset = (dp * (ranks * slots)).astype(F32)
    place_row = owner_row.astype(F32) * slots + slot_row - offset
    place_col = owner_col * slots + slot_col - offset
    number = (down - dp * per_group + 1).astype(F32)
    held_row = jnp.sum(
        jnp.where(along.astype(F32) == place_col, number, 0.0), axis=0, keepdims=True
    )
    places[...] = jnp.concatenate(
        [place_row, held_row, jnp.zeros((6, count), F32)], axis=0
    ).astype(I32)
    place_copy = pltpu.make_async_copy(places, place, place_sem.at[1])
    place_copy.start()

    pl.semaphore_wait(barrier, ranks + 2)

    core_copies = []
    for index, line in enumerate(order):
        lend_loads[index].wait()
        copy = pltpu.make_async_remote_copy(
            src_ref=lend.at[line],
            dst_ref=other.at[line],
            send_sem=core_send.at[index],
            recv_sem=core_recv.at[line],
            device_id={"dp": mate},
        )
        copy.start()
        core_copies.append(copy)
    place_copy.wait()

    def held(at):
        return place[1, at]

    def block_of(at):
        return jnp.clip(held(at) - 1, 0, per_group - 1)

    def place_of(index):
        return jnp.clip(place[0, dp * per_group + index], 0, ranks * slots - 1)

    def ready(k, index):
        if k == 0:
            line = order[index]
            own_loads[index].wait()
            pltpu.make_async_copy(other.at[line], other.at[line], core_recv.at[line]).wait()

    def both(k, index):
        line = order[index]
        return own[line, :, upper(k), cols(k)], other[line, :, upper(k), cols(k)]

    def pair_sum(k, index):
        ready(k, index)
        mine, its = both(k, index)
        pair[k][order[index]] = mine + its

    def ring(k, index, src, dst, target):
        return pltpu.make_async_remote_copy(
            src_ref=src,
            dst_ref=dst,
            send_sem=ring_send.at[k, index],
            recv_sem=ring_recv.at[k, index],
            device_id={"dp": target},
        )

    ring_copies = [None] * CHUNKS
    low, high = pl.ds(0, half), pl.ds(half, half)

    def far_sums(k):
        copies = [
            ring(k, 0, pair[k].at[across, low], relay_right[k], right),
            ring(k, 1, pair[k].at[across, high], relay_left[k], left),
            ring(k, 2, pair[k].at[ahead, high], from_left[k].at[high], right),
            ring(k, 3, pair[k].at[behind, low], from_right[k].at[low], left),
            ring(k, 4, pair[k].at[ahead, low], from_left[k].at[low], right),
            ring(k, 5, pair[k].at[behind, high], from_right[k].at[high], left),
        ]
        ring_copies[k] = copies
        pair_sum(k, 0)
        copies[0].start()
        copies[1].start()

    def near_sums(k):
        copies = ring_copies[k]
        pair_sum(k, 1)
        copies[2].start()
        pair_sum(k, 2)
        copies[3].start()

    def relay(k):
        copies = ring_copies[k]
        copies[0].wait_recv()
        pair[k][ahead, low] = pair[k][ahead, low] + relay_right[k][...]
        copies[4].start()
        copies[1].wait_recv()
        pair[k][behind, high] = pair[k][behind, high] + relay_left[k][...]
        copies[5].start()
    def finish(k):
        ready(k, 3)
        mine, its = both(k, 3)
        total = mine.astype(F32) + its.astype(F32)
        for copy in ring_copies[k][2:]:
            copy.wait_recv()
        total = total + from_left[k][...].astype(F32) + from_right[k][...].astype(F32)
        reduced[k][...] = total.astype(BF16)

    def strip_part(k):
        return pl.ds(pl.multiple_of(rank * strip + PARTS[k][0] * height, height), height)

    def to_owners(k):
        def visit(target):
            for slot in range(slots):
                outgoing[k][target, slot] = reduced[k][block_of(target * slots + slot)]
            pltpu.make_async_remote_copy(
                src_ref=outgoing[k].at[target],
                dst_ref=block.at[:, strip_part(k), cols(k)],
                send_sem=owner_send.at[k],
                recv_sem=owner_recv.at[k],
                device_id={"fsdp": target},
            ).start()

        each_target(visit)
        for slot in range(slots):
            block[slot, strip_part(k), cols(k)] = reduced[k][block_of(rank * slots + slot)]

    def moments(k):
        step = 4

        @pl.loop(0, per_group // step)
        def _(turn):
            here = pl.ds(turn * step, step)
            grad = reduced[k][here].astype(F32)
            first_new = 0.9 * first[here, upper(k), cols(k)] + 0.1 * grad
            second_new = 0.95 * second[here, upper(k), cols(k)] + 0.05 * grad * grad
            first_out[here, upper(k), cols(k)] = first_new
            second_out[here, upper(k), cols(k)] = second_new
            adam = first_new / (jnp.sqrt(second_new) + 1e-08)
            adam = jnp.sum((adam * adam).reshape(step, height // 8, 8, -1), axis=1)
            adam_sums[k, here] = functools.reduce(
                jnp.add, [adam[:, :, at * 128 : at * 128 + 128] for at in range(PARTS[k][2])]
            )

    far_sums(0)
    near_sums(0)
    far_sums(1)
    relay(0)
    for load in loads:
        load.start()
    for k in chunks:
        if k + 1 < CHUNKS:
            near_sums(k + 1)
        if k + 2 < CHUNKS:
            far_sums(k + 2)
        if k + 1 < CHUNKS:
            relay(k + 1)
        if k == 1:
            loads[2].wait()
            loads[3].wait()
        if 1 <= k < CHUNKS - 2:
            moments(k - 1)
        finish(k)
        to_owners(k)
    for k in range(CHUNKS - 3, CHUNKS):
        moments(k)

    def arrived(ref, sem):
        pltpu.make_async_copy(ref, ref, sem).wait()

    for k in chunks:
        arrived(outgoing[k].at[pl.ds(0, ranks - 1)], owner_recv.at[k])
    loads[0].wait()
    loads[1].wait()

    def precondition(slot):
        product = jnp.dot(root_left[slot], block[slot], preferred_element_type=F32)
        direction[slot] = jnp.dot(
            product.astype(BF16), root_right[slot], preferred_element_type=F32
        ).astype(BF16)

    def first_legs(slot):
        for index, (first_leg, second_leg) in enumerate(legs_of(slot)):
            target = at_offset(first_leg[0] + second_leg[0], first_leg[1] + second_leg[1])
            pltpu.make_async_remote_copy(
                src_ref=direction.at[slot, strip_rows(target)],
                dst_ref=relayed.at[slot, index],
                send_sem=back_send.at[slot],
                recv_sem=relay_recv.at[slot, index],
                device_id={"fsdp": at_offset(*first_leg)},
            ).start()

    def direct(slot):
        for offset in NEAR:
            target = at_offset(*offset)
            pltpu.make_async_remote_copy(
                src_ref=direction.at[slot, strip_rows(target)],
                dst_ref=returned.at[rank, slot],
                send_sem=back_send.at[slot],
                recv_sem=back_recv.at[slot],
                device_id={"fsdp": target},
            ).start()
        returned[rank, slot] = direction[slot, strip_rows(rank)]

    def second_legs(slot):
        for index, (first_leg, second_leg) in enumerate(legs_of(slot)):
            origin = at_offset(-first_leg[0], -first_leg[1])
            arrived(relayed.at[slot, index], relay_recv.at[slot, index])
            pltpu.make_async_remote_copy(
                src_ref=relayed.at[slot, index],
                dst_ref=returned.at[origin, slot],
                send_sem=relay_send.at[slot],
                recv_sem=back_recv.at[slot],
                device_id={"fsdp": at_offset(*second_leg)},
            ).start()

    def squares(slot):
        wide = direction[slot].astype(F32)
        wide = jnp.sum(jnp.sum((wide * wide).reshape(-1, 8, columns), axis=0), axis=0, keepdims=True)
        return jnp.sum(wide, axis=1, keepdims=True)

    def send_sums(target):
        pltpu.make_async_remote_copy(
            src_ref=sums,
            dst_ref=all_sums.at[rank],
            send_sem=sums_send,
            recv_sem=sums_recv,
            device_id={"fsdp": target},
        ).start()

    adam = jnp.sum(jnp.sum(jnp.sum(adam_sums[...], axis=0), axis=1), axis=1, keepdims=True)
    lane = lax.broadcasted_iota(I32, (8, 128), 1)
    precondition(0)
    first_legs(0)
    direct(0)
    precondition(1)
    first_legs(1)
    tile = jnp.where(lane == 0, adam[:8], 0.0) + jnp.where(lane == 1, adam[8:], 0.0)
    for slot in range(slots):
        tile = tile + jnp.where(lane == 2 + slot, squares(slot), 0.0)
    sums[...] = tile
    all_sums[rank] = tile
    each_target(send_sums)
    direct(1)
    second_legs(0)
    second_legs(1)

    loads[4].wait()
    loads[5].wait()
    for stat, contract, out in ((stat_left, 1, left_out), (stat_right, 0, right_out)):
        for slot in range(slots):
            gram = lax.dot_general(
                block[slot],
                block[slot],
                (((contract,), (contract,)), ((), ())),
                preferred_element_type=F32,
            )
            used = held(rank * slots + slot) > 0
            out[slot] = 0.95 * stat[slot] + 0.05 * jnp.where(used, gram, 0.0)

    arrived(all_sums.at[pl.ds(0, ranks - 1)], sums_recv)
    for index in range(per_group):
        at = place_of(index)
        row = all_sums[at // slots, pl.ds(0, 1)]
        sizes[index : index + 1] = jnp.where(lane[:1] == 2 + at % slots, row, 0.0)
    total = jnp.sum(all_sums[...], axis=0)
    adam_sq = jnp.concatenate([total[:, 0:1], total[:, 1:2]], axis=0)
    direction_sq = jnp.sum(sizes[...], axis=1, keepdims=True)
    graft[...] = jnp.broadcast_to(jnp.sqrt(adam_sq / (direction_sq + 1e-06)), graft.shape)
    for slot in range(slots):
        arrived(returned.at[pl.ds(0, ranks - 1), slot], back_recv.at[slot])

    for k in chunks:
        for copy in ring_copies[k]:
            copy.wait_send()
    for copy in core_copies:
        copy.wait_send()
    for k in chunks:
        arrived(outgoing[k].at[pl.ds(0, ranks - 1)], owner_send.at[k])
    for slot in range(slots):
        arrived(direction.at[slot, pl.ds(0, (ranks - 1) * strip)], back_send.at[slot])
        arrived(relayed.at[slot], relay_send.at[slot])
    arrived(all_sums.at[pl.ds(0, ranks - 1)], sums_send)


def exchange(block_owner, gradients, root_left, root_right, first, second, left, right, ranks):
    lines, _, per_group, strip, columns = gradients.shape
    slots, rows, _ = root_left.shape
    height = strip // 2
    widths = [tiles * 128 for _, _, tiles in PARTS]
    half = per_group // 2
    far = pl.BlockSpec(memory_space=pltpu.HBM)
    dma = pltpu.SemaphoreType.DMA
    vmem = pltpu.VMEM
    return pl.pallas_call(
        exchange_kernel,
        out_shape=(
            pltpu.VMEM((ranks, slots, strip, columns), BF16),
            pltpu.VMEM((per_group, 128), F32),
            pltpu.VMEM((8, 128), I32),
            pltpu.VMEM(first.shape, F32),
            pltpu.VMEM(first.shape, F32),
            pltpu.VMEM(left.shape, F32),
            pltpu.VMEM(right.shape, F32),
        ),
        in_specs=[far] * 8,
        out_specs=(pl.BlockSpec(memory_space=pltpu.VMEM),) * 7,
        scratch_shapes=[
            vmem(block_owner.shape, I32),
            pltpu.SMEM((8, 128), I32),
            vmem((lines, per_group, strip, columns), BF16),
            vmem((lines, per_group, strip, columns), BF16),
            vmem((lines, per_group, strip, columns), BF16),
            [vmem((lines, per_group, height, wide), BF16) for wide in widths],
            [vmem((half, height, wide), BF16) for wide in widths],
            [vmem((half, height, wide), BF16) for wide in widths],
            [vmem((per_group, height, wide), BF16) for wide in widths],
            [vmem((per_group, height, wide), BF16) for wide in widths],
            [vmem((per_group, height, wide), BF16) for wide in widths],
            [vmem((ranks, slots, height, wide), BF16) for wide in widths],
            vmem((slots, rows, columns), BF16),
            vmem((slots, rows, columns), BF16),
            vmem((slots, rows, columns), BF16),
            vmem(first.shape, F32),
            vmem(first.shape, F32),
            vmem(left.shape, F32),
            vmem(right.shape, F32),
            vmem((slots, rows, columns), BF16),
            vmem((slots, len(LEGS), strip, columns), BF16),
            vmem((8, 128), F32),
            vmem((ranks, 8, 128), F32),
            vmem((per_group, 128), F32),
            vmem((CHUNKS, per_group, 8, 128), F32),
            dma((2,)),
            dma((2, 4)),
            dma((6,)),
            dma((4,)),
            dma((4,)),
            dma((CHUNKS, 6)),
            dma((CHUNKS, 6)),
            dma((CHUNKS,)),
            dma((CHUNKS,)),
            dma((slots,)),
            dma((slots,)),
            dma((slots,)),
            dma((slots, len(LEGS))),
            dma,
            dma,
        ],
        compiler_params=pltpu.CompilerParams(
            collective_id=0, has_side_effects=True, vmem_limit_bytes=40 * 2**20
        ),
        cost_estimate=pl.CostEstimate(
            flops=8 * slots * rows * rows * columns, bytes_accessed=18 * 2**20, transcendentals=0
        ),
        name="exchange",
    )(
        *(
            pltpu.with_memory_space_constraint(value, pltpu.HBM)
            for value in (
                block_owner,
                gradients,
                root_left,
                root_right,
                first,
                second,
                left,
                right,
            )
        )
    )


def publish_kernel(
    returned,
    graft,
    places,
    first,
    second,
    left,
    right,
    update_out,
    first_out,
    second_out,
    left_out,
    right_out,
    place,
    update,
    sems,
):
    per_group, strip, columns = update.shape
    ranks, slots = returned.shape[:2]
    place_copy = pltpu.make_async_copy(places, place, sems.at[5])
    place_copy.start()
    pairs = ((left, left_out), (right, right_out), (first, first_out), (second, second_out))
    copies = [
        pltpu.make_async_copy(src, out, sems.at[index]) for index, (src, out) in enumerate(pairs)
    ]
    for copy in copies:
        copy.start()
    place_copy.wait()
    dp = lax.axis_index("dp")

    @pl.loop(0, per_group)
    def _(index):
        at = jnp.clip(place[0, dp * per_group + index], 0, ranks * slots - 1)
        scale = -graft[pl.ds(index, 1)]
        value = returned[at // slots, at % slots].astype(F32)
        update[index] = (value * jnp.concatenate([scale] * (columns // 128), axis=1)).astype(BF16)

    copies.append(pltpu.make_async_copy(update, update_out, sems.at[4]))
    copies[-1].start()
    for copy in copies:
        copy.wait()


def publish(results):
    returned, graft, places, first, second, left, right = results
    anywhere = pl.BlockSpec(memory_space=pl.ANY)
    near = pl.BlockSpec(memory_space=pltpu.VMEM)
    shapes = [(first.shape, BF16)] + [(value.shape, F32) for value in results[3:]]
    return pl.pallas_call(
        publish_kernel,
        out_shape=[jax.ShapeDtypeStruct(*shape) for shape in shapes],
        in_specs=[near, near] + [anywhere] * 5,
        out_specs=[pl.BlockSpec(memory_space=pltpu.HBM)] * 5,
        scratch_shapes=[
            pltpu.SMEM((8, 128), I32),
            pltpu.VMEM(first.shape, BF16),
            pltpu.SemaphoreType.DMA((6,)),
        ],
        compiler_params=pltpu.CompilerParams(vmem_limit_bytes=4 * 2**20),
        name="publish",
    )(*(pltpu.with_memory_space_constraint(value, pltpu.VMEM) for value in results))


def shards(
    gradients,
    block_owner,
    left_stat,
    right_stat,
    root_left,
    root_right,
    moment_first,
    moment_second,
):
    dp_count = lax.axis_size("dp")
    ranks = lax.axis_size("fsdp")
    count = block_owner.shape[0]
    strip, columns = gradients.shape[2:]
    results = exchange(
        block_owner.reshape(1, count),
        gradients.reshape(dp_count // 2, 2, count // dp_count, strip, columns),
        root_left,
        root_right,
        moment_first,
        moment_second,
        left_stat,
        right_stat,
        ranks,
    )
    return tuple(publish(results))


def solution(mesh):
    placed = (
        P("dp", None, "fsdp", None),
        P(),
        P(("dp", "fsdp"), None, None),
        P(("dp", "fsdp"), None, None),
        P(("dp", "fsdp"), None, None),
        P(("dp", "fsdp"), None, None),
        P("dp", "fsdp", None),
        P("dp", "fsdp", None),
    )
    return jax.shard_map(
        shards,
        mesh=mesh,
        in_specs=placed,
        out_specs=(
            P("dp", "fsdp", None),
            P("dp", "fsdp", None),
            P("dp", "fsdp", None),
            P(("dp", "fsdp"), None, None),
            P(("dp", "fsdp"), None, None),
        ),
        check_vma=False,
    )
```

```python
import functools

import jax
import jax.numpy as jnp
from jax import lax
from jax.experimental import pallas as pl
from jax.experimental.pallas import tpu as pltpu
from jax.sharding import PartitionSpec as P

F32 = jnp.float32
BF16 = jnp.bfloat16
I32 = jnp.int32
PARTS = ((0, 0, 1), (0, 1, 1), (0, 2, 2), (1, 0, 2), (1, 2, 1), (1, 3, 1))
CHUNKS = len(PARTS)
SIDE = 4
OFFSETS = (
    *((2, 2), (2, 1), (2, -1), (1, 2), (-1, 2), (2, 0), (0, 2)),
    *((1, 1), (-1, -1), (1, -1), (-1, 1), (1, 0), (-1, 0), (0, 1), (0, -1)),
)


def exchange_kernel(
    owner_ref,
    grad_ref,
    root_left_ref,
    root_right_ref,
    first_ref,
    second_ref,
    left_ref,
    right_ref,
    returned,
    graft,
    places,
    first_out,
    second_out,
    left_out,
    right_out,
    owner,
    place,
    own,
    lend,
    other,
    pair,
    relay_right,
    relay_left,
    from_left,
    from_right,
    reduced,
    outgoing,
    block,
    root_left,
    root_right,
    first,
    second,
    stat_left,
    stat_right,
    direction,
    sums,
    all_sums,
    sizes,
    adam_sums,
    place_sem,
    own_sem,
    load_sem,
    core_send,
    core_recv,
    ring_send,
    ring_recv,
    owner_send,
    owner_recv,
    back_send,
    back_recv,
    sums_send,
    sums_recv,
):
    lines, _, per_group, strip, columns = grad_ref.shape
    height = strip // 2
    half = per_group // 2
    slots, rows = block.shape[:2]
    ranks = rows // strip
    count = owner.shape[1]
    dp = lax.axis_index("dp")
    rank = lax.axis_index("fsdp")
    x = dp // 2
    core = dp % 2
    y = rank % SIDE
    z = rank // SIDE
    mate = x * 2 + (1 - core)
    sign = 1 - 2 * core
    ahead = (x + lines + sign) % lines
    behind = (x + lines - sign) % lines
    across = (x + 2) % lines
    right = ahead * 2 + core
    left = behind * 2 + core
    chunks = range(CHUNKS)

    def upper(k):
        return pl.ds(PARTS[k][0] * height, height)

    def cols(k):
        return pl.ds(PARTS[k][1] * 128, PARTS[k][2] * 128)

    def strip_rows(at):
        return pl.ds(pl.multiple_of(at * strip, strip), strip)

    def at_offset(dy, dz):
        target_y = (y + SIDE + sign * dy) % SIDE
        target_z = (z + SIDE + sign * dz) % SIDE
        return target_z * SIDE + target_y

    def each_target(visit):
        @pl.loop(0, SIDE)
        def _(turn):
            for index, (dy, shift) in enumerate(((1, 0), (3, 2), (2, 3), (0, 1))):
                dz = (turn + shift) % SIDE
                target = at_offset(dy, dz)
                if index < 3:
                    visit(target)
                else:
                    pl.when(turn < SIDE - 1)(functools.partial(visit, target))

    owner_load = pltpu.make_async_copy(owner_ref, owner, place_sem.at[0])
    owner_load.start()
    order = (across, ahead, behind, x)
    lend_loads, own_loads = [], []
    for index, line in enumerate(order):
        lend_loads.append(
            pltpu.make_async_copy(grad_ref.at[line, 1 - core], lend.at[line], own_sem.at[0, index])
        )
        own_loads.append(
            pltpu.make_async_copy(grad_ref.at[line, core], own.at[line], own_sem.at[1, index])
        )
    for load in lend_loads + own_loads:
        load.start()
    loads = [
        pltpu.make_async_copy(src, dst, load_sem.at[index])
        for index, (src, dst) in enumerate(
            (
                (root_left_ref, root_left),
                (root_right_ref, root_right),
                (first_ref, first),
                (second_ref, second),
                (left_ref, stat_left),
                (right_ref, stat_right),
            )
        )
    ]
    barrier = pltpu.get_barrier_semaphore()
    for partner in (mate, right, left):
        pl.semaphore_signal(barrier, inc=1, device_id={"dp": partner})

    @pl.loop(1, ranks)
    def _(step):
        pl.semaphore_signal(barrier, inc=1, device_id={"fsdp": (rank + step) % ranks})

    owner_load.wait()
    along = lax.broadcasted_iota(I32, (count, count), 1)
    down = lax.broadcasted_iota(I32, (count, count), 0)
    owner_row = owner[...]
    owner_all = jnp.broadcast_to(owner_row, (count, count)).astype(F32)
    owner_col = jnp.sum(jnp.where(along == down, owner_all, 0.0), axis=1, keepdims=True)
    same = owner_all == owner_col
    slot_row = jnp.sum(jnp.where(same & (down < along), 1.0, 0.0), axis=0, keepdims=True)
    slot_col = jnp.sum(jnp.where(same & (along < down), 1.0, 0.0), axis=1, keepdims=True)
    offset = (dp * (ranks * slots)).astype(F32)
    place_row = owner_row.astype(F32) * slots + slot_row - offset
    place_col = owner_col * slots + slot_col - offset
    number = (down - dp * per_group + 1).astype(F32)
    held_row = jnp.sum(
        jnp.where(along.astype(F32) == place_col, number, 0.0), axis=0, keepdims=True
    )
    places[...] = jnp.concatenate(
        [place_row, held_row, jnp.zeros((6, count), F32)], axis=0
    ).astype(I32)
    place_copy = pltpu.make_async_copy(places, place, place_sem.at[1])
    place_copy.start()

    pl.semaphore_wait(barrier, ranks + 2)

    core_copies = []
    everything, top, bottom = pl.ds(0, strip), pl.ds(0, height), pl.ds(height, height)
    pieces = ((0, top), (0, bottom), (1, everything), (2, everything), (3, everything))
    for at, (index, there) in enumerate(pieces):
        if at != 1:
            lend_loads[index].wait()
        copy = pltpu.make_async_remote_copy(
            src_ref=lend.at[order[index], :, there],
            dst_ref=other.at[order[index], :, there],
            send_sem=core_send.at[at],
            recv_sem=core_recv.at[lines if at == 1 else order[index]],
            device_id={"dp": mate},
        )
        copy.start()
        core_copies.append(copy)
    place_copy.wait()

    def held(at):
        return place[1, at]

    def block_of(at):
        return jnp.clip(held(at) - 1, 0, per_group - 1)

    def place_of(index):
        return jnp.clip(place[0, dp * per_group + index], 0, ranks * slots - 1)

    def ready(k, index):
        if k == 0:
            own_loads[index].wait()
        if PARTS[k][1] == 0 and (k == 0 or index == 0):
            at = index + 1 if index else PARTS[k][0]
            ref = other.at[order[index], :, pieces[at][1]]
            sem = core_recv.at[lines if at == 1 else order[index]]
            pltpu.make_async_copy(ref, ref, sem).wait()

    def both(k, index):
        line = order[index]
        return own[line, :, upper(k), cols(k)], other[line, :, upper(k), cols(k)]

    def pair_sum(k, index):
        ready(k, index)
        mine, its = both(k, index)
        pair[k][order[index]] = mine + its

    def ring(k, index, src, dst, target):
        return pltpu.make_async_remote_copy(
            src_ref=src,
            dst_ref=dst,
            send_sem=ring_send.at[k, index],
            recv_sem=ring_recv.at[k, index],
            device_id={"dp": target},
        )

    ring_copies = [None] * CHUNKS
    low, high = pl.ds(0, half), pl.ds(half, half)

    def far_sums(k):
        copies = [
            ring(k, 0, pair[k].at[across, low], relay_right[k], right),
            ring(k, 1, pair[k].at[across, high], relay_left[k], left),
            ring(k, 2, pair[k].at[ahead, high], from_left[k].at[high], right),
            ring(k, 3, pair[k].at[behind, low], from_right[k].at[low], left),
            ring(k, 4, pair[k].at[ahead, low], from_left[k].at[low], right),
            ring(k, 5, pair[k].at[behind, high], from_right[k].at[high], left),
        ]
        ring_copies[k] = copies
        pair_sum(k, 0)
        copies[0].start()
        copies[1].start()

    def near_sums(k):
        copies = ring_copies[k]
        pair_sum(k, 1)
        copies[2].start()
        pair_sum(k, 2)
        copies[3].start()

    def relay(k):
        copies = ring_copies[k]
        copies[0].wait_recv()
        pair[k][ahead, low] = pair[k][ahead, low] + relay_right[k][...]
        copies[4].start()
        copies[1].wait_recv()
        pair[k][behind, high] = pair[k][behind, high] + relay_left[k][...]
        copies[5].start()
    def finish(k):
        ready(k, 3)
        mine, its = both(k, 3)
        total = mine.astype(F32) + its.astype(F32)
        for copy in ring_copies[k][2:]:
            copy.wait_recv()
        total = total + from_left[k][...].astype(F32) + from_right[k][...].astype(F32)
        reduced[k][...] = total.astype(BF16)

    def strip_part(k):
        return pl.ds(pl.multiple_of(rank * strip + PARTS[k][0] * height, height), height)

    def to_owners(k):
        def visit(target):
            for slot in range(slots):
                outgoing[k][target, slot] = reduced[k][block_of(target * slots + slot)]
            pltpu.make_async_remote_copy(
                src_ref=outgoing[k].at[target],
                dst_ref=block.at[:, strip_part(k), cols(k)],
                send_sem=owner_send.at[k],
                recv_sem=owner_recv.at[k],
                device_id={"fsdp": target},
            ).start()

        each_target(visit)
        for slot in range(slots):
            block[slot, strip_part(k), cols(k)] = reduced[k][block_of(rank * slots + slot)]

    def moments(k):
        step = 4

        @pl.loop(0, per_group // step)
        def _(turn):
            here = pl.ds(turn * step, step)
            grad = reduced[k][here].astype(F32)
            first_new = 0.9 * first[here, upper(k), cols(k)] + 0.1 * grad
            second_new = 0.95 * second[here, upper(k), cols(k)] + 0.05 * grad * grad
            first_out[here, upper(k), cols(k)] = first_new
            second_out[here, upper(k), cols(k)] = second_new
            adam = first_new / (jnp.sqrt(second_new) + 1e-08)
            adam = jnp.sum((adam * adam).reshape(step, height // 8, 8, -1), axis=1)
            adam_sums[k, here] = functools.reduce(
                jnp.add, [adam[:, :, at * 128 : at * 128 + 128] for at in range(PARTS[k][2])]
            )

    far_sums(0)
    near_sums(0)
    far_sums(1)
    relay(0)
    for load in loads:
        load.start()
    for k in chunks:
        if k + 1 < CHUNKS:
            near_sums(k + 1)
        if k + 2 < CHUNKS:
            far_sums(k + 2)
        if k + 1 < CHUNKS:
            relay(k + 1)
        if k == 1:
            loads[2].wait()
            loads[3].wait()
        if 1 <= k < CHUNKS - 2:
            moments(k - 1)
        finish(k)
        to_owners(k)
    for k in range(CHUNKS - 3, CHUNKS):
        moments(k)

    def arrived(ref, sem):
        pltpu.make_async_copy(ref, ref, sem).wait()

    for k in chunks:
        arrived(outgoing[k].at[pl.ds(0, ranks - 1)], owner_recv.at[k])
    loads[0].wait()
    loads[1].wait()

    def precondition(slot):
        product = jnp.dot(root_left[slot], block[slot], preferred_element_type=F32)
        direction[slot] = jnp.dot(
            product.astype(BF16), root_right[slot], preferred_element_type=F32
        ).astype(BF16)

    def send_back(slot):
        for offset in OFFSETS:
            target = at_offset(*offset)
            pltpu.make_async_remote_copy(
                src_ref=direction.at[slot, strip_rows(target)],
                dst_ref=returned.at[rank, slot],
                send_sem=back_send.at[slot],
                recv_sem=back_recv.at[slot],
                device_id={"fsdp": target},
            ).start()
        returned[rank, slot] = direction[slot, strip_rows(rank)]

    def squares(slot):
        wide = direction[slot].astype(F32)
        wide = jnp.sum(jnp.sum((wide * wide).reshape(-1, 8, columns), axis=0), axis=0, keepdims=True)
        return jnp.sum(wide, axis=1, keepdims=True)

    def send_sums(target):
        pltpu.make_async_remote_copy(
            src_ref=sums,
            dst_ref=all_sums.at[rank],
            send_sem=sums_send,
            recv_sem=sums_recv,
            device_id={"fsdp": target},
        ).start()

    adam = jnp.sum(jnp.sum(jnp.sum(adam_sums[...], axis=0), axis=1), axis=1, keepdims=True)
    lane = lax.broadcasted_iota(I32, (8, 128), 1)
    precondition(0)
    send_back(0)
    precondition(1)
    tile = jnp.where(lane == 0, adam[:8], 0.0) + jnp.where(lane == 1, adam[8:], 0.0)
    for slot in range(slots):
        tile = tile + jnp.where(lane == 2 + slot, squares(slot), 0.0)
    sums[...] = tile
    all_sums[rank] = tile
    each_target(send_sums)
    send_back(1)

    loads[4].wait()
    loads[5].wait()
    for stat, contract, out in ((stat_left, 1, left_out), (stat_right, 0, right_out)):
        for slot in range(slots):
            gram = lax.dot_general(
                block[slot],
                block[slot],
                (((contract,), (contract,)), ((), ())),
                preferred_element_type=F32,
            )
            used = held(rank * slots + slot) > 0
            out[slot] = 0.95 * stat[slot] + 0.05 * jnp.where(used, gram, 0.0)

    arrived(all_sums.at[pl.ds(0, ranks - 1)], sums_recv)
    for index in range(per_group):
        at = place_of(index)
        row = all_sums[at // slots, pl.ds(0, 1)]
        sizes[index : index + 1] = jnp.where(lane[:1] == 2 + at % slots, row, 0.0)
    total = jnp.sum(all_sums[...], axis=0)
    adam_sq = jnp.concatenate([total[:, 0:1], total[:, 1:2]], axis=0)
    direction_sq = jnp.sum(sizes[...], axis=1, keepdims=True)
    graft[...] = jnp.broadcast_to(jnp.sqrt(adam_sq / (direction_sq + 1e-06)), graft.shape)
    for slot in range(slots):
        arrived(returned.at[pl.ds(0, ranks - 1), slot], back_recv.at[slot])

    for k in chunks:
        for copy in ring_copies[k]:
            copy.wait_send()
    for copy in core_copies:
        copy.wait_send()
    for k in chunks:
        arrived(outgoing[k].at[pl.ds(0, ranks - 1)], owner_send.at[k])
    for slot in range(slots):
        arrived(direction.at[slot, pl.ds(0, (ranks - 1) * strip)], back_send.at[slot])
    arrived(all_sums.at[pl.ds(0, ranks - 1)], sums_send)


def exchange(block_owner, gradients, root_left, root_right, first, second, left, right, ranks):
    lines, _, per_group, strip, columns = gradients.shape
    slots, rows, _ = root_left.shape
    height = strip // 2
    widths = [tiles * 128 for _, _, tiles in PARTS]
    half = per_group // 2
    far = pl.BlockSpec(memory_space=pltpu.HBM)
    dma = pltpu.SemaphoreType.DMA
    vmem = pltpu.VMEM
    return pl.pallas_call(
        exchange_kernel,
        out_shape=(
            pltpu.VMEM((ranks, slots, strip, columns), BF16),
            pltpu.VMEM((per_group, 128), F32),
            pltpu.VMEM((8, 128), I32),
            pltpu.VMEM(first.shape, F32),
            pltpu.VMEM(first.shape, F32),
            pltpu.VMEM(left.shape, F32),
            pltpu.VMEM(right.shape, F32),
        ),
        in_specs=[far] * 8,
        out_specs=(pl.BlockSpec(memory_space=pltpu.VMEM),) * 7,
        scratch_shapes=[
            vmem(block_owner.shape, I32),
            pltpu.SMEM((8, 128), I32),
            vmem((lines, per_group, strip, columns), BF16),
            vmem((lines, per_group, strip, columns), BF16),
            vmem((lines, per_group, strip, columns), BF16),
            [vmem((lines, per_group, height, wide), BF16) for wide in widths],
            [vmem((half, height, wide), BF16) for wide in widths],
            [vmem((half, height, wide), BF16) for wide in widths],
            [vmem((per_group, height, wide), BF16) for wide in widths],
            [vmem((per_group, height, wide), BF16) for wide in widths],
            [vmem((per_group, height, wide), BF16) for wide in widths],
            [vmem((ranks, slots, height, wide), BF16) for wide in widths],
            vmem((slots, rows, columns), BF16),
            vmem((slots, rows, columns), BF16),
            vmem((slots, rows, columns), BF16),
            vmem(first.shape, F32),
            vmem(first.shape, F32),
            vmem(left.shape, F32),
            vmem(right.shape, F32),
            vmem((slots, rows, columns), BF16),
            vmem((8, 128), F32),
            vmem((ranks, 8, 128), F32),
            vmem((per_group, 128), F32),
            vmem((CHUNKS, per_group, 8, 128), F32),
            dma((2,)),
            dma((2, 4)),
            dma((6,)),
            dma((5,)),
            dma((5,)),
            dma((CHUNKS, 6)),
            dma((CHUNKS, 6)),
            dma((CHUNKS,)),
            dma((CHUNKS,)),
            dma((slots,)),
            dma((slots,)),
            dma,
            dma,
        ],
        compiler_params=pltpu.CompilerParams(
            collective_id=0, has_side_effects=True, vmem_limit_bytes=40 * 2**20
        ),
        cost_estimate=pl.CostEstimate(
            flops=8 * slots * rows * rows * columns, bytes_accessed=18 * 2**20, transcendentals=0
        ),
        name="exchange",
    )(
        *(
            pltpu.with_memory_space_constraint(value, pltpu.HBM)
            for value in (
                block_owner,
                gradients,
                root_left,
                root_right,
                first,
                second,
                left,
                right,
            )
        )
    )


def publish_kernel(
    returned,
    graft,
    places,
    first,
    second,
    left,
    right,
    update_out,
    first_out,
    second_out,
    left_out,
    right_out,
    place,
    update,
    sems,
):
    per_group, strip, columns = update.shape
    ranks, slots = returned.shape[:2]
    place_copy = pltpu.make_async_copy(places, place, sems.at[5])
    place_copy.start()
    pairs = ((left, left_out), (right, right_out), (first, first_out), (second, second_out))
    copies = [
        pltpu.make_async_copy(src, out, sems.at[index]) for index, (src, out) in enumerate(pairs)
    ]
    for copy in copies:
        copy.start()
    place_copy.wait()
    dp = lax.axis_index("dp")

    @pl.loop(0, per_group)
    def _(index):
        at = jnp.clip(place[0, dp * per_group + index], 0, ranks * slots - 1)
        scale = -graft[pl.ds(index, 1)]
        value = returned[at // slots, at % slots].astype(F32)
        update[index] = (value * jnp.concatenate([scale] * (columns // 128), axis=1)).astype(BF16)

    copies.append(pltpu.make_async_copy(update, update_out, sems.at[4]))
    copies[-1].start()
    for copy in copies:
        copy.wait()


def publish(results):
    returned, graft, places, first, second, left, right = results
    anywhere = pl.BlockSpec(memory_space=pl.ANY)
    near = pl.BlockSpec(memory_space=pltpu.VMEM)
    shapes = [(first.shape, BF16)] + [(value.shape, F32) for value in results[3:]]
    return pl.pallas_call(
        publish_kernel,
        out_shape=[jax.ShapeDtypeStruct(*shape) for shape in shapes],
        in_specs=[near, near] + [anywhere] * 5,
        out_specs=[pl.BlockSpec(memory_space=pltpu.HBM)] * 5,
        scratch_shapes=[
            pltpu.SMEM((8, 128), I32),
            pltpu.VMEM(first.shape, BF16),
            pltpu.SemaphoreType.DMA((6,)),
        ],
        compiler_params=pltpu.CompilerParams(vmem_limit_bytes=4 * 2**20),
        name="publish",
    )(*(pltpu.with_memory_space_constraint(value, pltpu.VMEM) for value in results))


def shards(
    gradients,
    block_owner,
    left_stat,
    right_stat,
    root_left,
    root_right,
    moment_first,
    moment_second,
):
    dp_count = lax.axis_size("dp")
    ranks = lax.axis_size("fsdp")
    count = block_owner.shape[0]
    strip, columns = gradients.shape[2:]
    results = exchange(
        block_owner.reshape(1, count),
        gradients.reshape(dp_count // 2, 2, count // dp_count, strip, columns),
        root_left,
        root_right,
        moment_first,
        moment_second,
        left_stat,
        right_stat,
        ranks,
    )
    return tuple(publish(results))


def solution(mesh):
    placed = (
        P("dp", None, "fsdp", None),
        P(),
        P(("dp", "fsdp"), None, None),
        P(("dp", "fsdp"), None, None),
        P(("dp", "fsdp"), None, None),
        P(("dp", "fsdp"), None, None),
        P("dp", "fsdp", None),
        P("dp", "fsdp", None),
    )
    return jax.shard_map(
        shards,
        mesh=mesh,
        in_specs=placed,
        out_specs=(
            P("dp", "fsdp", None),
            P("dp", "fsdp", None),
            P("dp", "fsdp", None),
            P(("dp", "fsdp"), None, None),
            P(("dp", "fsdp"), None, None),
        ),
        check_vma=False,
    )
```

```python
import functools

import jax
import jax.numpy as jnp
from jax import lax
from jax.experimental import pallas as pl
from jax.experimental.pallas import tpu as pltpu
from jax.sharding import PartitionSpec as P

F32 = jnp.float32
BF16 = jnp.bfloat16
I32 = jnp.int32
PARTS = ((0, 0, 1), (0, 1, 1), (1, 0, 2), (0, 2, 2), (1, 2, 1), (1, 3, 1))
CHUNKS = len(PARTS)
EARLY = 3
SIDE = 4
OFFSETS = (
    *((2, 2), (2, 1), (2, -1), (1, 2), (-1, 2), (2, 0), (0, 2)),
    *((1, 1), (-1, -1), (1, -1), (-1, 1), (1, 0), (-1, 0), (0, 1), (0, -1)),
)


def exchange_kernel(
    owner_ref,
    grad_ref,
    root_left_ref,
    root_right_ref,
    first_ref,
    second_ref,
    left_ref,
    right_ref,
    returned,
    graft,
    places,
    first_out,
    second_out,
    left_out,
    right_out,
    owner,
    place,
    own,
    lend,
    other,
    pair,
    relay_right,
    relay_left,
    from_left,
    from_right,
    reduced,
    outgoing,
    block,
    root_left,
    root_right,
    first,
    second,
    stat_left,
    stat_right,
    partial,
    direction,
    sums,
    all_sums,
    sizes,
    adam_sums,
    place_sem,
    own_sem,
    load_sem,
    core_send,
    core_recv,
    ring_send,
    ring_recv,
    owner_send,
    owner_recv,
    back_send,
    back_recv,
    sums_send,
    sums_recv,
):
    lines, _, per_group, strip, columns = grad_ref.shape
    height = strip // 2
    half = per_group // 2
    slots, rows = block.shape[:2]
    ranks = rows // strip
    count = owner.shape[1]
    dp = lax.axis_index("dp")
    rank = lax.axis_index("fsdp")
    x = dp // 2
    core = dp % 2
    y = rank % SIDE
    z = rank // SIDE
    mate = x * 2 + (1 - core)
    sign = 1 - 2 * core
    ahead = (x + lines + sign) % lines
    behind = (x + lines - sign) % lines
    across = (x + 2) % lines
    right = ahead * 2 + core
    left = behind * 2 + core
    chunks = range(CHUNKS)

    def upper(k):
        return pl.ds(PARTS[k][0] * height, height)

    def cols(k):
        return pl.ds(PARTS[k][1] * 128, PARTS[k][2] * 128)

    def strip_rows(at):
        return pl.ds(pl.multiple_of(at * strip, strip), strip)

    def at_offset(dy, dz):
        target_y = (y + SIDE + sign * dy) % SIDE
        target_z = (z + SIDE + sign * dz) % SIDE
        return target_z * SIDE + target_y

    def each_target(visit):
        @pl.loop(0, SIDE)
        def _(turn):
            for index, (dy, shift) in enumerate(((1, 0), (3, 2), (2, 3), (0, 1))):
                dz = (turn + shift) % SIDE
                target = at_offset(dy, dz)
                if index < 3:
                    visit(target)
                else:
                    pl.when(turn < SIDE - 1)(functools.partial(visit, target))

    owner_load = pltpu.make_async_copy(owner_ref, owner, place_sem.at[0])
    owner_load.start()
    order = (across, ahead, behind, x)
    lend_loads, own_loads = [], []
    for index, line in enumerate(order):
        lend_loads.append(
            pltpu.make_async_copy(grad_ref.at[line, 1 - core], lend.at[line], own_sem.at[0, index])
        )
        own_loads.append(
            pltpu.make_async_copy(grad_ref.at[line, core], own.at[line], own_sem.at[1, index])
        )
    for load in lend_loads + own_loads:
        load.start()
    loads = [
        pltpu.make_async_copy(src, dst, load_sem.at[index])
        for index, (src, dst) in enumerate(
            (
                (root_left_ref, root_left),
                (root_right_ref, root_right),
                (first_ref, first),
                (second_ref, second),
                (left_ref, stat_left),
                (right_ref, stat_right),
            )
        )
    ]
    barrier = pltpu.get_barrier_semaphore()
    for partner in (mate, right, left):
        pl.semaphore_signal(barrier, inc=1, device_id={"dp": partner})

    @pl.loop(1, ranks)
    def _(step):
        pl.semaphore_signal(barrier, inc=1, device_id={"fsdp": (rank + step) % ranks})

    owner_load.wait()
    along = lax.broadcasted_iota(I32, (count, count), 1)
    down = lax.broadcasted_iota(I32, (count, count), 0)
    owner_row = owner[...]
    owner_all = jnp.broadcast_to(owner_row, (count, count)).astype(F32)
    owner_col = jnp.sum(jnp.where(along == down, owner_all, 0.0), axis=1, keepdims=True)
    same = owner_all == owner_col
    slot_row = jnp.sum(jnp.where(same & (down < along), 1.0, 0.0), axis=0, keepdims=True)
    slot_col = jnp.sum(jnp.where(same & (along < down), 1.0, 0.0), axis=1, keepdims=True)
    offset = (dp * (ranks * slots)).astype(F32)
    place_row = owner_row.astype(F32) * slots + slot_row - offset
    place_col = owner_col * slots + slot_col - offset
    number = (down - dp * per_group + 1).astype(F32)
    held_row = jnp.sum(
        jnp.where(along.astype(F32) == place_col, number, 0.0), axis=0, keepdims=True
    )
    places[...] = jnp.concatenate(
        [place_row, held_row, jnp.zeros((6, count), F32)], axis=0
    ).astype(I32)
    place_copy = pltpu.make_async_copy(places, place, place_sem.at[1])
    place_copy.start()

    pl.semaphore_wait(barrier, ranks + 2)

    core_copies = []
    everything, top, bottom = pl.ds(0, strip), pl.ds(0, height), pl.ds(height, height)
    pieces = ((0, top), (0, bottom), (1, everything), (2, everything), (3, everything))
    for at, (index, there) in enumerate(pieces):
        if at != 1:
            lend_loads[index].wait()
        copy = pltpu.make_async_remote_copy(
            src_ref=lend.at[order[index], :, there],
            dst_ref=other.at[order[index], :, there],
            send_sem=core_send.at[at],
            recv_sem=core_recv.at[lines if at == 1 else order[index]],
            device_id={"dp": mate},
        )
        copy.start()
        core_copies.append(copy)
    place_copy.wait()

    def held(at):
        return place[1, at]

    def block_of(at):
        return jnp.clip(held(at) - 1, 0, per_group - 1)

    def place_of(index):
        return jnp.clip(place[0, dp * per_group + index], 0, ranks * slots - 1)

    def ready(k, index):
        if k == 0:
            own_loads[index].wait()
        if PARTS[k][1] == 0 and (k == 0 or index == 0):
            at = index + 1 if index else PARTS[k][0]
            ref = other.at[order[index], :, pieces[at][1]]
            sem = core_recv.at[lines if at == 1 else order[index]]
            pltpu.make_async_copy(ref, ref, sem).wait()

    def both(k, index):
        line = order[index]
        return own[line, :, upper(k), cols(k)], other[line, :, upper(k), cols(k)]

    def pair_sum(k, index):
        ready(k, index)
        mine, its = both(k, index)
        pair[k][order[index]] = mine + its

    def ring(k, index, src, dst, target):
        return pltpu.make_async_remote_copy(
            src_ref=src,
            dst_ref=dst,
            send_sem=ring_send.at[k, index],
            recv_sem=ring_recv.at[k, index],
            device_id={"dp": target},
        )

    ring_copies = [None] * CHUNKS
    low, high = pl.ds(0, half), pl.ds(half, half)

    def far_sums(k):
        copies = [
            ring(k, 0, pair[k].at[across, low], relay_right[k], right),
            ring(k, 1, pair[k].at[across, high], relay_left[k], left),
            ring(k, 2, pair[k].at[ahead, high], from_left[k].at[high], right),
            ring(k, 3, pair[k].at[behind, low], from_right[k].at[low], left),
            ring(k, 4, pair[k].at[ahead, low], from_left[k].at[low], right),
            ring(k, 5, pair[k].at[behind, high], from_right[k].at[high], left),
        ]
        ring_copies[k] = copies
        pair_sum(k, 0)
        copies[0].start()
        copies[1].start()

    def near_sums(k):
        copies = ring_copies[k]
        pair_sum(k, 1)
        copies[2].start()
        pair_sum(k, 2)
        copies[3].start()

    def relay(k):
        copies = ring_copies[k]
        copies[0].wait_recv()
        pair[k][ahead, low] = pair[k][ahead, low] + relay_right[k][...]
        copies[4].start()
        copies[1].wait_recv()
        pair[k][behind, high] = pair[k][behind, high] + relay_left[k][...]
        copies[5].start()
    def finish(k):
        ready(k, 3)
        mine, its = both(k, 3)
        total = mine.astype(F32) + its.astype(F32)
        for copy in ring_copies[k][2:]:
            copy.wait_recv()
        total = total + from_left[k][...].astype(F32) + from_right[k][...].astype(F32)
        reduced[k][...] = total.astype(BF16)

    def strip_part(k):
        return pl.ds(pl.multiple_of(rank * strip + PARTS[k][0] * height, height), height)

    def to_owners(k):
        def visit(target):
            for slot in range(slots):
                outgoing[k][target, slot] = reduced[k][block_of(target * slots + slot)]
            pltpu.make_async_remote_copy(
                src_ref=outgoing[k].at[target],
                dst_ref=block.at[:, strip_part(k), cols(k)],
                send_sem=owner_send.at[k],
                recv_sem=owner_recv.at[k],
                device_id={"fsdp": target},
            ).start()

        each_target(visit)
        for slot in range(slots):
            block[slot, strip_part(k), cols(k)] = reduced[k][block_of(rank * slots + slot)]

    def moments(k):
        step = 4

        @pl.loop(0, per_group // step)
        def _(turn):
            here = pl.ds(turn * step, step)
            grad = reduced[k][here].astype(F32)
            first_new = 0.9 * first[here, upper(k), cols(k)] + 0.1 * grad
            second_new = 0.95 * second[here, upper(k), cols(k)] + 0.05 * grad * grad
            first_out[here, upper(k), cols(k)] = first_new
            second_out[here, upper(k), cols(k)] = second_new
            adam = first_new / (jnp.sqrt(second_new) + 1e-08)
            adam = jnp.sum((adam * adam).reshape(step, height // 8, 8, -1), axis=1)
            adam_sums[k, here] = functools.reduce(
                jnp.add, [adam[:, :, at * 128 : at * 128 + 128] for at in range(PARTS[k][2])]
            )

    far_sums(0)
    near_sums(0)
    far_sums(1)
    relay(0)
    for load in loads:
        load.start()
    for k in chunks:
        if k + 1 < CHUNKS:
            near_sums(k + 1)
        if k + 2 < CHUNKS:
            far_sums(k + 2)
        if k + 1 < CHUNKS:
            relay(k + 1)
        if k == 1:
            loads[2].wait()
            loads[3].wait()
        if 1 <= k < CHUNKS - 2:
            moments(k - 1)
        finish(k)
        to_owners(k)
    def arrived(ref, sem):
        pltpu.make_async_copy(ref, ref, sem).wait()

    def owners_have(k):
        arrived(outgoing[k].at[pl.ds(0, ranks - 1)], owner_recv.at[k])

    def part_product(slot, there):
        part = jnp.dot(root_left[slot], block[slot, :, there], preferred_element_type=F32)
        return jnp.dot(part.astype(BF16), root_right[slot, there], preferred_element_type=F32)

    front, back = pl.ds(0, columns // 2), pl.ds(columns // 2, columns // 2)
    loads[0].wait()
    loads[1].wait()
    for k in range(EARLY):
        owners_have(k)
    for slot in range(slots):
        partial[slot] = part_product(slot, front)
    for k in range(CHUNKS - 3, CHUNKS):
        moments(k)
    for k in range(EARLY, CHUNKS):
        owners_have(k)

    def precondition(slot):
        direction[slot] = (partial[slot] + part_product(slot, back)).astype(BF16)

    def send_back(slot):
        for offset in OFFSETS:
            target = at_offset(*offset)
            pltpu.make_async_remote_copy(
                src_ref=direction.at[slot, strip_rows(target)],
                dst_ref=returned.at[rank, slot],
                send_sem=back_send.at[slot],
                recv_sem=back_recv.at[slot],
                device_id={"fsdp": target},
            ).start()
        returned[rank, slot] = direction[slot, strip_rows(rank)]

    def squares(slot):
        wide = direction[slot].astype(F32)
        wide = jnp.sum(jnp.sum((wide * wide).reshape(-1, 8, columns), axis=0), axis=0, keepdims=True)
        return jnp.sum(wide, axis=1, keepdims=True)

    def send_sums(target):
        pltpu.make_async_remote_copy(
            src_ref=sums,
            dst_ref=all_sums.at[rank],
            send_sem=sums_send,
            recv_sem=sums_recv,
            device_id={"fsdp": target},
        ).start()

    adam = jnp.sum(jnp.sum(jnp.sum(adam_sums[...], axis=0), axis=1), axis=1, keepdims=True)
    lane = lax.broadcasted_iota(I32, (8, 128), 1)
    precondition(0)
    send_back(0)
    precondition(1)
    tile = jnp.where(lane == 0, adam[:8], 0.0) + jnp.where(lane == 1, adam[8:], 0.0)
    for slot in range(slots):
        tile = tile + jnp.where(lane == 2 + slot, squares(slot), 0.0)
    sums[...] = tile
    all_sums[rank] = tile
    each_target(send_sums)
    send_back(1)

    loads[4].wait()
    loads[5].wait()
    for stat, contract, out in ((stat_left, 1, left_out), (stat_right, 0, right_out)):
        for slot in range(slots):
            gram = lax.dot_general(
                block[slot],
                block[slot],
                (((contract,), (contract,)), ((), ())),
                preferred_element_type=F32,
            )
            used = held(rank * slots + slot) > 0
            out[slot] = 0.95 * stat[slot] + 0.05 * jnp.where(used, gram, 0.0)

    arrived(all_sums.at[pl.ds(0, ranks - 1)], sums_recv)
    for index in range(per_group):
        at = place_of(index)
        row = all_sums[at // slots, pl.ds(0, 1)]
        sizes[index : index + 1] = jnp.where(lane[:1] == 2 + at % slots, row, 0.0)
    total = jnp.sum(all_sums[...], axis=0)
    adam_sq = jnp.concatenate([total[:, 0:1], total[:, 1:2]], axis=0)
    direction_sq = jnp.sum(sizes[...], axis=1, keepdims=True)
    graft[...] = jnp.broadcast_to(jnp.sqrt(adam_sq / (direction_sq + 1e-06)), graft.shape)
    for slot in range(slots):
        arrived(returned.at[pl.ds(0, ranks - 1), slot], back_recv.at[slot])

    for k in chunks:
        for copy in ring_copies[k]:
            copy.wait_send()
    for copy in core_copies:
        copy.wait_send()
    for k in chunks:
        arrived(outgoing[k].at[pl.ds(0, ranks - 1)], owner_send.at[k])
    for slot in range(slots):
        arrived(direction.at[slot, pl.ds(0, (ranks - 1) * strip)], back_send.at[slot])
    arrived(all_sums.at[pl.ds(0, ranks - 1)], sums_send)


def exchange(block_owner, gradients, root_left, root_right, first, second, left, right, ranks):
    lines, _, per_group, strip, columns = gradients.shape
    slots, rows, _ = root_left.shape
    height = strip // 2
    widths = [tiles * 128 for _, _, tiles in PARTS]
    half = per_group // 2
    far = pl.BlockSpec(memory_space=pltpu.HBM)
    dma = pltpu.SemaphoreType.DMA
    vmem = pltpu.VMEM
    return pl.pallas_call(
        exchange_kernel,
        out_shape=(
            pltpu.VMEM((ranks, slots, strip, columns), BF16),
            pltpu.VMEM((per_group, 128), F32),
            pltpu.VMEM((8, 128), I32),
            pltpu.VMEM(first.shape, F32),
            pltpu.VMEM(first.shape, F32),
            pltpu.VMEM(left.shape, F32),
            pltpu.VMEM(right.shape, F32),
        ),
        in_specs=[far] * 8,
        out_specs=(pl.BlockSpec(memory_space=pltpu.VMEM),) * 7,
        scratch_shapes=[
            vmem(block_owner.shape, I32),
            pltpu.SMEM((8, 128), I32),
            vmem((lines, per_group, strip, columns), BF16),
            vmem((lines, per_group, strip, columns), BF16),
            vmem((lines, per_group, strip, columns), BF16),
            [vmem((lines, per_group, height, wide), BF16) for wide in widths],
            [vmem((half, height, wide), BF16) for wide in widths],
            [vmem((half, height, wide), BF16) for wide in widths],
            [vmem((per_group, height, wide), BF16) for wide in widths],
            [vmem((per_group, height, wide), BF16) for wide in widths],
            [vmem((per_group, height, wide), BF16) for wide in widths],
            [vmem((ranks, slots, height, wide), BF16) for wide in widths],
            vmem((slots, rows, columns), BF16),
            vmem((slots, rows, columns), BF16),
            vmem((slots, rows, columns), BF16),
            vmem(first.shape, F32),
            vmem(first.shape, F32),
            vmem(left.shape, F32),
            vmem(right.shape, F32),
            vmem((slots, rows, columns), F32),
            vmem((slots, rows, columns), BF16),
            vmem((8, 128), F32),
            vmem((ranks, 8, 128), F32),
            vmem((per_group, 128), F32),
            vmem((CHUNKS, per_group, 8, 128), F32),
            dma((2,)),
            dma((2, 4)),
            dma((6,)),
            dma((5,)),
            dma((5,)),
            dma((CHUNKS, 6)),
            dma((CHUNKS, 6)),
            dma((CHUNKS,)),
            dma((CHUNKS,)),
            dma((slots,)),
            dma((slots,)),
            dma,
            dma,
        ],
        compiler_params=pltpu.CompilerParams(
            collective_id=0, has_side_effects=True, vmem_limit_bytes=40 * 2**20
        ),
        cost_estimate=pl.CostEstimate(
            flops=8 * slots * rows * rows * columns, bytes_accessed=18 * 2**20, transcendentals=0
        ),
        name="exchange",
    )(
        *(
            pltpu.with_memory_space_constraint(value, pltpu.HBM)
            for value in (
                block_owner,
                gradients,
                root_left,
                root_right,
                first,
                second,
                left,
                right,
            )
        )
    )


def publish_kernel(
    returned,
    graft,
    places,
    first,
    second,
    left,
    right,
    update_out,
    first_out,
    second_out,
    left_out,
    right_out,
    place,
    update,
    sems,
):
    per_group, strip, columns = update.shape
    ranks, slots = returned.shape[:2]
    place_copy = pltpu.make_async_copy(places, place, sems.at[9])
    place_copy.start()
    pairs = ((left, left_out), (right, right_out), (first, first_out), (second, second_out))
    copies = []
    for index, (src, out) in enumerate(pairs):
        part = src.shape[0] // 2
        for at in range(2):
            here = pl.ds(at * part, part)
            copies.append(
                pltpu.make_async_copy(src.at[here], out.at[here], sems.at[2 * index + at])
            )
    for copy in copies:
        copy.start()
    place_copy.wait()
    dp = lax.axis_index("dp")

    @pl.loop(0, per_group)
    def _(index):
        at = jnp.clip(place[0, dp * per_group + index], 0, ranks * slots - 1)
        scale = -graft[pl.ds(index, 1)]
        value = returned[at // slots, at % slots].astype(F32)
        update[index] = (value * jnp.concatenate([scale] * (columns // 128), axis=1)).astype(BF16)

    copies.append(pltpu.make_async_copy(update, update_out, sems.at[8]))
    copies[-1].start()
    for copy in copies:
        copy.wait()


def publish(results):
    returned, graft, places, first, second, left, right = results
    anywhere = pl.BlockSpec(memory_space=pl.ANY)
    near = pl.BlockSpec(memory_space=pltpu.VMEM)
    shapes = [(first.shape, BF16)] + [(value.shape, F32) for value in results[3:]]
    return pl.pallas_call(
        publish_kernel,
        out_shape=[jax.ShapeDtypeStruct(*shape) for shape in shapes],
        in_specs=[near, near] + [anywhere] * 5,
        out_specs=[pl.BlockSpec(memory_space=pltpu.HBM)] * 5,
        scratch_shapes=[
            pltpu.SMEM((8, 128), I32),
            pltpu.VMEM(first.shape, BF16),
            pltpu.SemaphoreType.DMA((10,)),
        ],
        compiler_params=pltpu.CompilerParams(vmem_limit_bytes=4 * 2**20),
        name="publish",
    )(*(pltpu.with_memory_space_constraint(value, pltpu.VMEM) for value in results))


def shards(
    gradients,
    block_owner,
    left_stat,
    right_stat,
    root_left,
    root_right,
    moment_first,
    moment_second,
):
    dp_count = lax.axis_size("dp")
    ranks = lax.axis_size("fsdp")
    count = block_owner.shape[0]
    strip, columns = gradients.shape[2:]
    results = exchange(
        block_owner.reshape(1, count),
        gradients.reshape(dp_count // 2, 2, count // dp_count, strip, columns),
        root_left,
        root_right,
        moment_first,
        moment_second,
        left_stat,
        right_stat,
        ranks,
    )
    return tuple(publish(results))


def solution(mesh):
    placed = (
        P("dp", None, "fsdp", None),
        P(),
        P(("dp", "fsdp"), None, None),
        P(("dp", "fsdp"), None, None),
        P(("dp", "fsdp"), None, None),
        P(("dp", "fsdp"), None, None),
        P("dp", "fsdp", None),
        P("dp", "fsdp", None),
    )
    return jax.shard_map(
        shards,
        mesh=mesh,
        in_specs=placed,
        out_specs=(
            P("dp", "fsdp", None),
            P("dp", "fsdp", None),
            P("dp", "fsdp", None),
            P(("dp", "fsdp"), None, None),
            P(("dp", "fsdp"), None, None),
        ),
        check_vma=False,
    )
```

```python
import functools

import jax
import jax.numpy as jnp
from jax import lax
from jax.experimental import pallas as pl
from jax.experimental.pallas import tpu as pltpu
from jax.sharding import PartitionSpec as P

F32 = jnp.float32
BF16 = jnp.bfloat16
I32 = jnp.int32
PARTS = ((0, 0, 1), (0, 1, 1), (0, 2, 2), (1, 0, 2), (1, 2, 1), (1, 3, 1))
CHUNKS = len(PARTS)
LATE = (CHUNKS - 2, CHUNKS - 1)
SIDE = 4
OFFSETS = (
    *((2, 2), (2, 1), (2, -1), (1, 2), (-1, 2), (2, 0), (0, 2)),
    *((1, 1), (-1, -1), (1, -1), (-1, 1), (1, 0), (-1, 0), (0, 1), (0, -1)),
)


def exchange_kernel(
    owner_ref,
    grad_ref,
    root_left_ref,
    root_right_ref,
    first_ref,
    second_ref,
    left_ref,
    right_ref,
    returned,
    graft,
    places,
    first_out,
    second_out,
    left_out,
    right_out,
    owner,
    place,
    own,
    lend,
    other,
    pair,
    relay_right,
    relay_left,
    from_left,
    from_right,
    reduced,
    outgoing,
    block,
    root_left,
    root_right,
    first,
    second,
    stat_left,
    stat_right,
    direction,
    sums,
    all_sums,
    sizes,
    adam_sums,
    place_sem,
    own_sem,
    load_sem,
    core_send,
    core_recv,
    ring_send,
    ring_recv,
    owner_send,
    owner_recv,
    back_send,
    back_recv,
    sums_send,
    sums_recv,
):
    lines, _, per_group, strip, columns = grad_ref.shape
    height = strip // 2
    half = per_group // 2
    slots, rows = block.shape[:2]
    ranks = rows // strip
    count = owner.shape[1]
    dp = lax.axis_index("dp")
    rank = lax.axis_index("fsdp")
    x = dp // 2
    core = dp % 2
    y = rank % SIDE
    z = rank // SIDE
    mate = x * 2 + (1 - core)
    sign = 1 - 2 * core
    ahead = (x + lines + sign) % lines
    behind = (x + lines - sign) % lines
    across = (x + 2) % lines
    right = ahead * 2 + core
    left = behind * 2 + core
    chunks = range(CHUNKS)

    def upper(k):
        return pl.ds(PARTS[k][0] * height, height)

    def cols(k):
        return pl.ds(PARTS[k][1] * 128, PARTS[k][2] * 128)

    def strip_rows(at):
        return pl.ds(pl.multiple_of(at * strip, strip), strip)

    def at_offset(dy, dz):
        target_y = (y + SIDE + sign * dy) % SIDE
        target_z = (z + SIDE + sign * dz) % SIDE
        return target_z * SIDE + target_y

    def each_target(visit):
        @pl.loop(0, SIDE)
        def _(turn):
            for index, (dy, shift) in enumerate(((1, 0), (3, 2), (2, 3), (0, 1))):
                dz = (turn + shift) % SIDE
                target = at_offset(dy, dz)
                if index < 3:
                    visit(target)
                else:
                    pl.when(turn < SIDE - 1)(functools.partial(visit, target))

    owner_load = pltpu.make_async_copy(owner_ref, owner, place_sem.at[0])
    owner_load.start()
    order = (across, ahead, behind, x)
    lend_loads, own_loads = [], []
    for index, line in enumerate(order):
        lend_loads.append(
            pltpu.make_async_copy(grad_ref.at[line, 1 - core], lend.at[line], own_sem.at[0, index])
        )
        own_loads.append(
            pltpu.make_async_copy(grad_ref.at[line, core], own.at[line], own_sem.at[1, index])
        )
    for load in lend_loads + own_loads:
        load.start()
    loads = [
        pltpu.make_async_copy(src, dst, load_sem.at[index])
        for index, (src, dst) in enumerate(
            (
                (root_left_ref, root_left),
                (root_right_ref, root_right),
                (first_ref, first),
                (second_ref, second),
                (left_ref, stat_left),
                (right_ref, stat_right),
            )
        )
    ]
    barrier = pltpu.get_barrier_semaphore()
    for partner in (mate, right, left):
        pl.semaphore_signal(barrier, inc=1, device_id={"dp": partner})

    @pl.loop(1, ranks)
    def _(step):
        pl.semaphore_signal(barrier, inc=1, device_id={"fsdp": (rank + step) % ranks})

    owner_load.wait()
    along = lax.broadcasted_iota(I32, (count, count), 1)
    down = lax.broadcasted_iota(I32, (count, count), 0)
    owner_row = owner[...]
    owner_all = jnp.broadcast_to(owner_row, (count, count)).astype(F32)
    owner_col = jnp.sum(jnp.where(along == down, owner_all, 0.0), axis=1, keepdims=True)
    same = owner_all == owner_col
    slot_row = jnp.sum(jnp.where(same & (down < along), 1.0, 0.0), axis=0, keepdims=True)
    slot_col = jnp.sum(jnp.where(same & (along < down), 1.0, 0.0), axis=1, keepdims=True)
    offset = (dp * (ranks * slots)).astype(F32)
    place_row = owner_row.astype(F32) * slots + slot_row - offset
    place_col = owner_col * slots + slot_col - offset
    number = (down - dp * per_group + 1).astype(F32)
    held_row = jnp.sum(
        jnp.where(along.astype(F32) == place_col, number, 0.0), axis=0, keepdims=True
    )
    places[...] = jnp.concatenate(
        [place_row, held_row, jnp.zeros((6, count), F32)], axis=0
    ).astype(I32)
    place_copy = pltpu.make_async_copy(places, place, place_sem.at[1])
    place_copy.start()

    pl.semaphore_wait(barrier, ranks + 2)

    core_copies = []
    everything, top, bottom = pl.ds(0, strip), pl.ds(0, height), pl.ds(height, height)
    pieces = ((0, top), (0, bottom), (1, everything), (2, everything), (3, everything))
    for at, (index, there) in enumerate(pieces):
        if at != 1:
            lend_loads[index].wait()
        copy = pltpu.make_async_remote_copy(
            src_ref=lend.at[order[index], :, there],
            dst_ref=other.at[order[index], :, there],
            send_sem=core_send.at[at],
            recv_sem=core_recv.at[lines if at == 1 else order[index]],
            device_id={"dp": mate},
        )
        copy.start()
        core_copies.append(copy)
    place_copy.wait()

    def held(at):
        return place[1, at]

    def block_of(at):
        return jnp.clip(held(at) - 1, 0, per_group - 1)

    def place_of(index):
        return jnp.clip(place[0, dp * per_group + index], 0, ranks * slots - 1)

    def ready(k, index):
        if k == 0:
            own_loads[index].wait()
        if PARTS[k][1] == 0 and (k == 0 or index == 0):
            at = index + 1 if index else PARTS[k][0]
            ref = other.at[order[index], :, pieces[at][1]]
            sem = core_recv.at[lines if at == 1 else order[index]]
            pltpu.make_async_copy(ref, ref, sem).wait()

    def both(k, index):
        line = order[index]
        return own[line, :, upper(k), cols(k)], other[line, :, upper(k), cols(k)]

    def pair_sum(k, index):
        ready(k, index)
        mine, its = both(k, index)
        pair[k][order[index]] = mine + its

    def ring(k, index, src, dst, target):
        return pltpu.make_async_remote_copy(
            src_ref=src,
            dst_ref=dst,
            send_sem=ring_send.at[k, index],
            recv_sem=ring_recv.at[k, index],
            device_id={"dp": target},
        )

    ring_copies = [None] * CHUNKS
    low, high = pl.ds(0, half), pl.ds(half, half)

    def far_sums(k):
        copies = [
            ring(k, 0, pair[k].at[across, low], relay_right[k], right),
            ring(k, 1, pair[k].at[across, high], relay_left[k], left),
            ring(k, 2, pair[k].at[ahead, high], from_left[k].at[high], right),
            ring(k, 3, pair[k].at[behind, low], from_right[k].at[low], left),
            ring(k, 4, pair[k].at[ahead, low], from_left[k].at[low], right),
            ring(k, 5, pair[k].at[behind, high], from_right[k].at[high], left),
        ]
        ring_copies[k] = copies
        pair_sum(k, 0)
        copies[0].start()
        copies[1].start()

    def near_sums(k):
        copies = ring_copies[k]
        pair_sum(k, 1)
        copies[2].start()
        pair_sum(k, 2)
        copies[3].start()

    def relay(k):
        copies = ring_copies[k]
        copies[0].wait_recv()
        pair[k][ahead, low] = pair[k][ahead, low] + relay_right[k][...]
        copies[4].start()
        copies[1].wait_recv()
        pair[k][behind, high] = pair[k][behind, high] + relay_left[k][...]
        copies[5].start()
    def finish(k):
        ready(k, 3)
        mine, its = both(k, 3)
        total = mine.astype(F32) + its.astype(F32)
        for copy in ring_copies[k][2:]:
            copy.wait_recv()
        total = total + from_left[k][...].astype(F32) + from_right[k][...].astype(F32)
        reduced[k][...] = total.astype(BF16)

    def strip_part(k):
        return pl.ds(pl.multiple_of(rank * strip + PARTS[k][0] * height, height), height)

    def to_owners(k, only=None):
        which = range(slots) if only is None else (only,)

        def visit(target):
            for slot in which:
                outgoing[k][target, slot] = reduced[k][block_of(target * slots + slot)]
            if only is None:
                src, dst = outgoing[k].at[target], block.at[:, strip_part(k), cols(k)]
            else:
                src, dst = outgoing[k].at[target, only], block.at[only, strip_part(k), cols(k)]
            pltpu.make_async_remote_copy(
                src_ref=src,
                dst_ref=dst,
                send_sem=owner_send.at[k, which[0]],
                recv_sem=owner_recv.at[k, which[0]],
                device_id={"fsdp": target},
            ).start()

        each_target(visit)
        for slot in which:
            block[slot, strip_part(k), cols(k)] = reduced[k][block_of(rank * slots + slot)]

    def owner_messages(k, slot):
        if k in LATE:
            return outgoing[k].at[pl.ds(0, ranks - 1), slot]
        return outgoing[k].at[pl.ds(0, ranks - 1)]

    def moments(k):
        step = 4

        @pl.loop(0, per_group // step)
        def _(turn):
            here = pl.ds(turn * step, step)
            grad = reduced[k][here].astype(F32)
            first_new = 0.9 * first[here, upper(k), cols(k)] + 0.1 * grad
            second_new = 0.95 * second[here, upper(k), cols(k)] + 0.05 * grad * grad
            first_out[here, upper(k), cols(k)] = first_new
            second_out[here, upper(k), cols(k)] = second_new
            adam = first_new / (jnp.sqrt(second_new) + 1e-08)
            adam = jnp.sum((adam * adam).reshape(step, height // 8, 8, -1), axis=1)
            adam_sums[k, here] = functools.reduce(
                jnp.add, [adam[:, :, at * 128 : at * 128 + 128] for at in range(PARTS[k][2])]
            )

    far_sums(0)
    near_sums(0)
    far_sums(1)
    relay(0)
    for load in loads:
        load.start()
    for k in chunks:
        if k + 1 < CHUNKS:
            near_sums(k + 1)
        if k + 2 < CHUNKS:
            far_sums(k + 2)
        if k + 1 < CHUNKS:
            relay(k + 1)
        if k == 1:
            loads[2].wait()
            loads[3].wait()
        if 1 <= k < CHUNKS - 2:
            moments(k - 1)
        finish(k)
        to_owners(k, 0 if k in LATE else None)
    for slot in range(1, slots):
        for k in LATE:
            to_owners(k, slot)
    for k in range(CHUNKS - 3, CHUNKS):
        moments(k)

    def arrived(ref, sem):
        pltpu.make_async_copy(ref, ref, sem).wait()

    loads[0].wait()
    loads[1].wait()

    def owners_have(slot):
        for k in chunks:
            if slot == 0 or k in LATE:
                arrived(owner_messages(k, slot), owner_recv.at[k, slot])


    def precondition(slot):
        product = jnp.dot(root_left[slot], block[slot], preferred_element_type=F32)
        direction[slot] = jnp.dot(
            product.astype(BF16), root_right[slot], preferred_element_type=F32
        ).astype(BF16)

    def send_back(slot):
        for offset in OFFSETS:
            target = at_offset(*offset)
            pltpu.make_async_remote_copy(
                src_ref=direction.at[slot, strip_rows(target)],
                dst_ref=returned.at[rank, slot],
                send_sem=back_send.at[slot],
                recv_sem=back_recv.at[slot],
                device_id={"fsdp": target},
            ).start()
        returned[rank, slot] = direction[slot, strip_rows(rank)]

    def squares(slot):
        wide = direction[slot].astype(F32)
        wide = jnp.sum(jnp.sum((wide * wide).reshape(-1, 8, columns), axis=0), axis=0, keepdims=True)
        return jnp.sum(wide, axis=1, keepdims=True)

    def send_sums(target):
        pltpu.make_async_remote_copy(
            src_ref=sums,
            dst_ref=all_sums.at[rank],
            send_sem=sums_send,
            recv_sem=sums_recv,
            device_id={"fsdp": target},
        ).start()

    adam = jnp.sum(jnp.sum(jnp.sum(adam_sums[...], axis=0), axis=1), axis=1, keepdims=True)
    lane = lax.broadcasted_iota(I32, (8, 128), 1)
    owners_have(0)
    precondition(0)
    send_back(0)
    owners_have(1)
    precondition(1)
    tile = jnp.where(lane == 0, adam[:8], 0.0) + jnp.where(lane == 1, adam[8:], 0.0)
    for slot in range(slots):
        tile = tile + jnp.where(lane == 2 + slot, squares(slot), 0.0)
    sums[...] = tile
    all_sums[rank] = tile
    each_target(send_sums)
    send_back(1)

    loads[4].wait()
    loads[5].wait()
    for stat, contract, out in ((stat_left, 1, left_out), (stat_right, 0, right_out)):
        for slot in range(slots):
            gram = lax.dot_general(
                block[slot],
                block[slot],
                (((contract,), (contract,)), ((), ())),
                preferred_element_type=F32,
            )
            used = held(rank * slots + slot) > 0
            out[slot] = 0.95 * stat[slot] + 0.05 * jnp.where(used, gram, 0.0)

    arrived(all_sums.at[pl.ds(0, ranks - 1)], sums_recv)
    for index in range(per_group):
        at = place_of(index)
        row = all_sums[at // slots, pl.ds(0, 1)]
        sizes[index : index + 1] = jnp.where(lane[:1] == 2 + at % slots, row, 0.0)
    total = jnp.sum(all_sums[...], axis=0)
    adam_sq = jnp.concatenate([total[:, 0:1], total[:, 1:2]], axis=0)
    direction_sq = jnp.sum(sizes[...], axis=1, keepdims=True)
    graft[...] = jnp.broadcast_to(jnp.sqrt(adam_sq / (direction_sq + 1e-06)), graft.shape)
    for slot in range(slots):
        arrived(returned.at[pl.ds(0, ranks - 1), slot], back_recv.at[slot])

    for k in chunks:
        for copy in ring_copies[k]:
            copy.wait_send()
    for copy in core_copies:
        copy.wait_send()
    for k in chunks:
        for slot in range(slots if k in LATE else 1):
            arrived(owner_messages(k, slot), owner_send.at[k, slot])
    for slot in range(slots):
        arrived(direction.at[slot, pl.ds(0, (ranks - 1) * strip)], back_send.at[slot])
    arrived(all_sums.at[pl.ds(0, ranks - 1)], sums_send)


def exchange(block_owner, gradients, root_left, root_right, first, second, left, right, ranks):
    lines, _, per_group, strip, columns = gradients.shape
    slots, rows, _ = root_left.shape
    height = strip // 2
    widths = [tiles * 128 for _, _, tiles in PARTS]
    half = per_group // 2
    far = pl.BlockSpec(memory_space=pltpu.HBM)
    dma = pltpu.SemaphoreType.DMA
    vmem = pltpu.VMEM
    return pl.pallas_call(
        exchange_kernel,
        out_shape=(
            pltpu.VMEM((ranks, slots, strip, columns), BF16),
            pltpu.VMEM((per_group, 128), F32),
            pltpu.VMEM((8, 128), I32),
            pltpu.VMEM(first.shape, F32),
            pltpu.VMEM(first.shape, F32),
            pltpu.VMEM(left.shape, F32),
            pltpu.VMEM(right.shape, F32),
        ),
        in_specs=[far] * 8,
        out_specs=(pl.BlockSpec(memory_space=pltpu.VMEM),) * 7,
        scratch_shapes=[
            vmem(block_owner.shape, I32),
            pltpu.SMEM((8, 128), I32),
            vmem((lines, per_group, strip, columns), BF16),
            vmem((lines, per_group, strip, columns), BF16),
            vmem((lines, per_group, strip, columns), BF16),
            [vmem((lines, per_group, height, wide), BF16) for wide in widths],
            [vmem((half, height, wide), BF16) for wide in widths],
            [vmem((half, height, wide), BF16) for wide in widths],
            [vmem((per_group, height, wide), BF16) for wide in widths],
            [vmem((per_group, height, wide), BF16) for wide in widths],
            [vmem((per_group, height, wide), BF16) for wide in widths],
            [vmem((ranks, slots, height, wide), BF16) for wide in widths],
            vmem((slots, rows, columns), BF16),
            vmem((slots, rows, columns), BF16),
            vmem((slots, rows, columns), BF16),
            vmem(first.shape, F32),
            vmem(first.shape, F32),
            vmem(left.shape, F32),
            vmem(right.shape, F32),
            vmem((slots, rows, columns), BF16),
            vmem((8, 128), F32),
            vmem((ranks, 8, 128), F32),
            vmem((per_group, 128), F32),
            vmem((CHUNKS, per_group, 8, 128), F32),
            dma((2,)),
            dma((2, 4)),
            dma((6,)),
            dma((5,)),
            dma((5,)),
            dma((CHUNKS, 6)),
            dma((CHUNKS, 6)),
            dma((CHUNKS, slots)),
            dma((CHUNKS, slots)),
            dma((slots,)),
            dma((slots,)),
            dma,
            dma,
        ],
        compiler_params=pltpu.CompilerParams(
            collective_id=0, has_side_effects=True, vmem_limit_bytes=40 * 2**20
        ),
        cost_estimate=pl.CostEstimate(
            flops=8 * slots * rows * rows * columns, bytes_accessed=18 * 2**20, transcendentals=0
        ),
        name="exchange",
    )(
        *(
            pltpu.with_memory_space_constraint(value, pltpu.HBM)
            for value in (
                block_owner,
                gradients,
                root_left,
                root_right,
                first,
                second,
                left,
                right,
            )
        )
    )


def publish_kernel(
    returned,
    graft,
    places,
    first,
    second,
    left,
    right,
    update_out,
    first_out,
    second_out,
    left_out,
    right_out,
    place,
    update,
    sems,
):
    per_group, strip, columns = update.shape
    ranks, slots = returned.shape[:2]
    place_copy = pltpu.make_async_copy(places, place, sems.at[5])
    place_copy.start()
    pairs = ((left, left_out), (right, right_out), (first, first_out), (second, second_out))
    copies = [
        pltpu.make_async_copy(src, out, sems.at[index]) for index, (src, out) in enumerate(pairs)
    ]
    for copy in copies:
        copy.start()
    place_copy.wait()
    dp = lax.axis_index("dp")

    @pl.loop(0, per_group)
    def _(index):
        at = jnp.clip(place[0, dp * per_group + index], 0, ranks * slots - 1)
        scale = -graft[pl.ds(index, 1)]
        value = returned[at // slots, at % slots].astype(F32)
        update[index] = (value * jnp.concatenate([scale] * (columns // 128), axis=1)).astype(BF16)

    copies.append(pltpu.make_async_copy(update, update_out, sems.at[4]))
    copies[-1].start()
    for copy in copies:
        copy.wait()


def publish(results):
    returned, graft, places, first, second, left, right = results
    anywhere = pl.BlockSpec(memory_space=pl.ANY)
    near = pl.BlockSpec(memory_space=pltpu.VMEM)
    shapes = [(first.shape, BF16)] + [(value.shape, F32) for value in results[3:]]
    return pl.pallas_call(
        publish_kernel,
        out_shape=[jax.ShapeDtypeStruct(*shape) for shape in shapes],
        in_specs=[near, near] + [anywhere] * 5,
        out_specs=[pl.BlockSpec(memory_space=pltpu.HBM)] * 5,
        scratch_shapes=[
            pltpu.SMEM((8, 128), I32),
            pltpu.VMEM(first.shape, BF16),
            pltpu.SemaphoreType.DMA((6,)),
        ],
        compiler_params=pltpu.CompilerParams(vmem_limit_bytes=4 * 2**20),
        name="publish",
    )(*(pltpu.with_memory_space_constraint(value, pltpu.VMEM) for value in results))


def shards(
    gradients,
    block_owner,
    left_stat,
    right_stat,
    root_left,
    root_right,
    moment_first,
    moment_second,
):
    dp_count = lax.axis_size("dp")
    ranks = lax.axis_size("fsdp")
    count = block_owner.shape[0]
    strip, columns = gradients.shape[2:]
    results = exchange(
        block_owner.reshape(1, count),
        gradients.reshape(dp_count // 2, 2, count // dp_count, strip, columns),
        root_left,
        root_right,
        moment_first,
        moment_second,
        left_stat,
        right_stat,
        ranks,
    )
    return tuple(publish(results))


def solution(mesh):
    placed = (
        P("dp", None, "fsdp", None),
        P(),
        P(("dp", "fsdp"), None, None),
        P(("dp", "fsdp"), None, None),
        P(("dp", "fsdp"), None, None),
        P(("dp", "fsdp"), None, None),
        P("dp", "fsdp", None),
        P("dp", "fsdp", None),
    )
    return jax.shard_map(
        shards,
        mesh=mesh,
        in_specs=placed,
        out_specs=(
            P("dp", "fsdp", None),
            P("dp", "fsdp", None),
            P("dp", "fsdp", None),
            P(("dp", "fsdp"), None, None),
            P(("dp", "fsdp"), None, None),
        ),
        check_vma=False,
    )
```

```python
import functools

import jax
import jax.numpy as jnp
from jax import lax
from jax.experimental import pallas as pl
from jax.experimental.pallas import tpu as pltpu
from jax.sharding import PartitionSpec as P

F32 = jnp.float32
BF16 = jnp.bfloat16
I32 = jnp.int32
PARTS = ((0, 0, 1), (0, 1, 1), (0, 2, 2), (1, 0, 2), (1, 2, 1), (1, 3, 1))
CHUNKS = len(PARTS)
LATE = (CHUNKS - 2, CHUNKS - 1)
SIDE = 4
OFFSETS = (
    *((2, 2), (2, 1), (2, -1), (1, 2), (-1, 2), (2, 0), (0, 2)),
    *((1, 1), (-1, -1), (1, -1), (-1, 1), (1, 0), (-1, 0), (0, 1), (0, -1)),
)


def exchange_kernel(
    owner_ref,
    grad_ref,
    root_left_ref,
    root_right_ref,
    first_ref,
    second_ref,
    left_ref,
    right_ref,
    returned,
    graft,
    places,
    first_out,
    second_out,
    left_out,
    right_out,
    owner,
    place,
    own,
    lend,
    other,
    pair,
    relay_right,
    relay_left,
    from_left,
    from_right,
    reduced,
    outgoing,
    block,
    root_left,
    root_right,
    first,
    second,
    stat_left,
    stat_right,
    direction,
    sums,
    all_sums,
    sizes,
    adam_sums,
    place_sem,
    own_sem,
    load_sem,
    core_send,
    core_recv,
    ring_send,
    ring_recv,
    owner_send,
    owner_recv,
    back_send,
    back_recv,
    sums_send,
    sums_recv,
):
    lines, _, per_group, strip, columns = grad_ref.shape
    height = strip // 2
    half = per_group // 2
    slots, rows = block.shape[:2]
    ranks = rows // strip
    count = owner.shape[1]
    dp = lax.axis_index("dp")
    rank = lax.axis_index("fsdp")
    x = dp // 2
    core = dp % 2
    y = rank % SIDE
    z = rank // SIDE
    mate = x * 2 + (1 - core)
    sign = 1 - 2 * core
    ahead = (x + lines + sign) % lines
    behind = (x + lines - sign) % lines
    across = (x + 2) % lines
    right = ahead * 2 + core
    left = behind * 2 + core
    chunks = range(CHUNKS)

    def upper(k):
        return pl.ds(PARTS[k][0] * height, height)

    def cols(k):
        return pl.ds(PARTS[k][1] * 128, PARTS[k][2] * 128)

    def strip_rows(at):
        return pl.ds(pl.multiple_of(at * strip, strip), strip)

    def at_offset(dy, dz):
        target_y = (y + SIDE + sign * dy) % SIDE
        target_z = (z + SIDE + sign * dz) % SIDE
        return target_z * SIDE + target_y

    def each_target(visit):
        @pl.loop(0, SIDE)
        def _(turn):
            for index, (dy, shift) in enumerate(((1, 0), (3, 2), (2, 3), (0, 1))):
                dz = (turn + shift) % SIDE
                target = at_offset(dy, dz)
                if index < 3:
                    visit(target)
                else:
                    pl.when(turn < SIDE - 1)(functools.partial(visit, target))

    owner_load = pltpu.make_async_copy(owner_ref, owner, place_sem.at[0])
    owner_load.start()
    order = (across, ahead, behind, x)
    lend_loads, own_loads = [], []
    for index, line in enumerate(order):
        lend_loads.append(
            pltpu.make_async_copy(grad_ref.at[line, 1 - core], lend.at[line], own_sem.at[0, index])
        )
        own_loads.append(
            pltpu.make_async_copy(grad_ref.at[line, core], own.at[line], own_sem.at[1, index])
        )
    for load in lend_loads + own_loads:
        load.start()
    loads = [
        pltpu.make_async_copy(src, dst, load_sem.at[index])
        for index, (src, dst) in enumerate(
            (
                (root_left_ref, root_left),
                (root_right_ref, root_right),
                (first_ref, first),
                (second_ref, second),
                (left_ref, stat_left),
                (right_ref, stat_right),
            )
        )
    ]
    barrier = pltpu.get_barrier_semaphore()
    for partner in (mate, right, left):
        pl.semaphore_signal(barrier, inc=1, device_id={"dp": partner})

    @pl.loop(1, ranks)
    def _(step):
        pl.semaphore_signal(barrier, inc=1, device_id={"fsdp": (rank + step) % ranks})

    owner_load.wait()
    along = lax.broadcasted_iota(I32, (count, count), 1)
    down = lax.broadcasted_iota(I32, (count, count), 0)
    owner_row = owner[...]
    owner_all = jnp.broadcast_to(owner_row, (count, count)).astype(F32)
    owner_col = jnp.sum(jnp.where(along == down, owner_all, 0.0), axis=1, keepdims=True)
    same = owner_all == owner_col
    slot_row = jnp.sum(jnp.where(same & (down < along), 1.0, 0.0), axis=0, keepdims=True)
    slot_col = jnp.sum(jnp.where(same & (along < down), 1.0, 0.0), axis=1, keepdims=True)
    offset = (dp * (ranks * slots)).astype(F32)
    place_row = owner_row.astype(F32) * slots + slot_row - offset
    place_col = owner_col * slots + slot_col - offset
    number = (down - dp * per_group + 1).astype(F32)
    held_row = jnp.sum(
        jnp.where(along.astype(F32) == place_col, number, 0.0), axis=0, keepdims=True
    )
    places[...] = jnp.concatenate(
        [place_row, held_row, jnp.zeros((6, count), F32)], axis=0
    ).astype(I32)
    place_copy = pltpu.make_async_copy(places, place, place_sem.at[1])
    place_copy.start()

    pl.semaphore_wait(barrier, ranks + 2)

    core_copies = []
    everything, top, bottom = pl.ds(0, strip), pl.ds(0, height), pl.ds(height, height)
    pieces = ((0, top), (0, bottom), (1, everything), (2, everything), (3, everything))
    for at, (index, there) in enumerate(pieces):
        if at != 1:
            lend_loads[index].wait()
        copy = pltpu.make_async_remote_copy(
            src_ref=lend.at[order[index], :, there],
            dst_ref=other.at[order[index], :, there],
            send_sem=core_send.at[at],
            recv_sem=core_recv.at[lines if at == 1 else order[index]],
            device_id={"dp": mate},
        )
        copy.start()
        core_copies.append(copy)
    place_copy.wait()

    def held(at):
        return place[1, at]

    def block_of(at):
        return jnp.clip(held(at) - 1, 0, per_group - 1)

    def place_of(index):
        return jnp.clip(place[0, dp * per_group + index], 0, ranks * slots - 1)

    def ready(k, index):
        if k == 0:
            own_loads[index].wait()
        if PARTS[k][1] == 0 and (k == 0 or index == 0):
            at = index + 1 if index else PARTS[k][0]
            ref = other.at[order[index], :, pieces[at][1]]
            sem = core_recv.at[lines if at == 1 else order[index]]
            pltpu.make_async_copy(ref, ref, sem).wait()

    def both(k, index):
        line = order[index]
        return own[line, :, upper(k), cols(k)], other[line, :, upper(k), cols(k)]

    def pair_sum(k, index):
        ready(k, index)
        mine, its = both(k, index)
        pair[k][order[index]] = mine + its

    def ring(k, index, src, dst, target):
        return pltpu.make_async_remote_copy(
            src_ref=src,
            dst_ref=dst,
            send_sem=ring_send.at[k, index],
            recv_sem=ring_recv.at[k, index],
            device_id={"dp": target},
        )

    ring_copies = [None] * CHUNKS
    low, high = pl.ds(0, half), pl.ds(half, half)

    def far_sums(k):
        copies = [
            ring(k, 0, pair[k].at[across, low], relay_right[k], right),
            ring(k, 1, pair[k].at[across, high], relay_left[k], left),
            ring(k, 2, pair[k].at[ahead, high], from_left[k].at[high], right),
            ring(k, 3, pair[k].at[behind, low], from_right[k].at[low], left),
            ring(k, 4, pair[k].at[ahead, low], from_left[k].at[low], right),
            ring(k, 5, pair[k].at[behind, high], from_right[k].at[high], left),
        ]
        ring_copies[k] = copies
        pair_sum(k, 0)
        copies[0].start()
        copies[1].start()

    def near_sums(k):
        copies = ring_copies[k]
        pair_sum(k, 1)
        copies[2].start()
        pair_sum(k, 2)
        copies[3].start()

    def relay(k):
        copies = ring_copies[k]
        copies[0].wait_recv()
        pair[k][ahead, low] = pair[k][ahead, low] + relay_right[k][...]
        copies[4].start()
        copies[1].wait_recv()
        pair[k][behind, high] = pair[k][behind, high] + relay_left[k][...]
        copies[5].start()
    def finish(k):
        ready(k, 3)
        mine, its = both(k, 3)
        total = mine.astype(F32) + its.astype(F32)
        for copy in ring_copies[k][2:]:
            copy.wait_recv()
        total = total + from_left[k][...].astype(F32) + from_right[k][...].astype(F32)
        reduced[k][...] = total.astype(BF16)

    def strip_part(k):
        return pl.ds(pl.multiple_of(rank * strip + PARTS[k][0] * height, height), height)

    def to_owners(k, only=None):
        which = range(slots) if only is None else (only,)

        def visit(target):
            for slot in which:
                outgoing[k][target, slot] = reduced[k][block_of(target * slots + slot)]
            if only is None:
                src, dst = outgoing[k].at[target], block.at[:, strip_part(k), cols(k)]
            else:
                src, dst = outgoing[k].at[target, only], block.at[only, strip_part(k), cols(k)]
            pltpu.make_async_remote_copy(
                src_ref=src,
                dst_ref=dst,
                send_sem=owner_send.at[k, which[0]],
                recv_sem=owner_recv.at[k, which[0]],
                device_id={"fsdp": target},
            ).start()

        each_target(visit)
        for slot in which:
            block[slot, strip_part(k), cols(k)] = reduced[k][block_of(rank * slots + slot)]

    def owner_messages(k, slot):
        if k in LATE:
            return outgoing[k].at[pl.ds(0, ranks - 1), slot]
        return outgoing[k].at[pl.ds(0, ranks - 1)]

    def moments(k):
        step = 4

        @pl.loop(0, per_group // step)
        def _(turn):
            here = pl.ds(turn * step, step)
            grad = reduced[k][here].astype(F32)
            first_new = 0.9 * first[here, upper(k), cols(k)] + 0.1 * grad
            second_new = 0.95 * second[here, upper(k), cols(k)] + 0.05 * grad * grad
            first_out[here, upper(k), cols(k)] = first_new
            second_out[here, upper(k), cols(k)] = second_new
            adam = first_new / (jnp.sqrt(second_new) + 1e-08)
            adam = jnp.sum((adam * adam).reshape(step, height // 8, 8, -1), axis=1)
            adam_sums[k, here] = functools.reduce(
                jnp.add, [adam[:, :, at * 128 : at * 128 + 128] for at in range(PARTS[k][2])]
            )

    far_sums(0)
    near_sums(0)
    far_sums(1)
    relay(0)
    for load in loads:
        load.start()
    for k in chunks:
        if k + 1 < CHUNKS:
            near_sums(k + 1)
        if k + 2 < CHUNKS:
            far_sums(k + 2)
        if k + 1 < CHUNKS:
            relay(k + 1)
        if k == 1:
            loads[2].wait()
            loads[3].wait()
        if 1 <= k < CHUNKS - 2:
            moments(k - 1)
        finish(k)
        to_owners(k, 0 if k in LATE else None)
    for slot in range(1, slots):
        for k in LATE:
            to_owners(k, slot)

    def arrived(ref, sem):
        pltpu.make_async_copy(ref, ref, sem).wait()

    loads[0].wait()
    loads[1].wait()

    def owners_have(slot):
        for k in chunks:
            if slot == 0 or k in LATE:
                arrived(owner_messages(k, slot), owner_recv.at[k, slot])


    def precondition(slot):
        product = jnp.dot(root_left[slot], block[slot], preferred_element_type=F32)
        direction[slot] = jnp.dot(
            product.astype(BF16), root_right[slot], preferred_element_type=F32
        ).astype(BF16)

    def send_back(slot):
        for offset in OFFSETS:
            target = at_offset(*offset)
            pltpu.make_async_remote_copy(
                src_ref=direction.at[slot, strip_rows(target)],
                dst_ref=returned.at[rank, slot],
                send_sem=back_send.at[slot],
                recv_sem=back_recv.at[slot],
                device_id={"fsdp": target},
            ).start()
        returned[rank, slot] = direction[slot, strip_rows(rank)]

    def squares(slot):
        wide = direction[slot].astype(F32)
        wide = jnp.sum(jnp.sum((wide * wide).reshape(-1, 8, columns), axis=0), axis=0, keepdims=True)
        return jnp.sum(wide, axis=1, keepdims=True)

    def send_sums(target):
        pltpu.make_async_remote_copy(
            src_ref=sums,
            dst_ref=all_sums.at[rank],
            send_sem=sums_send,
            recv_sem=sums_recv,
            device_id={"fsdp": target},
        ).start()

    lane = lax.broadcasted_iota(I32, (8, 128), 1)
    owners_have(0)
    precondition(0)
    send_back(0)
    for k in range(CHUNKS - 3, CHUNKS):
        moments(k)
    owners_have(1)
    precondition(1)
    adam = jnp.sum(jnp.sum(jnp.sum(adam_sums[...], axis=0), axis=1), axis=1, keepdims=True)
    tile = jnp.where(lane == 0, adam[:8], 0.0) + jnp.where(lane == 1, adam[8:], 0.0)
    for slot in range(slots):
        tile = tile + jnp.where(lane == 2 + slot, squares(slot), 0.0)
    sums[...] = tile
    all_sums[rank] = tile
    each_target(send_sums)
    send_back(1)

    loads[4].wait()
    loads[5].wait()
    for stat, contract, out in ((stat_left, 1, left_out), (stat_right, 0, right_out)):
        for slot in range(slots):
            gram = lax.dot_general(
                block[slot],
                block[slot],
                (((contract,), (contract,)), ((), ())),
                preferred_element_type=F32,
            )
            used = held(rank * slots + slot) > 0
            out[slot] = 0.95 * stat[slot] + 0.05 * jnp.where(used, gram, 0.0)

    arrived(all_sums.at[pl.ds(0, ranks - 1)], sums_recv)
    for index in range(per_group):
        at = place_of(index)
        row = all_sums[at // slots, pl.ds(0, 1)]
        sizes[index : index + 1] = jnp.where(lane[:1] == 2 + at % slots, row, 0.0)
    total = jnp.sum(all_sums[...], axis=0)
    adam_sq = jnp.concatenate([total[:, 0:1], total[:, 1:2]], axis=0)
    direction_sq = jnp.sum(sizes[...], axis=1, keepdims=True)
    graft[...] = jnp.broadcast_to(jnp.sqrt(adam_sq / (direction_sq + 1e-06)), graft.shape)
    for slot in range(slots):
        arrived(returned.at[pl.ds(0, ranks - 1), slot], back_recv.at[slot])

    for k in chunks:
        for copy in ring_copies[k]:
            copy.wait_send()
    for copy in core_copies:
        copy.wait_send()
    for k in chunks:
        for slot in range(slots if k in LATE else 1):
            arrived(owner_messages(k, slot), owner_send.at[k, slot])
    for slot in range(slots):
        arrived(direction.at[slot, pl.ds(0, (ranks - 1) * strip)], back_send.at[slot])
    arrived(all_sums.at[pl.ds(0, ranks - 1)], sums_send)


def exchange(block_owner, gradients, root_left, root_right, first, second, left, right, ranks):
    lines, _, per_group, strip, columns = gradients.shape
    slots, rows, _ = root_left.shape
    height = strip // 2
    widths = [tiles * 128 for _, _, tiles in PARTS]
    half = per_group // 2
    far = pl.BlockSpec(memory_space=pltpu.HBM)
    dma = pltpu.SemaphoreType.DMA
    vmem = pltpu.VMEM
    return pl.pallas_call(
        exchange_kernel,
        out_shape=(
            pltpu.VMEM((ranks, slots, strip, columns), BF16),
            pltpu.VMEM((per_group, 128), F32),
            pltpu.VMEM((8, 128), I32),
            pltpu.VMEM(first.shape, F32),
            pltpu.VMEM(first.shape, F32),
            pltpu.VMEM(left.shape, F32),
            pltpu.VMEM(right.shape, F32),
        ),
        in_specs=[far] * 8,
        out_specs=(pl.BlockSpec(memory_space=pltpu.VMEM),) * 7,
        scratch_shapes=[
            vmem(block_owner.shape, I32),
            pltpu.SMEM((8, 128), I32),
            vmem((lines, per_group, strip, columns), BF16),
            vmem((lines, per_group, strip, columns), BF16),
            vmem((lines, per_group, strip, columns), BF16),
            [vmem((lines, per_group, height, wide), BF16) for wide in widths],
            [vmem((half, height, wide), BF16) for wide in widths],
            [vmem((half, height, wide), BF16) for wide in widths],
            [vmem((per_group, height, wide), BF16) for wide in widths],
            [vmem((per_group, height, wide), BF16) for wide in widths],
            [vmem((per_group, height, wide), BF16) for wide in widths],
            [vmem((ranks, slots, height, wide), BF16) for wide in widths],
            vmem((slots, rows, columns), BF16),
            vmem((slots, rows, columns), BF16),
            vmem((slots, rows, columns), BF16),
            vmem(first.shape, F32),
            vmem(first.shape, F32),
            vmem(left.shape, F32),
            vmem(right.shape, F32),
            vmem((slots, rows, columns), BF16),
            vmem((8, 128), F32),
            vmem((ranks, 8, 128), F32),
            vmem((per_group, 128), F32),
            vmem((CHUNKS, per_group, 8, 128), F32),
            dma((2,)),
            dma((2, 4)),
            dma((6,)),
            dma((5,)),
            dma((5,)),
            dma((CHUNKS, 6)),
            dma((CHUNKS, 6)),
            dma((CHUNKS, slots)),
            dma((CHUNKS, slots)),
            dma((slots,)),
            dma((slots,)),
            dma,
            dma,
        ],
        compiler_params=pltpu.CompilerParams(
            collective_id=0, has_side_effects=True, vmem_limit_bytes=40 * 2**20
        ),
        cost_estimate=pl.CostEstimate(
            flops=8 * slots * rows * rows * columns, bytes_accessed=18 * 2**20, transcendentals=0
        ),
        name="exchange",
    )(
        *(
            pltpu.with_memory_space_constraint(value, pltpu.HBM)
            for value in (
                block_owner,
                gradients,
                root_left,
                root_right,
                first,
                second,
                left,
                right,
            )
        )
    )


def publish_kernel(
    returned,
    graft,
    places,
    first,
    second,
    left,
    right,
    update_out,
    first_out,
    second_out,
    left_out,
    right_out,
    place,
    update,
    sems,
):
    per_group, strip, columns = update.shape
    ranks, slots = returned.shape[:2]
    place_copy = pltpu.make_async_copy(places, place, sems.at[5])
    place_copy.start()
    pairs = ((left, left_out), (right, right_out), (first, first_out), (second, second_out))
    copies = [
        pltpu.make_async_copy(src, out, sems.at[index]) for index, (src, out) in enumerate(pairs)
    ]
    for copy in copies:
        copy.start()
    place_copy.wait()
    dp = lax.axis_index("dp")

    @pl.loop(0, per_group)
    def _(index):
        at = jnp.clip(place[0, dp * per_group + index], 0, ranks * slots - 1)
        scale = -graft[pl.ds(index, 1)]
        value = returned[at // slots, at % slots].astype(F32)
        update[index] = (value * jnp.concatenate([scale] * (columns // 128), axis=1)).astype(BF16)

    copies.append(pltpu.make_async_copy(update, update_out, sems.at[4]))
    copies[-1].start()
    for copy in copies:
        copy.wait()


def publish(results):
    returned, graft, places, first, second, left, right = results
    anywhere = pl.BlockSpec(memory_space=pl.ANY)
    near = pl.BlockSpec(memory_space=pltpu.VMEM)
    shapes = [(first.shape, BF16)] + [(value.shape, F32) for value in results[3:]]
    return pl.pallas_call(
        publish_kernel,
        out_shape=[jax.ShapeDtypeStruct(*shape) for shape in shapes],
        in_specs=[near, near] + [anywhere] * 5,
        out_specs=[pl.BlockSpec(memory_space=pltpu.HBM)] * 5,
        scratch_shapes=[
            pltpu.SMEM((8, 128), I32),
            pltpu.VMEM(first.shape, BF16),
            pltpu.SemaphoreType.DMA((6,)),
        ],
        compiler_params=pltpu.CompilerParams(vmem_limit_bytes=4 * 2**20),
        name="publish",
    )(*(pltpu.with_memory_space_constraint(value, pltpu.VMEM) for value in results))


def shards(
    gradients,
    block_owner,
    left_stat,
    right_stat,
    root_left,
    root_right,
    moment_first,
    moment_second,
):
    dp_count = lax.axis_size("dp")
    ranks = lax.axis_size("fsdp")
    count = block_owner.shape[0]
    strip, columns = gradients.shape[2:]
    results = exchange(
        block_owner.reshape(1, count),
        gradients.reshape(dp_count // 2, 2, count // dp_count, strip, columns),
        root_left,
        root_right,
        moment_first,
        moment_second,
        left_stat,
        right_stat,
        ranks,
    )
    return tuple(publish(results))


def solution(mesh):
    placed = (
        P("dp", None, "fsdp", None),
        P(),
        P(("dp", "fsdp"), None, None),
        P(("dp", "fsdp"), None, None),
        P(("dp", "fsdp"), None, None),
        P(("dp", "fsdp"), None, None),
        P("dp", "fsdp", None),
        P("dp", "fsdp", None),
    )
    return jax.shard_map(
        shards,
        mesh=mesh,
        in_specs=placed,
        out_specs=(
            P("dp", "fsdp", None),
            P("dp", "fsdp", None),
            P("dp", "fsdp", None),
            P(("dp", "fsdp"), None, None),
            P(("dp", "fsdp"), None, None),
        ),
        check_vma=False,
    )
```

```python
import functools

import jax
import jax.numpy as jnp
from jax import lax
from jax.experimental import pallas as pl
from jax.experimental.pallas import tpu as pltpu
from jax.sharding import PartitionSpec as P

F32 = jnp.float32
BF16 = jnp.bfloat16
I32 = jnp.int32
PARTS = ((0, 0, 1), (0, 1, 1), (0, 2, 2), (1, 0, 2), (1, 2, 1), (1, 3, 1))
CHUNKS = len(PARTS)
LATE = (CHUNKS - 2, CHUNKS - 1)
SIDE = 4
OFFSETS = (
    *((2, 0), (-1, -1), (0, 2), (1, -1), (2, 1), (0, -1), (-1, 2), (1, 0)),
    *((2, 2), (-1, 0), (1, 2), (0, 1), (2, -1), (-1, 1), (1, 1)),
)


def exchange_kernel(
    owner_ref,
    grad_ref,
    root_left_ref,
    root_right_ref,
    first_ref,
    second_ref,
    left_ref,
    right_ref,
    returned,
    graft,
    places,
    first_out,
    second_out,
    left_out,
    right_out,
    owner,
    place,
    own,
    lend,
    other,
    pair,
    relay_right,
    relay_left,
    from_left,
    from_right,
    reduced,
    outgoing,
    block,
    root_left,
    root_right,
    first,
    second,
    stat_left,
    stat_right,
    direction,
    sums,
    all_sums,
    sizes,
    adam_sums,
    place_sem,
    own_sem,
    load_sem,
    core_send,
    core_recv,
    ring_send,
    ring_recv,
    owner_send,
    owner_recv,
    back_send,
    back_recv,
    sums_send,
    sums_recv,
):
    lines, _, per_group, strip, columns = grad_ref.shape
    height = strip // 2
    half = per_group // 2
    slots, rows = block.shape[:2]
    ranks = rows // strip
    count = owner.shape[1]
    dp = lax.axis_index("dp")
    rank = lax.axis_index("fsdp")
    x = dp // 2
    core = dp % 2
    y = rank % SIDE
    z = rank // SIDE
    mate = x * 2 + (1 - core)
    sign = 1 - 2 * core
    ahead = (x + lines + sign) % lines
    behind = (x + lines - sign) % lines
    across = (x + 2) % lines
    right = ahead * 2 + core
    left = behind * 2 + core
    chunks = range(CHUNKS)

    def upper(k):
        return pl.ds(PARTS[k][0] * height, height)

    def cols(k):
        return pl.ds(PARTS[k][1] * 128, PARTS[k][2] * 128)

    def strip_rows(at):
        return pl.ds(pl.multiple_of(at * strip, strip), strip)

    def at_offset(dy, dz):
        target_y = (y + SIDE + sign * dy) % SIDE
        target_z = (z + SIDE + sign * dz) % SIDE
        return target_z * SIDE + target_y

    def each_target(visit):
        @pl.loop(0, SIDE)
        def _(turn):
            for index, (dy, shift) in enumerate(((1, 0), (3, 2), (2, 3), (0, 1))):
                dz = (turn + shift) % SIDE
                target = at_offset(dy, dz)
                if index < 3:
                    visit(target)
                else:
                    pl.when(turn < SIDE - 1)(functools.partial(visit, target))

    owner_load = pltpu.make_async_copy(owner_ref, owner, place_sem.at[0])
    owner_load.start()
    order = (across, ahead, behind, x)
    lend_loads, own_loads = [], []
    for index, line in enumerate(order):
        lend_loads.append(
            pltpu.make_async_copy(grad_ref.at[line, 1 - core], lend.at[line], own_sem.at[0, index])
        )
        own_loads.append(
            pltpu.make_async_copy(grad_ref.at[line, core], own.at[line], own_sem.at[1, index])
        )
    for load in lend_loads + own_loads:
        load.start()
    loads = [
        pltpu.make_async_copy(src, dst, load_sem.at[index])
        for index, (src, dst) in enumerate(
            (
                (root_left_ref, root_left),
                (root_right_ref, root_right),
                (first_ref, first),
                (second_ref, second),
                (left_ref, stat_left),
                (right_ref, stat_right),
            )
        )
    ]
    barrier = pltpu.get_barrier_semaphore()
    for partner in (mate, right, left):
        pl.semaphore_signal(barrier, inc=1, device_id={"dp": partner})

    @pl.loop(1, ranks)
    def _(step):
        pl.semaphore_signal(barrier, inc=1, device_id={"fsdp": (rank + step) % ranks})

    owner_load.wait()
    along = lax.broadcasted_iota(I32, (count, count), 1)
    down = lax.broadcasted_iota(I32, (count, count), 0)
    owner_row = owner[...]
    owner_all = jnp.broadcast_to(owner_row, (count, count)).astype(F32)
    owner_col = jnp.sum(jnp.where(along == down, owner_all, 0.0), axis=1, keepdims=True)
    same = owner_all == owner_col
    slot_row = jnp.sum(jnp.where(same & (down < along), 1.0, 0.0), axis=0, keepdims=True)
    slot_col = jnp.sum(jnp.where(same & (along < down), 1.0, 0.0), axis=1, keepdims=True)
    offset = (dp * (ranks * slots)).astype(F32)
    place_row = owner_row.astype(F32) * slots + slot_row - offset
    place_col = owner_col * slots + slot_col - offset
    number = (down - dp * per_group + 1).astype(F32)
    held_row = jnp.sum(
        jnp.where(along.astype(F32) == place_col, number, 0.0), axis=0, keepdims=True
    )
    places[...] = jnp.concatenate(
        [place_row, held_row, jnp.zeros((6, count), F32)], axis=0
    ).astype(I32)
    place_copy = pltpu.make_async_copy(places, place, place_sem.at[1])
    place_copy.start()

    pl.semaphore_wait(barrier, ranks + 2)

    core_copies = []
    everything, top, bottom = pl.ds(0, strip), pl.ds(0, height), pl.ds(height, height)
    pieces = ((0, top), (0, bottom), (1, everything), (2, everything), (3, everything))
    for at, (index, there) in enumerate(pieces):
        if at != 1:
            lend_loads[index].wait()
        copy = pltpu.make_async_remote_copy(
            src_ref=lend.at[order[index], :, there],
            dst_ref=other.at[order[index], :, there],
            send_sem=core_send.at[at],
            recv_sem=core_recv.at[lines if at == 1 else order[index]],
            device_id={"dp": mate},
        )
        copy.start()
        core_copies.append(copy)
    place_copy.wait()

    def held(at):
        return place[1, at]

    def block_of(at):
        return jnp.clip(held(at) - 1, 0, per_group - 1)

    def place_of(index):
        return jnp.clip(place[0, dp * per_group + index], 0, ranks * slots - 1)

    def ready(k, index):
        if k == 0:
            own_loads[index].wait()
        if PARTS[k][1] == 0 and (k == 0 or index == 0):
            at = index + 1 if index else PARTS[k][0]
            ref = other.at[order[index], :, pieces[at][1]]
            sem = core_recv.at[lines if at == 1 else order[index]]
            pltpu.make_async_copy(ref, ref, sem).wait()

    def both(k, index):
        line = order[index]
        return own[line, :, upper(k), cols(k)], other[line, :, upper(k), cols(k)]

    def pair_sum(k, index):
        ready(k, index)
        mine, its = both(k, index)
        pair[k][order[index]] = mine + its

    def ring(k, index, src, dst, target):
        return pltpu.make_async_remote_copy(
            src_ref=src,
            dst_ref=dst,
            send_sem=ring_send.at[k, index],
            recv_sem=ring_recv.at[k, index],
            device_id={"dp": target},
        )

    ring_copies = [None] * CHUNKS
    low, high = pl.ds(0, half), pl.ds(half, half)

    def far_sums(k):
        copies = [
            ring(k, 0, pair[k].at[across, low], relay_right[k], right),
            ring(k, 1, pair[k].at[across, high], relay_left[k], left),
            ring(k, 2, pair[k].at[ahead, high], from_left[k].at[high], right),
            ring(k, 3, pair[k].at[behind, low], from_right[k].at[low], left),
            ring(k, 4, pair[k].at[ahead, low], from_left[k].at[low], right),
            ring(k, 5, pair[k].at[behind, high], from_right[k].at[high], left),
        ]
        ring_copies[k] = copies
        pair_sum(k, 0)
        copies[0].start()
        copies[1].start()

    def near_sums(k):
        copies = ring_copies[k]
        pair_sum(k, 1)
        copies[2].start()
        pair_sum(k, 2)
        copies[3].start()

    def relay(k):
        copies = ring_copies[k]
        copies[0].wait_recv()
        pair[k][ahead, low] = pair[k][ahead, low] + relay_right[k][...]
        copies[4].start()
        copies[1].wait_recv()
        pair[k][behind, high] = pair[k][behind, high] + relay_left[k][...]
        copies[5].start()
    def finish(k):
        ready(k, 3)
        mine, its = both(k, 3)
        total = mine.astype(F32) + its.astype(F32)
        for copy in ring_copies[k][2:]:
            copy.wait_recv()
        total = total + from_left[k][...].astype(F32) + from_right[k][...].astype(F32)
        reduced[k][...] = total.astype(BF16)

    def strip_part(k):
        return pl.ds(pl.multiple_of(rank * strip + PARTS[k][0] * height, height), height)

    def to_owners(k, only=None):
        which = range(slots) if only is None else (only,)

        def visit(target):
            for slot in which:
                outgoing[k][target, slot] = reduced[k][block_of(target * slots + slot)]
            if only is None:
                src, dst = outgoing[k].at[target], block.at[:, strip_part(k), cols(k)]
            else:
                src, dst = outgoing[k].at[target, only], block.at[only, strip_part(k), cols(k)]
            pltpu.make_async_remote_copy(
                src_ref=src,
                dst_ref=dst,
                send_sem=owner_send.at[k, which[0]],
                recv_sem=owner_recv.at[k, which[0]],
                device_id={"fsdp": target},
            ).start()

        each_target(visit)
        for slot in which:
            block[slot, strip_part(k), cols(k)] = reduced[k][block_of(rank * slots + slot)]

    def owner_messages(k, slot):
        if k in LATE:
            return outgoing[k].at[pl.ds(0, ranks - 1), slot]
        return outgoing[k].at[pl.ds(0, ranks - 1)]

    def moments(k):
        step = 4

        @pl.loop(0, per_group // step)
        def _(turn):
            here = pl.ds(turn * step, step)
            grad = reduced[k][here].astype(F32)
            first_new = 0.9 * first[here, upper(k), cols(k)] + 0.1 * grad
            second_new = 0.95 * second[here, upper(k), cols(k)] + 0.05 * grad * grad
            first_out[here, upper(k), cols(k)] = first_new
            second_out[here, upper(k), cols(k)] = second_new
            adam = first_new / (jnp.sqrt(second_new) + 1e-08)
            adam = jnp.sum((adam * adam).reshape(step, height // 8, 8, -1), axis=1)
            adam_sums[k, here] = functools.reduce(
                jnp.add, [adam[:, :, at * 128 : at * 128 + 128] for at in range(PARTS[k][2])]
            )

    far_sums(0)
    near_sums(0)
    far_sums(1)
    relay(0)
    for load in loads:
        load.start()
    for k in chunks:
        if k + 1 < CHUNKS:
            near_sums(k + 1)
        if k + 2 < CHUNKS:
            far_sums(k + 2)
        if k + 1 < CHUNKS:
            relay(k + 1)
        if k == 1:
            loads[2].wait()
            loads[3].wait()
        if 1 <= k < CHUNKS - 2:
            moments(k - 1)
        finish(k)
        to_owners(k, 0 if k in LATE else None)
    for slot in range(1, slots):
        for k in LATE:
            to_owners(k, slot)
    for k in range(CHUNKS - 3, CHUNKS):
        moments(k)

    def arrived(ref, sem):
        pltpu.make_async_copy(ref, ref, sem).wait()

    loads[0].wait()
    loads[1].wait()

    def owners_have(slot):
        for k in chunks:
            if slot == 0 or k in LATE:
                arrived(owner_messages(k, slot), owner_recv.at[k, slot])


    def precondition(slot):
        product = jnp.dot(root_left[slot], block[slot], preferred_element_type=F32)
        direction[slot] = jnp.dot(
            product.astype(BF16), root_right[slot], preferred_element_type=F32
        ).astype(BF16)

    def send_back(slot):
        for offset in OFFSETS:
            target = at_offset(*offset)
            pltpu.make_async_remote_copy(
                src_ref=direction.at[slot, strip_rows(target)],
                dst_ref=returned.at[rank, slot],
                send_sem=back_send.at[slot],
                recv_sem=back_recv.at[slot],
                device_id={"fsdp": target},
            ).start()
        returned[rank, slot] = direction[slot, strip_rows(rank)]

    def squares(slot):
        wide = direction[slot].astype(F32)
        wide = jnp.sum(jnp.sum((wide * wide).reshape(-1, 8, columns), axis=0), axis=0, keepdims=True)
        return jnp.sum(wide, axis=1, keepdims=True)

    def send_sums(target):
        pltpu.make_async_remote_copy(
            src_ref=sums,
            dst_ref=all_sums.at[rank],
            send_sem=sums_send,
            recv_sem=sums_recv,
            device_id={"fsdp": target},
        ).start()

    adam = jnp.sum(jnp.sum(jnp.sum(adam_sums[...], axis=0), axis=1), axis=1, keepdims=True)
    lane = lax.broadcasted_iota(I32, (8, 128), 1)
    owners_have(0)
    precondition(0)
    send_back(0)
    owners_have(1)
    precondition(1)
    tile = jnp.where(lane == 0, adam[:8], 0.0) + jnp.where(lane == 1, adam[8:], 0.0)
    for slot in range(slots):
        tile = tile + jnp.where(lane == 2 + slot, squares(slot), 0.0)
    sums[...] = tile
    all_sums[rank] = tile
    each_target(send_sums)
    send_back(1)

    loads[4].wait()
    loads[5].wait()
    for stat, contract, out in ((stat_left, 1, left_out), (stat_right, 0, right_out)):
        for slot in range(slots):
            gram = lax.dot_general(
                block[slot],
                block[slot],
                (((contract,), (contract,)), ((), ())),
                preferred_element_type=F32,
            )
            used = held(rank * slots + slot) > 0
            out[slot] = 0.95 * stat[slot] + 0.05 * jnp.where(used, gram, 0.0)

    arrived(all_sums.at[pl.ds(0, ranks - 1)], sums_recv)
    for index in range(per_group):
        at = place_of(index)
        row = all_sums[at // slots, pl.ds(0, 1)]
        sizes[index : index + 1] = jnp.where(lane[:1] == 2 + at % slots, row, 0.0)
    total = jnp.sum(all_sums[...], axis=0)
    adam_sq = jnp.concatenate([total[:, 0:1], total[:, 1:2]], axis=0)
    direction_sq = jnp.sum(sizes[...], axis=1, keepdims=True)
    graft[...] = jnp.broadcast_to(jnp.sqrt(adam_sq / (direction_sq + 1e-06)), graft.shape)
    for slot in range(slots):
        arrived(returned.at[pl.ds(0, ranks - 1), slot], back_recv.at[slot])

    for k in chunks:
        for copy in ring_copies[k]:
            copy.wait_send()
    for copy in core_copies:
        copy.wait_send()
    for k in chunks:
        for slot in range(slots if k in LATE else 1):
            arrived(owner_messages(k, slot), owner_send.at[k, slot])
    for slot in range(slots):
        arrived(direction.at[slot, pl.ds(0, (ranks - 1) * strip)], back_send.at[slot])
    arrived(all_sums.at[pl.ds(0, ranks - 1)], sums_send)


def exchange(block_owner, gradients, root_left, root_right, first, second, left, right, ranks):
    lines, _, per_group, strip, columns = gradients.shape
    slots, rows, _ = root_left.shape
    height = strip // 2
    widths = [tiles * 128 for _, _, tiles in PARTS]
    half = per_group // 2
    far = pl.BlockSpec(memory_space=pltpu.HBM)
    dma = pltpu.SemaphoreType.DMA
    vmem = pltpu.VMEM
    return pl.pallas_call(
        exchange_kernel,
        out_shape=(
            pltpu.VMEM((ranks, slots, strip, columns), BF16),
            pltpu.VMEM((per_group, 128), F32),
            pltpu.VMEM((8, 128), I32),
            pltpu.VMEM(first.shape, F32),
            pltpu.VMEM(first.shape, F32),
            pltpu.VMEM(left.shape, F32),
            pltpu.VMEM(right.shape, F32),
        ),
        in_specs=[far] * 8,
        out_specs=(pl.BlockSpec(memory_space=pltpu.VMEM),) * 7,
        scratch_shapes=[
            vmem(block_owner.shape, I32),
            pltpu.SMEM((8, 128), I32),
            vmem((lines, per_group, strip, columns), BF16),
            vmem((lines, per_group, strip, columns), BF16),
            vmem((lines, per_group, strip, columns), BF16),
            [vmem((lines, per_group, height, wide), BF16) for wide in widths],
            [vmem((half, height, wide), BF16) for wide in widths],
            [vmem((half, height, wide), BF16) for wide in widths],
            [vmem((per_group, height, wide), BF16) for wide in widths],
            [vmem((per_group, height, wide), BF16) for wide in widths],
            [vmem((per_group, height, wide), BF16) for wide in widths],
            [vmem((ranks, slots, height, wide), BF16) for wide in widths],
            vmem((slots, rows, columns), BF16),
            vmem((slots, rows, columns), BF16),
            vmem((slots, rows, columns), BF16),
            vmem(first.shape, F32),
            vmem(first.shape, F32),
            vmem(left.shape, F32),
            vmem(right.shape, F32),
            vmem((slots, rows, columns), BF16),
            vmem((8, 128), F32),
            vmem((ranks, 8, 128), F32),
            vmem((per_group, 128), F32),
            vmem((CHUNKS, per_group, 8, 128), F32),
            dma((2,)),
            dma((2, 4)),
            dma((6,)),
            dma((5,)),
            dma((5,)),
            dma((CHUNKS, 6)),
            dma((CHUNKS, 6)),
            dma((CHUNKS, slots)),
            dma((CHUNKS, slots)),
            dma((slots,)),
            dma((slots,)),
            dma,
            dma,
        ],
        compiler_params=pltpu.CompilerParams(
            collective_id=0, has_side_effects=True, vmem_limit_bytes=40 * 2**20
        ),
        cost_estimate=pl.CostEstimate(
            flops=8 * slots * rows * rows * columns, bytes_accessed=18 * 2**20, transcendentals=0
        ),
        name="exchange",
    )(
        *(
            pltpu.with_memory_space_constraint(value, pltpu.HBM)
            for value in (
                block_owner,
                gradients,
                root_left,
                root_right,
                first,
                second,
                left,
                right,
            )
        )
    )


def publish_kernel(
    returned,
    graft,
    places,
    first,
    second,
    left,
    right,
    update_out,
    first_out,
    second_out,
    left_out,
    right_out,
    place,
    update,
    sems,
):
    per_group, strip, columns = update.shape
    ranks, slots = returned.shape[:2]
    place_copy = pltpu.make_async_copy(places, place, sems.at[5])
    place_copy.start()
    pairs = ((left, left_out), (right, right_out), (first, first_out), (second, second_out))
    copies = [
        pltpu.make_async_copy(src, out, sems.at[index]) for index, (src, out) in enumerate(pairs)
    ]
    for copy in copies:
        copy.start()
    place_copy.wait()
    dp = lax.axis_index("dp")

    @pl.loop(0, per_group)
    def _(index):
        at = jnp.clip(place[0, dp * per_group + index], 0, ranks * slots - 1)
        scale = -graft[pl.ds(index, 1)]
        value = returned[at // slots, at % slots].astype(F32)
        update[index] = (value * jnp.concatenate([scale] * (columns // 128), axis=1)).astype(BF16)

    copies.append(pltpu.make_async_copy(update, update_out, sems.at[4]))
    copies[-1].start()
    for copy in copies:
        copy.wait()


def publish(results):
    returned, graft, places, first, second, left, right = results
    anywhere = pl.BlockSpec(memory_space=pl.ANY)
    near = pl.BlockSpec(memory_space=pltpu.VMEM)
    shapes = [(first.shape, BF16)] + [(value.shape, F32) for value in results[3:]]
    return pl.pallas_call(
        publish_kernel,
        out_shape=[jax.ShapeDtypeStruct(*shape) for shape in shapes],
        in_specs=[near, near] + [anywhere] * 5,
        out_specs=[pl.BlockSpec(memory_space=pltpu.HBM)] * 5,
        scratch_shapes=[
            pltpu.SMEM((8, 128), I32),
            pltpu.VMEM(first.shape, BF16),
            pltpu.SemaphoreType.DMA((6,)),
        ],
        compiler_params=pltpu.CompilerParams(vmem_limit_bytes=4 * 2**20),
        name="publish",
    )(*(pltpu.with_memory_space_constraint(value, pltpu.VMEM) for value in results))


def shards(
    gradients,
    block_owner,
    left_stat,
    right_stat,
    root_left,
    root_right,
    moment_first,
    moment_second,
):
    dp_count = lax.axis_size("dp")
    ranks = lax.axis_size("fsdp")
    count = block_owner.shape[0]
    strip, columns = gradients.shape[2:]
    results = exchange(
        block_owner.reshape(1, count),
        gradients.reshape(dp_count // 2, 2, count // dp_count, strip, columns),
        root_left,
        root_right,
        moment_first,
        moment_second,
        left_stat,
        right_stat,
        ranks,
    )
    return tuple(publish(results))


def solution(mesh):
    placed = (
        P("dp", None, "fsdp", None),
        P(),
        P(("dp", "fsdp"), None, None),
        P(("dp", "fsdp"), None, None),
        P(("dp", "fsdp"), None, None),
        P(("dp", "fsdp"), None, None),
        P("dp", "fsdp", None),
        P("dp", "fsdp", None),
    )
    return jax.shard_map(
        shards,
        mesh=mesh,
        in_specs=placed,
        out_specs=(
            P("dp", "fsdp", None),
            P("dp", "fsdp", None),
            P("dp", "fsdp", None),
            P(("dp", "fsdp"), None, None),
            P(("dp", "fsdp"), None, None),
        ),
        check_vma=False,
    )
```
